32 devices in a mesh: pipe: 2 (over core), ctx: 4 (over y, x), tensor: 4 (over z).
Axes of the slice: x: 2, y: 2, z: 4, core: 2. Of those that a mesh axis runs over, the one named last changes fastest.
Arguments:
- inputs: bfloat16 [2, 1024, 2048], P(None, 'ctx'), may hold values from -6 to 6
- out_grad: bfloat16 [2, 1024, 2048], P(None, 'ctx'), may hold values from -6 to 6
- positions: int32 [2, 1024], P(None, 'ctx'), may hold values from 0 to 255, as said below
- attn_gain: bfloat16 [2, 2048], P('pipe', 'ctx'), may hold values from 0.25 to 1.75
- w_query: bfloat16 [2, 2048, 2048], P('pipe', 'ctx', 'tensor'), may hold values from -0.125 to 0.125
- w_key: bfloat16 [2, 2048, 512], P('pipe', 'ctx', 'tensor'), may hold values from -0.125 to 0.125
- w_value: bfloat16 [2, 2048, 512], P('pipe', 'ctx', 'tensor'), may hold values from -0.125 to 0.125
- w_out: bfloat16 [2, 2048, 2048], P('pipe', 'tensor', 'ctx'), may hold values from -0.5 to 0.5
- ffn_gain: bfloat16 [2, 2048], P('pipe', 'ctx'), may hold values from 0.25 to 1.75
- w_gate: bfloat16 [2, 2048, 8192], P('pipe', 'ctx', 'tensor'), may hold values from -0.125 to 0.125
- w_up: bfloat16 [2, 2048, 8192], P('pipe', 'ctx', 'tensor'), may hold values from -0.125 to 0.125
- w_down: bfloat16 [2, 8192, 2048], P('pipe', 'tensor', 'ctx'), may hold values from -0.0625 to 0.0625
Outputs:
- section_outputs: bfloat16 [2, 2, 1024, 2048], P('pipe', None, 'ctx')
- boundary_grads: bfloat16 [2, 2, 1024, 2048], P('pipe', None, 'ctx')
- attn_gain_grad: float32 [2, 2048], P('pipe', 'ctx')
- w_query_grad: float32 [2, 2048, 2048], P('pipe', 'ctx', 'tensor')
- w_key_grad: float32 [2, 2048, 512], P('pipe', 'ctx', 'tensor')
- w_value_grad: float32 [2, 2048, 512], P('pipe', 'ctx', 'tensor')
- w_out_grad: float32 [2, 2048, 2048], P('pipe', 'tensor', 'ctx')
- ffn_gain_grad: float32 [2, 2048], P('pipe', 'ctx')
- w_gate_grad: float32 [2, 2048, 8192], P('pipe', 'ctx', 'tensor')
- w_up_grad: float32 [2, 2048, 8192], P('pipe', 'ctx', 'tensor')
- w_down_grad: float32 [2, 8192, 2048], P('pipe', 'tensor', 'ctx')
The draws below stay inside these ranges and needn't reach their ends.
Inputs may be any that keep to these rules, and one draw needn't show every extreme that they name: positions[m, 0] = 0 and each entry is 0 or the entry before it plus 1, so sequences are runs of consecutive tokens; no sequence has more than 256 tokens and every micro-batch has one of exactly 256.
All inputs are finite; a program needn't handle non-finite values.
Results may differ from the reference program's by a relative error of at most 0.025.
Values may be sent and summed in bfloat16 or wider, within the bound.
No kernel may reach another device: no remote copies, remote signals or barrier semaphores. Data moves between devices by JAX's collectives and lax.ppermute only.
A program may use at most 320 MiB of HBM per device.

```python
import math
import jax
import jax.numpy as jnp
from jax import lax

D = 2048
HEADS = 32
KV_HEADS = 8
HEAD_DIM = 64
FF = 8192
MICRO = 2
MAXLEN = 256
SECTIONS = 2
TOKENS = 1024


def draw_positions(key, part):
    index_row = jnp.arange(TOKENS, dtype=jnp.int32)
    half_span = MAXLEN // 2
    shifted = index_row - half_span
    forced = (index_row == 0) | (shifted >= 0) & (shifted % MAXLEN == 0)
    long_run = (shifted >= 0) & (shifted < MAXLEN)
    extra = jax.random.randint(key, (MICRO, TOKENS), 0, 64) == 0
    starts = forced[None, :] | extra & jnp.logical_not(long_run)[None, :]
    first_index = lax.cummax(jnp.where(starts, index_row[None, :], 0), axis=1)
    return (index_row[None, :] - first_index).astype(jnp.int32)


def levels(key, dims, cuts, least, high):
    def one(position, shards_of):
        heights = jax.random.uniform(jax.random.fold_in(jax.random.fold_in(key, 6), position), (shards_of,), jnp.float32, least / len(cuts), high / len(cuts))
        return jnp.repeat(jnp.exp(heights), dims[position] // shards_of).reshape((-1,) + (1,) * (len(dims) - position - 1))

    level = one(*cuts[0])
    for cut in cuts[1:]:
        level = level * one(*cut)
    return level


def noise(key, shape, deviation, bound, split=(), held_as=jnp.bfloat16):
    result = jax.random.normal(key, shape, jnp.float32) * deviation
    if len(split) > 0:
        result = levels(key, shape, split, -0.22, 0.18) * result
    return jnp.clip(result, min=-bound, max=bound).astype(held_as)


def setup_inputs(seed: int = 0) -> dict:
    seeds = jax.random.split(jax.random.key(seed), 13)
    inputs = noise(seeds[0], (MICRO, TOKENS, D), 1.0, 6.0, ((1, 4),))
    out_grad = noise(seeds[1], (MICRO, TOKENS, D), 1.0, 6.0, ((1, 4),))
    positions = draw_positions(jax.random.fold_in(seeds[12], 71), 0)
    attn_gain = jnp.clip(1.0 + 0.15 * jax.random.normal(seeds[3], (SECTIONS, D), jnp.float32), 0.25, 1.75).astype(jnp.bfloat16)
    w_query = noise(seeds[4], (SECTIONS, D, HEADS * HEAD_DIM), D ** -0.5, 0.125, ((0, 2), (1, 4), (2, 4)))
    w_key = noise(seeds[5], (SECTIONS, D, KV_HEADS * HEAD_DIM), D ** -0.5, 0.125, ((0, 2), (1, 4), (2, 4)))
    w_value = noise(seeds[6], (SECTIONS, D, KV_HEADS * HEAD_DIM), D ** -0.5, 0.125, ((0, 2), (1, 4), (2, 4)))
    w_out = noise(seeds[7], (SECTIONS, HEADS * HEAD_DIM, D), (HEADS * HEAD_DIM // 16) ** -0.5, 0.5, ((0, 2), (1, 4), (2, 4)))
    ffn_gain = jnp.clip(1.0 + 0.15 * jax.random.normal(seeds[8], (SECTIONS, D), jnp.float32), 0.25, 1.75).astype(jnp.bfloat16)
    w_gate = noise(seeds[9], (SECTIONS, D, FF), D ** -0.5, 0.125, ((0, 2), (1, 4), (2, 4)))
    w_up = noise(seeds[10], (SECTIONS, D, FF), D ** -0.5, 0.125, ((0, 2), (1, 4), (2, 4)))
    w_down = noise(seeds[11], (SECTIONS, FF, D), FF ** -0.5, 0.0625, ((0, 2), (1, 4), (2, 4)))
    return dict(inputs=inputs, out_grad=out_grad, positions=positions, attn_gain=attn_gain, w_query=w_query, w_key=w_key, w_value=w_value, w_out=w_out, ffn_gain=ffn_gain, w_gate=w_gate, w_up=w_up, w_down=w_down)


epsilon = 1e-05
rope_base = 500000.0

def rounded(value):
    return lax.optimization_barrier(value.astype(jnp.bfloat16)).astype(jnp.float32)

def rows_product(left, right):
    return lax.dot_general(left, right, (((0,), (0,)), ((), ())), preferred_element_type=jnp.float32)

def cols_product(left, right):
    return lax.dot_general(left, right, (((1,), (1,)), ((), ())), preferred_element_type=jnp.float32)

def rope_tables(positions_row, width):
    frequency = jnp.exp(jnp.arange(width // 2, dtype=jnp.float32) * (-2.0 * math.log(rope_base) / width))
    angles = positions_row.astype(jnp.float32)[:, None] * frequency[None, :]
    cosine_table = jnp.concatenate([jnp.cos(angles), jnp.cos(angles)], axis=1)
    sine_table = jnp.concatenate([jnp.sin(angles), jnp.sin(angles)], axis=1)
    return (cosine_table, sine_table)

def rotate(values, cosine_table, sine_table):
    half_width = values.shape[-1] // 2
    turned = jnp.concatenate([-values[..., half_width:], values[..., :half_width]], axis=-1)
    return values * cosine_table[:, None, :] + turned * sine_table[:, None, :]

def rotate_back(grads_in, cosine_table, sine_table):
    half_width = grads_in.shape[-1] // 2
    scaled = grads_in * sine_table[:, None, :]
    turned = jnp.concatenate([-scaled[..., half_width:], scaled[..., :half_width]], axis=-1)
    return grads_in * cosine_table[:, None, :] - turned

def norm_forward(stream, gain_vector):
    inv_rms = lax.rsqrt(lax.optimization_barrier(jnp.mean(stream * stream, axis=-1)) + epsilon)
    return (stream * inv_rms[:, None] * gain_vector[None, :], inv_rms)

def norm_backward(stream, inv_rms, gain_vector, upstream):
    weighted = upstream * gain_vector[None, :]
    gain_grad = lax.optimization_barrier(jnp.sum(upstream * stream * inv_rms[:, None], axis=0))
    inner_mean = lax.optimization_barrier(jnp.mean(stream * weighted, axis=-1))
    stream_grad = weighted * inv_rms[:, None] - stream * (inv_rms * inv_rms * inv_rms * inner_mean)[:, None]
    return (stream_grad, gain_grad)

def scores(query_block, key_block, query_pos, query_index, key_index):
    raw_scores = jnp.einsum('qkgd,skd->kgqs', query_block.astype(jnp.float32), key_block.astype(jnp.float32)) * HEAD_DIM ** (-0.5)
    distance = query_index[:, None] - key_index[None, :]
    allowed = (distance >= 0) & (distance <= query_pos[:, None])
    return jnp.where(allowed[None, None], raw_scores, -1e+30)

def attend(query_block, key_block, value_block, query_pos, query_index, key_index):
    masked = scores(query_block, key_block, query_pos, query_index, key_index)
    row_top = lax.optimization_barrier(jnp.max(masked, axis=-1, keepdims=True))
    exponent = jnp.exp(masked - row_top)
    row_total = lax.optimization_barrier(jnp.sum(exponent, axis=-1, keepdims=True))
    weights_block = rounded(exponent / row_total)
    mixed_rows = jnp.einsum('kgqs,skd->qkgd', weights_block, value_block.astype(jnp.float32))
    return (mixed_rows, (row_top + jnp.log(row_total))[..., 0])

def attend_back(query_block, key_block, value_block, query_pos, query_index, key_index, log_block, mixed_block, grad_block):
    masked = scores(query_block, key_block, query_pos, query_index, key_index)
    probability = jnp.exp(masked - log_block[..., None])
    grad_float = grad_block.astype(jnp.float32)
    prob_grad = jnp.einsum('qkgd,skd->kgqs', grad_float, value_block.astype(jnp.float32))
    row_delta = jnp.transpose(lax.optimization_barrier(jnp.sum(grad_float * mixed_block.astype(jnp.float32), axis=-1)), (1, 2, 0))
    score_grad = rounded(probability * (prob_grad - row_delta[..., None]))
    scale_factor = HEAD_DIM ** (-0.5)
    query_grad = jnp.einsum('kgqs,skd->qkgd', score_grad, key_block.astype(jnp.float32)) * scale_factor
    key_part = jnp.einsum('kgqs,qkgd->skd', score_grad, query_block.astype(jnp.float32)) * scale_factor
    value_part = jnp.einsum('kgqs,qkgd->skd', rounded(probability), grad_float)
    return (query_grad, key_part, value_part)

def attention_forward(queries, keys_window, values_window, positions_row, row_base):
    length = queries.shape[0]
    block_count = length // MAXLEN

    def one_block(block_index):
        row_start = block_index * MAXLEN
        query_block = lax.dynamic_slice_in_dim(queries, row_start, MAXLEN, 0)
        key_block = lax.dynamic_slice_in_dim(keys_window, row_start, 2 * MAXLEN, 0)
        value_block = lax.dynamic_slice_in_dim(values_window, row_start, 2 * MAXLEN, 0)
        query_pos = lax.dynamic_slice_in_dim(positions_row, row_start, MAXLEN, 0)
        query_index = row_base + row_start + jnp.arange(MAXLEN, dtype=jnp.int32)
        key_index = row_base + row_start - MAXLEN + jnp.arange(2 * MAXLEN, dtype=jnp.int32)
        return attend(query_block, key_block, value_block, query_pos, query_index, key_index)
    mixed_rows, log_totals = lax.map(one_block, jnp.arange(block_count, dtype=jnp.int32))
    return (mixed_rows.reshape((length,) + mixed_rows.shape[2:]), log_totals)

def attention_backward(queries, keys_window, values_window, positions_row, row_base, log_totals, mixed_all, grad_all):
    length = queries.shape[0]
    block_count = length // MAXLEN
    zero_grads = jnp.zeros(keys_window.shape, jnp.float32)

    def one_block(carry, block_index):
        key_grads, value_grads = carry
        row_start = block_index * MAXLEN
        query_block = lax.dynamic_slice_in_dim(queries, row_start, MAXLEN, 0)
        key_block = lax.dynamic_slice_in_dim(keys_window, row_start, 2 * MAXLEN, 0)
        value_block = lax.dynamic_slice_in_dim(values_window, row_start, 2 * MAXLEN, 0)
        query_pos = lax.dynamic_slice_in_dim(positions_row, row_start, MAXLEN, 0)
        mixed_block = lax.dynamic_slice_in_dim(mixed_all, row_start, MAXLEN, 0)
        grad_block = lax.dynamic_slice_in_dim(grad_all, row_start, MAXLEN, 0)
        query_index = row_base + row_start + jnp.arange(MAXLEN, dtype=jnp.int32)
        key_index = row_base + row_start - MAXLEN + jnp.arange(2 * MAXLEN, dtype=jnp.int32)
        query_grad, key_part, value_part = attend_back(query_block, key_block, value_block, query_pos, query_index, key_index, log_totals[block_index], mixed_block, grad_block)
        key_grads = lax.dynamic_update_slice_in_dim(key_grads, lax.dynamic_slice_in_dim(key_grads, row_start, 2 * MAXLEN, 0) + key_part, row_start, 0)
        value_grads = lax.dynamic_update_slice_in_dim(value_grads, lax.dynamic_slice_in_dim(value_grads, row_start, 2 * MAXLEN, 0) + value_part, row_start, 0)
        return ((key_grads, value_grads), query_grad)
    (key_grads, value_grads), query_grads = lax.scan(one_block, (zero_grads, zero_grads), jnp.arange(block_count, dtype=jnp.int32))
    return (query_grads.reshape((length,) + query_grads.shape[2:]), key_grads, value_grads)

def layer_forward(stream_bf, positions_row, weights):
    attn_gain, w_query, w_key, w_value, w_out, ffn_gain, w_gate, w_up, w_down = weights
    length = stream_bf.shape[0]
    stream_in = stream_bf.astype(jnp.float32)
    normed, inv_attn = norm_forward(stream_in, attn_gain.astype(jnp.float32))
    normed_attn = normed.astype(jnp.bfloat16)
    cosine_table, sine_table = rope_tables(positions_row, HEAD_DIM)
    queries = rotate(jnp.dot(normed_attn, w_query, preferred_element_type=jnp.float32).reshape(length, HEADS, HEAD_DIM), cosine_table, sine_table).astype(jnp.bfloat16)
    keys_own = rotate(jnp.dot(normed_attn, w_key, preferred_element_type=jnp.float32).reshape(length, KV_HEADS, HEAD_DIM), cosine_table, sine_table).astype(jnp.bfloat16)
    values_own = jnp.dot(normed_attn, w_value, preferred_element_type=jnp.float32).astype(jnp.bfloat16).reshape(length, KV_HEADS, HEAD_DIM)
    zero_rows = jnp.zeros((MAXLEN, KV_HEADS, HEAD_DIM), jnp.bfloat16)
    keys_window = jnp.concatenate([zero_rows, keys_own], axis=0)
    values_window = jnp.concatenate([zero_rows, values_own], axis=0)
    grouped = queries.reshape(length, KV_HEADS, HEADS // KV_HEADS, HEAD_DIM)
    mixed_rows, log_totals = attention_forward(grouped, keys_window, values_window, positions_row, 0)
    attn_mixed = mixed_rows.astype(jnp.bfloat16).reshape(length, HEADS * HEAD_DIM)
    stream_mid = stream_in + jnp.dot(attn_mixed, w_out, preferred_element_type=jnp.float32)
    normed_two, inv_ffn = norm_forward(stream_mid, ffn_gain.astype(jnp.float32))
    normed_ffn = normed_two.astype(jnp.bfloat16)
    gate_proj = jnp.dot(normed_ffn, w_gate, preferred_element_type=jnp.float32)
    up_proj = jnp.dot(normed_ffn, w_up, preferred_element_type=jnp.float32)
    hidden = (jax.nn.silu(gate_proj) * up_proj).astype(jnp.bfloat16)
    stream_out = stream_mid + jnp.dot(hidden, w_down, preferred_element_type=jnp.float32)
    saved_state = (stream_in, inv_attn, normed_attn, grouped, keys_window, values_window, positions_row, cosine_table, sine_table, log_totals, attn_mixed, stream_mid, inv_ffn, normed_ffn, gate_proj, up_proj, hidden)
    return (stream_out, saved_state)

def layer_backward(upstream, saved_state, weights):
    attn_gain, w_query, w_key, w_value, w_out, ffn_gain, w_gate, w_up, w_down = weights
    stream_in, inv_attn, normed_attn, grouped, keys_window, values_window, positions_row, cosine_table, sine_table, log_totals, attn_mixed, stream_mid, inv_ffn, normed_ffn, gate_proj, up_proj, hidden = saved_state
    length = stream_in.shape[0]
    upstream_b = upstream.astype(jnp.bfloat16)
    down_term = rows_product(hidden, upstream_b)
    hidden_grad = cols_product(upstream_b, w_down)
    sigmoid_gate = jax.nn.sigmoid(gate_proj)
    gate_grad = (hidden_grad * up_proj * sigmoid_gate * (1.0 + gate_proj * (1.0 - sigmoid_gate))).astype(jnp.bfloat16)
    up_grad = (hidden_grad * gate_proj * sigmoid_gate).astype(jnp.bfloat16)
    gate_term = rows_product(normed_ffn, gate_grad)
    up_term = rows_product(normed_ffn, up_grad)
    normed_ffn_grad = cols_product(gate_grad, w_gate) + cols_product(up_grad, w_up)
    mid_part, ffn_gain_term = norm_backward(stream_mid, inv_ffn, ffn_gain.astype(jnp.float32), normed_ffn_grad)
    mid_grad = upstream + mid_part
    mid_grad_b = mid_grad.astype(jnp.bfloat16)
    out_term = rows_product(attn_mixed, mid_grad_b)
    mixed_grad = cols_product(mid_grad_b, w_out).astype(jnp.bfloat16)
    grouped_shape = grouped.shape
    query_grads, key_grads, value_grads = attention_backward(grouped, keys_window, values_window, positions_row, 0, log_totals, attn_mixed.reshape(grouped_shape), mixed_grad.reshape(grouped_shape))
    key_grads = key_grads[MAXLEN:]
    value_grads = value_grads[MAXLEN:]
    query_grad_b = rotate_back(query_grads.reshape(length, HEADS, HEAD_DIM), cosine_table, sine_table).astype(jnp.bfloat16).reshape(length, HEADS * HEAD_DIM)
    key_grad_b = rotate_back(key_grads, cosine_table, sine_table).astype(jnp.bfloat16).reshape(length, KV_HEADS * HEAD_DIM)
    value_grad_b = value_grads.astype(jnp.bfloat16).reshape(length, KV_HEADS * HEAD_DIM)
    query_term = rows_product(normed_attn, query_grad_b)
    key_term = rows_product(normed_attn, key_grad_b)
    value_term = rows_product(normed_attn, value_grad_b)
    normed_attn_grad = cols_product(query_grad_b, w_query) + cols_product(key_grad_b, w_key) + cols_product(value_grad_b, w_value)
    input_part, attn_gain_term = norm_backward(stream_in, inv_attn, attn_gain.astype(jnp.float32), normed_attn_grad)
    stream_grad = mid_grad + input_part
    return (stream_grad, (attn_gain_term, query_term, key_term, value_term, out_term, ffn_gain_term, gate_term, up_term, down_term))

def reference(inputs, out_grad, positions, attn_gain, w_query, w_key, w_value, w_out, ffn_gain, w_gate, w_up, w_down):
    all_weights = (attn_gain, w_query, w_key, w_value, w_out, ffn_gain, w_gate, w_up, w_down)
    section_count = 2
    produced = [[], []]
    saved = [[], []]
    for micro_index in range(MICRO):
        stream = inputs[micro_index]
        for section_index in range(section_count):
            weights = tuple((array[section_index] for array in all_weights))
            stream_out, saved_state = layer_forward(stream, positions[micro_index], weights)
            stream = stream_out.astype(jnp.bfloat16)
            produced[section_index].append(stream)
            saved[section_index].append(saved_state)
    boundary = [[None] * MICRO, [None] * MICRO]
    totals = [None, None]
    for micro_index in range(MICRO):
        upstream = out_grad[micro_index].astype(jnp.float32)
        for section_index in (1, 0):
            weights = tuple((array[section_index] for array in all_weights))
            stream_grad, weight_grads = layer_backward(upstream, saved[section_index][micro_index], weights)
            sent_grad = lax.optimization_barrier(stream_grad.astype(jnp.bfloat16))
            boundary[section_index][micro_index] = sent_grad
            upstream = sent_grad.astype(jnp.float32)
            if totals[section_index] is None:
                totals[section_index] = weight_grads
            else:
                totals[section_index] = tuple((first + second for first, second in zip(totals[section_index], weight_grads)))
    section_outputs = jnp.stack([jnp.stack(produced[section_index]) for section_index in range(section_count)])
    boundary_grads = jnp.stack([jnp.stack(boundary[section_index]) for section_index in range(section_count)])
    stacked = [jnp.stack([totals[0][member], totals[1][member]]) for member in range(9)]
    return (section_outputs, boundary_grads, stacked[0], stacked[1], stacked[2], stacked[3], stacked[4], stacked[5], stacked[6], stacked[7], stacked[8])
```

```python
import math

import jax
import jax.numpy as jnp
from jax import lax
from jax.sharding import PartitionSpec as P

HEADS = 32
KV_HEADS = 8
HEAD_DIM = 64
MAXLEN = 256

epsilon = 1e-05
rope_base = 500000.0
bf16 = jnp.bfloat16
f32 = jnp.float32


def swap_cores(block):
    return lax.ppermute(block, "pipe", [(0, 1), (1, 0)])


def from_behind(block, axis, distance):
    devices = range(lax.axis_size(axis))
    route = [(i - distance, i) for i in devices if i - distance in devices]
    return lax.ppermute(block, axis, route)


def product(left, right):
    return lax.dot_general(
        left, right, (((1,), (0,)), ((), ())), preferred_element_type=f32
    )


def rows_product(left, right):
    return lax.dot_general(
        left, right, (((0,), (0,)), ((), ())), preferred_element_type=f32
    )


def cols_product(left, right):
    return lax.dot_general(
        left, right, (((1,), (1,)), ((), ())), preferred_element_type=f32
    )


def rope_tables(positions_row, width):
    frequency = jnp.exp(
        jnp.arange(width // 2, dtype=f32) * (-2.0 * math.log(rope_base) / width)
    )
    angles = positions_row.astype(f32)[:, None] * frequency[None, :]
    cosine_table = jnp.concatenate([jnp.cos(angles), jnp.cos(angles)], axis=1)
    sine_table = jnp.concatenate([jnp.sin(angles), jnp.sin(angles)], axis=1)
    return (cosine_table, sine_table)


def rotate(values, cosine_table, sine_table):
    half_width = values.shape[-1] // 2
    turned = jnp.concatenate([-values[..., half_width:], values[..., :half_width]], axis=-1)
    return values * cosine_table[:, None, :] + turned * sine_table[:, None, :]


def rotate_back(grads_in, cosine_table, sine_table):
    half_width = grads_in.shape[-1] // 2
    scaled = grads_in * sine_table[:, None, :]
    turned = jnp.concatenate([-scaled[..., half_width:], scaled[..., :half_width]], axis=-1)
    return grads_in * cosine_table[:, None, :] - turned


def norm_forward(stream, gain_vector):
    inv_rms = lax.rsqrt(jnp.mean(stream * stream, axis=-1) + epsilon)
    return ((stream * inv_rms[:, None] * gain_vector[None, :]).astype(bf16), inv_rms)


def norm_backward(stream, inv_rms, gain_vector, upstream):
    weighted = upstream * gain_vector[None, :]
    gain_grad = jnp.sum(upstream * stream * inv_rms[:, None], axis=0)
    inner_mean = jnp.mean(stream * weighted, axis=-1)
    stream_grad = (
        weighted * inv_rms[:, None] - stream * (inv_rms * inv_rms * inv_rms * inner_mean)[:, None]
    )
    return (stream_grad, gain_grad)


def scores(query_block, key_block, allowed):
    raw_scores = jnp.einsum(
        "qkgd,skd->kgqs", query_block, key_block, preferred_element_type=f32
    ) * HEAD_DIM ** (-0.5)
    return jnp.where(allowed[None, None], raw_scores, -1e30)


def attend(query_block, key_block, value_block, allowed):
    masked = scores(query_block, key_block, allowed)
    row_top = jnp.max(masked, axis=-1, keepdims=True)
    exponent = jnp.exp(masked - row_top)
    row_total = jnp.sum(exponent, axis=-1, keepdims=True)
    weights_block = (exponent / row_total).astype(bf16)
    mixed_rows = jnp.einsum(
        "kgqs,skd->qkgd", weights_block, value_block, preferred_element_type=f32
    )
    return (mixed_rows, (row_top + jnp.log(row_total))[..., 0])


def attend_back(
    query_block, key_block, value_block, allowed, log_block, mixed_block, grad_block
):
    masked = scores(query_block, key_block, allowed)
    probability = jnp.exp(masked - log_block[..., None])
    prob_grad = jnp.einsum(
        "qkgd,skd->kgqs", grad_block, value_block, preferred_element_type=f32
    )
    row_delta = jnp.transpose(
        jnp.sum(grad_block.astype(f32) * mixed_block.astype(f32), axis=-1),
        (1, 2, 0),
    )
    score_grad = (probability * (prob_grad - row_delta[..., None])).astype(bf16)
    scale_factor = HEAD_DIM ** (-0.5)
    query_grad = (
        jnp.einsum("kgqs,skd->qkgd", score_grad, key_block, preferred_element_type=f32)
        * scale_factor
    )
    key_part = (
        jnp.einsum("kgqs,qkgd->skd", score_grad, query_block, preferred_element_type=f32)
        * scale_factor
    )
    value_part = jnp.einsum(
        "kgqs,qkgd->skd",
        probability.astype(bf16),
        grad_block,
        preferred_element_type=f32,
    )
    return (query_grad, key_part, value_part)


def sum_tensor(partial):
    return lax.psum(partial.astype(bf16), "tensor").astype(f32)


def own_share(partial, rows):
    arrived = swap_cores(partial[rows:].astype(bf16))
    return partial[:rows] + arrived.astype(f32)


def attention_forward(stream, gain, wide, place):
    allowed, cosine, sine, sizes = place
    n_query, n_key = sizes
    rows = stream.shape[0]
    groups = n_key // HEAD_DIM
    normed, inv_rms = norm_forward(stream, gain)
    raw = product(normed, wide[:, : n_query + 2 * n_key])
    queries = rotate(raw[:, :n_query].reshape(rows, -1, HEAD_DIM), cosine, sine).astype(bf16)
    keys = rotate(
        raw[:, n_query : n_query + n_key].reshape(rows, -1, HEAD_DIM), cosine, sine
    ).astype(bf16)
    values = raw[:, n_query + n_key :].astype(bf16)
    own = jnp.concatenate([keys.reshape(rows, n_key), values], axis=1)
    tail = from_behind(own, "ctx", 1)
    window = jnp.concatenate([tail, own], axis=0)
    keys_window = window[:, :n_key].reshape(2 * rows, groups, HEAD_DIM)
    values_window = window[:, n_key:].reshape(2 * rows, groups, HEAD_DIM)
    grouped = queries.reshape(rows, groups, HEADS // KV_HEADS, HEAD_DIM)
    mixed_rows, log_totals = attend(grouped, keys_window, values_window, allowed)
    mixed = mixed_rows.astype(bf16).reshape(rows, n_query)
    partial = cols_product(mixed, wide[:, n_query + 2 * n_key :])
    middle = stream + sum_tensor(partial)
    saved = (stream, inv_rms, normed, grouped, keys_window, values_window, log_totals, mixed)
    return middle, saved


def ffn_forward_in(middle, gain, wide, hidden_width):
    normed, inv_rms = norm_forward(middle, gain)
    both = jnp.concatenate([normed, swap_cores(normed)], axis=0)
    gate_up = product(both, wide[:, : 2 * hidden_width])
    gate = gate_up[:, :hidden_width]
    up = gate_up[:, hidden_width:]
    hidden = (jax.nn.silu(gate) * up).astype(bf16)
    return (middle, inv_rms, both, gate, up, hidden)


def ffn_forward_out(state, wide, hidden_width):
    middle, hidden = state[0], state[-1]
    partial = cols_product(hidden, wide[:, 2 * hidden_width :])
    return (middle + sum_tensor(own_share(partial, middle.shape[0]))).astype(bf16)


def ffn_backward(upstream, upstream_both, state, gain, wide, hidden_width):
    middle, inv_rms, both, gate, up, hidden = state
    hidden_grad = product(upstream_both, wide[:, 2 * hidden_width :])
    sigmoid_gate = jax.nn.sigmoid(gate)
    gate_grad = (hidden_grad * up * sigmoid_gate * (1.0 + gate * (1.0 - sigmoid_gate))).astype(bf16)
    up_grad = (hidden_grad * gate * sigmoid_gate).astype(bf16)
    grads = jnp.concatenate([gate_grad, up_grad], axis=1)
    partial = cols_product(grads, wide[:, : 2 * hidden_width])
    normed_grad = sum_tensor(own_share(partial, middle.shape[0]))
    down_term = rows_product(upstream_both, hidden).astype(bf16)
    wide_term = rows_product(both, grads).astype(bf16)
    mid_part, gain_term = norm_backward(middle, inv_rms, gain, normed_grad)
    return upstream + mid_part, gain_term, wide_term, down_term


def attention_backward(mid_grad, saved, gain, wide, place):
    allowed, cosine, sine, sizes = place
    n_query, n_key = sizes
    stream, inv_rms, normed, grouped, keys_window, values_window, log_totals, mixed = saved
    rows = stream.shape[0]
    mid_grad_b = mid_grad.astype(bf16)
    out_term = rows_product(mid_grad_b, mixed)
    mixed_grad = product(mid_grad_b, wide[:, n_query + 2 * n_key :]).astype(bf16)
    query_grads, key_grads, value_grads = attend_back(
        grouped,
        keys_window,
        values_window,
        allowed,
        log_totals,
        mixed.reshape(grouped.shape),
        mixed_grad.reshape(grouped.shape),
    )
    both = jnp.concatenate(
        [key_grads.reshape(2 * rows, n_key), value_grads.reshape(2 * rows, n_key)], axis=1
    )
    back = from_behind(both[:rows].astype(bf16), "ctx", -1)
    own = both[rows:] + back.astype(f32)
    query_grad_b = rotate_back(query_grads.reshape(rows, -1, HEAD_DIM), cosine, sine)
    key_grad_b = rotate_back(own[:, :n_key].reshape(rows, -1, HEAD_DIM), cosine, sine)
    grads = jnp.concatenate(
        [
            query_grad_b.reshape(rows, n_query).astype(bf16),
            key_grad_b.reshape(rows, n_key).astype(bf16),
            own[:, n_key:].astype(bf16),
        ],
        axis=1,
    )
    normed_grad = sum_tensor(cols_product(grads, wide[:, : n_query + 2 * n_key]))
    wide_term = rows_product(normed, grads)
    term = jnp.concatenate([wide_term.astype(bf16), out_term.astype(bf16)], axis=1)
    part, gain_term = norm_backward(stream, inv_rms, gain, normed_grad)
    return mid_grad + part, gain_term, term


def on_device(
    inputs,
    out_grad,
    positions,
    attn_gain,
    w_query,
    w_key,
    w_value,
    w_out,
    ffn_gain,
    w_gate,
    w_up,
    w_down,
):
    core = lax.axis_index("pipe")
    first = core == 0
    shard = lax.axis_index("ctx")
    rows = inputs.shape[1]
    width = inputs.shape[2]
    n_query = w_query.shape[2]
    n_key = w_key.shape[2]
    half = w_gate.shape[2] // 2

    def pick(pair, index):
        return lax.dynamic_index_in_dim(pair, index, 0, keepdims=False)

    def mine_theirs(array, axis):
        size = array.shape[axis] // 2
        mine = lax.dynamic_slice_in_dim(array, core * size, size, axis)
        theirs = lax.dynamic_slice_in_dim(array, (1 - core) * size, size, axis)
        return mine, theirs

    gains = lax.all_gather(
        jnp.concatenate([attn_gain, ffn_gain], axis=0), ("pipe", "ctx"), axis=0, tiled=False
    )
    gains = gains.reshape(2, -1, 2, attn_gain.shape[1]).transpose(0, 2, 1, 3)
    gains = gains.reshape(2, 2, width).astype(f32)
    attn_shard = jnp.concatenate([w_query[0], w_key[0], w_value[0], w_out[0].T], axis=1)
    attn_wide = lax.all_gather(attn_shard, ("pipe", "ctx"), axis=0, tiled=True)
    attn_wide = attn_wide.reshape(2, width, -1)
    gate_mine, gate_theirs = mine_theirs(w_gate[0], 1)
    up_mine, up_theirs = mine_theirs(w_up[0], 1)
    down_mine, down_theirs = mine_theirs(w_down[0], 0)
    keep = jnp.concatenate([gate_mine, up_mine, down_mine.T], axis=1)
    give = jnp.concatenate([gate_theirs, up_theirs, down_theirs.T], axis=1)
    got = swap_cores(give)
    ffn_wide = [
        lax.all_gather(jnp.where(first, keep, got), "ctx", axis=0, tiled=True),
        lax.all_gather(jnp.where(first, got, keep), "ctx", axis=0, tiled=True),
    ]

    pos_row = pick(positions, core)
    cosine, sine = rope_tables(pos_row, HEAD_DIM)
    query_index = jnp.arange(rows, dtype=jnp.int32)
    key_index = jnp.arange(2 * rows, dtype=jnp.int32) - rows
    distance = query_index[:, None] - key_index[None, :]
    allowed = (distance >= 0) & (distance <= pos_row[:, None])
    place = (allowed, cosine, sine, (n_query, n_key))

    stream = pick(inputs, core)
    outs = []
    saved = []
    for section in range(2):
        middle, attn_saved = attention_forward(
            stream.astype(f32), gains[section, 0], attn_wide[section], place
        )
        state = ffn_forward_in(middle, gains[section, 1], ffn_wide[section], half)
        stream = ffn_forward_out(state, ffn_wide[section], half)
        outs.append(stream)
        saved.append((attn_saved, state))

    own_grad = pick(out_grad, core)
    both_grad = jnp.concatenate([own_grad, pick(out_grad, 1 - core)], axis=0)
    grads = [None, None]
    boundary = [None, None]
    for section in (1, 0):
        attn_saved, state = saved[section]
        mid_grad, ffn_gain_term, wide_term, down_term = ffn_backward(
            own_grad.astype(f32), both_grad, state, gains[section, 1], ffn_wide[section], half
        )
        down_share = lax.psum_scatter(down_term, "ctx", scatter_dimension=0, tiled=True)
        wide_share = lax.psum_scatter(wide_term, "ctx", scatter_dimension=0, tiled=True)
        stream_grad, attn_gain_term, attn_term = attention_backward(
            mid_grad, attn_saved, gains[section, 0], attn_wide[section], place
        )
        attn_mine, attn_theirs = mine_theirs(attn_term, 1)
        attn_sum = (attn_mine.astype(f32) + swap_cores(attn_theirs).astype(f32)).astype(bf16)
        attn_share = lax.psum_scatter(attn_sum, "ctx", scatter_dimension=0, tiled=True)
        own_grad = stream_grad.astype(bf16)
        boundary[section] = own_grad
        if section == 1:
            both_grad = jnp.concatenate([own_grad, swap_cores(own_grad)], axis=0)
        grads[section] = (wide_share, down_share, attn_share, attn_gain_term, ffn_gain_term)

    def to_owner(pair):
        keep_part = jnp.where(first, pair[0], pair[1])
        got_part = swap_cores(jnp.where(first, pair[1], pair[0]))
        return jnp.where(first, keep_part, got_part), jnp.where(first, got_part, keep_part)

    section_outputs = jnp.stack(to_owner(outs))
    boundary_grads = jnp.stack(to_owner(boundary))
    wide_a, wide_b = to_owner((grads[0][0], grads[1][0]))
    down_a, down_b = to_owner((grads[0][1], grads[1][1]))
    attn_full = jnp.concatenate(to_owner((grads[0][2], grads[1][2])), axis=1).astype(f32)
    gain_terms = jnp.stack([jnp.stack(grads[0][3:]), jnp.stack(grads[1][3:])])
    gain_sum = pick(lax.psum(gain_terms, ("pipe", "ctx")), core)
    own_width = attn_gain.shape[1]
    gain_own = lax.dynamic_slice_in_dim(gain_sum, shard * own_width, own_width, 1)
    key_at = n_query + n_key
    value_at = key_at + n_key
    return (
        section_outputs[None],
        boundary_grads[None],
        gain_own[0][None],
        attn_full[:, :n_query][None],
        attn_full[:, n_query:key_at][None],
        attn_full[:, key_at:value_at][None],
        attn_full[:, value_at:].T[None],
        gain_own[1][None],
        jnp.concatenate([wide_a[:, :half], wide_b[:, :half]], axis=1).astype(f32)[None],
        jnp.concatenate([wide_a[:, half:], wide_b[:, half:]], axis=1).astype(f32)[None],
        jnp.concatenate([down_a.T, down_b.T], axis=0).astype(f32)[None],
    )


def solution(mesh):
    in_specs = (
        P(None, "ctx", None),
        P(None, "ctx", None),
        P(None, "ctx"),
        P("pipe", "ctx"),
        P("pipe", "ctx", "tensor"),
        P("pipe", "ctx", "tensor"),
        P("pipe", "ctx", "tensor"),
        P("pipe", "tensor", "ctx"),
        P("pipe", "ctx"),
        P("pipe", "ctx", "tensor"),
        P("pipe", "ctx", "tensor"),
        P("pipe", "tensor", "ctx"),
    )
    out_specs = (
        P("pipe", None, "ctx", None),
        P("pipe", None, "ctx", None),
        P("pipe", "ctx"),
        P("pipe", "ctx", "tensor"),
        P("pipe", "ctx", "tensor"),
        P("pipe", "ctx", "tensor"),
        P("pipe", "tensor", "ctx"),
        P("pipe", "ctx"),
        P("pipe", "ctx", "tensor"),
        P("pipe", "ctx", "tensor"),
        P("pipe", "tensor", "ctx"),
    )
    return jax.shard_map(
        on_device, mesh=mesh, in_specs=in_specs, out_specs=out_specs, check_vma=False
    )
```

```python
import math

import jax
import jax.numpy as jnp
from jax import lax
from jax.experimental import pallas as pl
from jax.experimental.pallas import tpu as pltpu
from jax.sharding import PartitionSpec as P

HEADS = 32
KV_HEADS = 8
HEAD_DIM = 64
MAXLEN = 256

epsilon = 1e-05
rope_base = 500000.0
bf16 = jnp.bfloat16
f32 = jnp.float32


def swap_cores(block):
    return lax.ppermute(block, "pipe", [(0, 1), (1, 0)])


def from_behind(block, axis, distance):
    devices = range(lax.axis_size(axis))
    route = [(i - distance, i) for i in devices if i - distance in devices]
    return lax.ppermute(block, axis, route)


def ring_order(count):
    across = 1 << (count.bit_length() - 1) // 2
    down = count // across
    walk = [(0, x) for x in range(across)]
    for y in range(1, down):
        columns = range(1, across)
        walk += [(y, x) for x in (columns if y % 2 == 0 else reversed(columns))]
    walk += [(y, 0) for y in range(down - 1, 0, -1)]
    return [y * across + x for y, x in walk]


def ring_tools():
    count = lax.axis_size("ctx")
    order = ring_order(count)
    place = [order.index(device) for device in range(count)]
    ahead = [(order[i], order[(i + 1) % count]) for i in range(count)]
    behind = [(b, a) for a, b in ahead]
    at = jnp.asarray(place, jnp.int32)[lax.axis_index("ctx")]
    table = jnp.asarray(order * 2, jnp.int32)

    def device_at(distance):
        return table[at + distance % count]

    return count, ahead, behind, device_at


def ring_gather(block):
    count, ahead, behind, device_at = ring_tools()
    half = block.shape[1] // 2
    out = jnp.zeros((count,) + block.shape, block.dtype)

    def put(out, piece, distance, column=0):
        return lax.dynamic_update_slice(out, piece[None], (device_at(distance), 0, column))

    out = put(out, block, 0)
    from_back, from_front = block, block
    for distance in range(1, count // 2):
        from_back = lax.ppermute(from_back, "ctx", ahead)
        from_front = lax.ppermute(from_front, "ctx", behind)
        out = put(out, from_back, -distance)
        out = put(out, from_front, distance)
    left = lax.ppermute(from_back[:, :half], "ctx", ahead)
    right = lax.ppermute(from_front[:, half:], "ctx", behind)
    out = put(out, left, count // 2)
    return put(out, right, count // 2, half)


def ring_scatter(terms):
    count, ahead, behind, device_at = ring_tools()
    half = terms.shape[2] // 2

    def term(distance):
        return lax.dynamic_index_in_dim(terms, device_at(distance), 0, keepdims=False)

    far = term(count // 2)
    to_front = lax.ppermute(far[:, :half], "ctx", ahead)
    to_back = lax.ppermute(far[:, half:], "ctx", behind)
    for distance in range(count // 2 - 1, 0, -1):
        front, back = term(distance), term(-distance)
        if distance == count // 2 - 1:
            front = jnp.concatenate([add_bf16(front[:, :half], to_front), front[:, half:]], axis=1)
            back = jnp.concatenate([back[:, :half], add_bf16(back[:, half:], to_back)], axis=1)
        else:
            front, back = add_bf16(front, to_front), add_bf16(back, to_back)
        to_front = lax.ppermute(front, "ctx", ahead)
        to_back = lax.ppermute(back, "ctx", behind)
    return term(0).astype(f32) + to_front.astype(f32) + to_back.astype(f32)


def add_bf16(a, b):
    return (a.astype(f32) + b.astype(f32)).astype(bf16)


def token_terms_kernel(left_ref, right_ref, out_ref):
    out_ref[...] = lax.dot_general(
        left_ref[...], right_ref[...], (((0,), (0,)), ((), ())), preferred_element_type=f32
    ).astype(bf16)


def token_terms(left, right):
    tokens, width = left.shape
    units = right.shape[1]
    tile, column = min(width, 1024), min(units, 1024)
    return pl.pallas_call(
        token_terms_kernel,
        grid=(units // column, width // tile),
        in_specs=[
            pl.BlockSpec((tokens, tile), lambda j, i: (0, i)),
            pl.BlockSpec((tokens, column), lambda j, i: (0, j)),
        ],
        out_specs=pl.BlockSpec((tile, column), lambda j, i: (i, j)),
        out_shape=jax.ShapeDtypeStruct((width, units), bf16),
        compiler_params=pltpu.CompilerParams(vmem_limit_bytes=40 * 2**20),
        cost_estimate=pl.CostEstimate(
            flops=2 * tokens * width * units,
            bytes_accessed=2 * (width * units + tokens * width + tokens * units),
            transcendentals=0,
        ),
        name="token_terms",
    )(left, right)


def wide_outputs_kernel(core_ref, low_ref, high_ref, got_ref, gate_ref, up_ref):
    first = core_ref[0] == 0
    units = got_ref.shape[1] // 2
    keep = jnp.where(first, low_ref[...], high_ref[...])
    got = got_ref[...]
    for side in range(2):
        part = jnp.where(first == (side == 0), keep, got).astype(f32)
        gate_ref[:, side * units : (side + 1) * units] = part[:, :units]
        up_ref[:, side * units : (side + 1) * units] = part[:, units:]


def down_outputs_kernel(core_ref, low_ref, high_ref, got_ref, down_ref):
    first = core_ref[0] == 0
    units = got_ref.shape[1]
    keep = jnp.where(first, low_ref[...], high_ref[...])
    got = got_ref[...]
    for side in range(2):
        part = jnp.where(first == (side == 0), keep, got).astype(f32)
        down_ref[side * units : (side + 1) * units, :] = part.T


def section_outputs_call(kernel, core, low, high, got, specs, shapes, name):
    rows, wide = got.shape
    tile = 128
    block = pl.BlockSpec((tile, wide), lambda i, core: (i, 0))
    return pl.pallas_call(
        kernel,
        grid_spec=pltpu.PrefetchScalarGridSpec(
            num_scalar_prefetch=1,
            grid=(rows // tile,),
            in_specs=[block, block, block],
            out_specs=specs(tile),
        ),
        out_shape=shapes,
        compiler_params=pltpu.CompilerParams(vmem_limit_bytes=40 * 2**20),
        cost_estimate=pl.CostEstimate(
            flops=0, bytes_accessed=3 * rows * wide * 2 + 2 * rows * wide * 4, transcendentals=0
        ),
        name=name,
    )(core.reshape(1), low, high, got)


def wide_outputs(core, low, high, got):
    rows, units = got.shape[0], got.shape[1] // 2
    return section_outputs_call(
        wide_outputs_kernel,
        core,
        low,
        high,
        got,
        lambda tile: [pl.BlockSpec((tile, 2 * units), lambda i, core: (i, 0))] * 2,
        [jax.ShapeDtypeStruct((rows, 2 * units), f32)] * 2,
        "wide_outputs",
    )


def down_outputs(core, low, high, got):
    rows, units = got.shape
    return section_outputs_call(
        down_outputs_kernel,
        core,
        low,
        high,
        got,
        lambda tile: pl.BlockSpec((2 * units, tile), lambda i, core: (0, i)),
        jax.ShapeDtypeStruct((2 * units, rows), f32),
        "down_outputs",
    )


def pin(value, *others):
    return lax.optimization_barrier((value, *others))


def share_gains(terms):
    core, shard = lax.axis_index("pipe"), lax.axis_index("ctx")
    count = lax.axis_size("ctx")
    own = lax.dynamic_index_in_dim(terms, core, 0, keepdims=False)
    other = lax.dynamic_index_in_dim(terms, 1 - core, 0, keepdims=False)
    total = own + swap_cores(other)
    blocks = total.reshape(2, count, -1)

    def block(index):
        return lax.dynamic_index_in_dim(blocks, index, 1, keepdims=False)

    result = block(shard)
    for step in range(1, count):
        route = [(i, i ^ step) for i in range(count)]
        result = result + lax.ppermute(block(shard ^ step), "ctx", route)
    return result


def product(left, right):
    return lax.dot_general(
        left, right, (((1,), (0,)), ((), ())), preferred_element_type=f32
    )


def rows_product(left, right):
    return lax.dot_general(
        left, right, (((0,), (0,)), ((), ())), preferred_element_type=f32
    )


def cols_product(left, right):
    return lax.dot_general(
        left, right, (((1,), (1,)), ((), ())), preferred_element_type=f32
    )


def rope_tables(positions_row, width):
    frequency = jnp.exp(
        jnp.arange(width // 2, dtype=f32) * (-2.0 * math.log(rope_base) / width)
    )
    angles = positions_row.astype(f32)[:, None] * frequency[None, :]
    cosine_table = jnp.concatenate([jnp.cos(angles), jnp.cos(angles)], axis=1)
    sine_table = jnp.concatenate([jnp.sin(angles), jnp.sin(angles)], axis=1)
    return (cosine_table, sine_table)


def rotate(values, cosine_table, sine_table):
    half_width = values.shape[-1] // 2
    turned = jnp.concatenate([-values[..., half_width:], values[..., :half_width]], axis=-1)
    return values * cosine_table[:, None, :] + turned * sine_table[:, None, :]


def rotate_back(grads_in, cosine_table, sine_table):
    half_width = grads_in.shape[-1] // 2
    scaled = grads_in * sine_table[:, None, :]
    turned = jnp.concatenate([-scaled[..., half_width:], scaled[..., :half_width]], axis=-1)
    return grads_in * cosine_table[:, None, :] - turned


def norm_forward(stream, gain_vector):
    inv_rms = lax.rsqrt(jnp.mean(stream * stream, axis=-1) + epsilon)
    return ((stream * inv_rms[:, None] * gain_vector[None, :]).astype(bf16), inv_rms)


def norm_backward(stream, inv_rms, gain_vector, upstream):
    weighted = upstream * gain_vector[None, :]
    gain_grad = jnp.sum(upstream * stream * inv_rms[:, None], axis=0)
    inner_mean = jnp.mean(stream * weighted, axis=-1)
    stream_grad = (
        weighted * inv_rms[:, None] - stream * (inv_rms * inv_rms * inv_rms * inner_mean)[:, None]
    )
    return (stream_grad, gain_grad)


def scores(query_block, key_block, allowed):
    raw_scores = jnp.einsum(
        "qkgd,skd->kgqs", query_block, key_block, preferred_element_type=f32
    ) * HEAD_DIM ** (-0.5)
    return jnp.where(allowed[None, None], raw_scores, -1e30)


def attend(query_block, key_block, value_block, allowed):
    masked = scores(query_block, key_block, allowed)
    row_top = jnp.max(masked, axis=-1, keepdims=True)
    exponent = jnp.exp(masked - row_top)
    row_total = jnp.sum(exponent, axis=-1, keepdims=True)
    weights_block = (exponent / row_total).astype(bf16)
    mixed_rows = jnp.einsum(
        "kgqs,skd->qkgd", weights_block, value_block, preferred_element_type=f32
    )
    return (mixed_rows, (row_top + jnp.log(row_total))[..., 0])


def attend_back(
    query_block, key_block, value_block, allowed, log_block, mixed_block, grad_block
):
    masked = scores(query_block, key_block, allowed)
    probability = jnp.exp(masked - log_block[..., None])
    prob_grad = jnp.einsum(
        "qkgd,skd->kgqs", grad_block, value_block, preferred_element_type=f32
    )
    row_delta = jnp.transpose(
        jnp.sum(grad_block.astype(f32) * mixed_block.astype(f32), axis=-1),
        (1, 2, 0),
    )
    score_grad = (probability * (prob_grad - row_delta[..., None])).astype(bf16)
    scale_factor = HEAD_DIM ** (-0.5)
    query_grad = (
        jnp.einsum("kgqs,skd->qkgd", score_grad, key_block, preferred_element_type=f32)
        * scale_factor
    )
    key_part = (
        jnp.einsum("kgqs,qkgd->skd", score_grad, query_block, preferred_element_type=f32)
        * scale_factor
    )
    value_part = jnp.einsum(
        "kgqs,qkgd->skd",
        probability.astype(bf16),
        grad_block,
        preferred_element_type=f32,
    )
    return (query_grad, key_part, value_part)


def sum_tensor(partial, *others):
    partial = partial.astype(bf16)
    if others:
        partial, *others = pin(partial, *others)
    return lax.psum(partial, "tensor").astype(f32), *others


def own_share(partial, rows):
    arrived = swap_cores(partial[rows:].astype(bf16))
    return partial[:rows] + arrived.astype(f32)


def attention_forward(stream, gain, wide, place, *others):
    allowed, cosine, sine, sizes = place
    n_query, n_key = sizes
    rows = stream.shape[0]
    groups = n_key // HEAD_DIM
    normed, inv_rms = norm_forward(stream, gain)
    raw = product(normed, wide[:, : n_query + 2 * n_key])
    queries = rotate(raw[:, :n_query].reshape(rows, -1, HEAD_DIM), cosine, sine).astype(bf16)
    keys = rotate(
        raw[:, n_query : n_query + n_key].reshape(rows, -1, HEAD_DIM), cosine, sine
    ).astype(bf16)
    values = raw[:, n_query + n_key :].astype(bf16)
    own = jnp.concatenate([keys.reshape(rows, n_key), values], axis=1)
    tail = from_behind(own, "ctx", 1)
    window = jnp.concatenate([tail, own], axis=0)
    keys_window = window[:, :n_key].reshape(2 * rows, groups, HEAD_DIM)
    values_window = window[:, n_key:].reshape(2 * rows, groups, HEAD_DIM)
    grouped = queries.reshape(rows, groups, HEADS // KV_HEADS, HEAD_DIM)
    mixed_rows, log_totals = attend(grouped, keys_window, values_window, allowed)
    mixed = mixed_rows.astype(bf16).reshape(rows, n_query)
    partial = cols_product(mixed, wide[:, n_query + 2 * n_key :])
    total, *others = sum_tensor(partial, *others)
    saved = (stream, inv_rms, normed, grouped, keys_window, values_window, log_totals, mixed)
    return stream + total, saved, *others


def ffn_forward_in(middle, gain, wide, hidden_width):
    normed, inv_rms = norm_forward(middle, gain)
    both = jnp.concatenate([normed, swap_cores(normed)], axis=0)
    gate_up = product(both, wide)
    gate = gate_up[:, :hidden_width]
    up = gate_up[:, hidden_width:]
    hidden = (jax.nn.silu(gate) * up).astype(bf16)
    return (middle, inv_rms, both, gate, up, hidden)


def ffn_forward_out(state, down, *others):
    middle, hidden = state[0], state[-1]
    partial = own_share(cols_product(hidden, down), middle.shape[0])
    total, *others = sum_tensor(partial, *others)
    return (middle + total).astype(bf16), *others


def ffn_backward(upstream, upstream_both, state, gain, wide, down, *others):
    middle, inv_rms, both, gate, up, hidden = state
    hidden_grad = product(upstream_both, down)
    sigmoid_gate = jax.nn.sigmoid(gate)
    gate_grad = (hidden_grad * up * sigmoid_gate * (1.0 + gate * (1.0 - sigmoid_gate))).astype(bf16)
    up_grad = (hidden_grad * gate * sigmoid_gate).astype(bf16)
    grads = jnp.concatenate([gate_grad, up_grad], axis=1)
    partial = own_share(cols_product(grads, wide), middle.shape[0])
    normed_grad, *others = sum_tensor(partial, *others)
    down_share = lax.psum_scatter(
        token_terms(upstream_both, hidden), "ctx", scatter_dimension=0, tiled=True
    )
    normed_grad, terms = pin(normed_grad, token_terms(both, grads))
    wide_share = lax.psum_scatter(terms, "ctx", scatter_dimension=0, tiled=True)
    mid_part, gain_term = norm_backward(middle, inv_rms, gain, normed_grad)
    return upstream + mid_part, gain_term, wide_share, down_share, *others


def attention_backward(mid_grad, saved, gain, wide, place, *others):
    allowed, cosine, sine, sizes = place
    n_query, n_key = sizes
    stream, inv_rms, normed, grouped, keys_window, values_window, log_totals, mixed = saved
    rows = stream.shape[0]
    mid_grad_b = mid_grad.astype(bf16)
    mixed_grad = product(mid_grad_b, wide[:, n_query + 2 * n_key :]).astype(bf16)
    query_grads, key_grads, value_grads = attend_back(
        grouped,
        keys_window,
        values_window,
        allowed,
        log_totals,
        mixed.reshape(grouped.shape),
        mixed_grad.reshape(grouped.shape),
    )
    both = jnp.concatenate(
        [key_grads.reshape(2 * rows, n_key), value_grads.reshape(2 * rows, n_key)], axis=1
    )
    back = from_behind(both[:rows].astype(bf16), "ctx", -1)
    own = both[rows:] + back.astype(f32)
    query_grad_b = rotate_back(query_grads.reshape(rows, -1, HEAD_DIM), cosine, sine)
    key_grad_b = rotate_back(own[:, :n_key].reshape(rows, -1, HEAD_DIM), cosine, sine)
    grads = jnp.concatenate(
        [
            query_grad_b.reshape(rows, n_query).astype(bf16),
            key_grad_b.reshape(rows, n_key).astype(bf16),
            own[:, n_key:].astype(bf16),
        ],
        axis=1,
    )
    partial = cols_product(grads, wide[:, : n_query + 2 * n_key])
    normed_grad, *others = sum_tensor(partial, *others)
    terms = jnp.concatenate(
        [rows_product(normed, grads).astype(bf16), rows_product(mid_grad_b, mixed).astype(bf16)],
        axis=1,
    )
    count = lax.axis_size("ctx")
    terms = terms.reshape(count, 2, -1, terms.shape[1])
    core = lax.axis_index("pipe")
    mine = lax.dynamic_index_in_dim(terms, core, 1, keepdims=False)
    theirs = lax.dynamic_index_in_dim(terms, 1 - core, 1, keepdims=False)
    normed_grad, summed = pin(normed_grad, add_bf16(mine, swap_cores(theirs)))
    part, gain_term = norm_backward(stream, inv_rms, gain, normed_grad)
    return mid_grad + part, gain_term, ring_scatter(summed).astype(bf16), *others


def on_device(
    inputs,
    out_grad,
    positions,
    attn_gain,
    w_query,
    w_key,
    w_value,
    w_out,
    ffn_gain,
    w_gate,
    w_up,
    w_down,
):
    core = lax.axis_index("pipe")
    first = core == 0
    shard = lax.axis_index("ctx")
    rows = inputs.shape[1]
    width = inputs.shape[2]
    n_query = w_query.shape[2]
    n_key = w_key.shape[2]
    half = w_gate.shape[2] // 2

    def pick(pair, index):
        return lax.dynamic_index_in_dim(pair, index, 0, keepdims=False)

    def mine_theirs(array, axis):
        size = array.shape[axis] // 2
        mine = lax.dynamic_slice_in_dim(array, core * size, size, axis)
        theirs = lax.dynamic_slice_in_dim(array, (1 - core) * size, size, axis)
        return mine, theirs

    count = lax.axis_size("ctx")
    gain_row = jnp.concatenate([attn_gain, ffn_gain], axis=1)
    attn_shard = jnp.concatenate([w_query[0], w_key[0], w_value[0], w_out[0].T], axis=1)
    wide_columns = attn_shard.shape[1]
    gain_rows = jnp.pad(gain_row, ((0, 15), (0, wide_columns - gain_row.shape[1])))
    rows_mine, rows_theirs = mine_theirs(attn_shard, 0)
    attn_keep = jnp.concatenate([rows_mine, gain_rows], axis=0)
    attn_got = swap_cores(jnp.concatenate([rows_theirs, gain_rows], axis=0))

    def attn_weights(pieces):
        got = swap_cores(pieces)
        both = jnp.stack([jnp.where(first, pieces, got), jnp.where(first, got, pieces)], axis=1)
        part_rows = attn_shard.shape[0] // 2
        wide = both[:, :, :part_rows].reshape(width, wide_columns)
        row = pieces[:, part_rows, : gain_row.shape[1]].astype(f32)
        return wide, row.reshape(count, 2, -1).transpose(1, 0, 2).reshape(2, width)

    gate_mine, gate_theirs = mine_theirs(w_gate[0], 1)
    up_mine, up_theirs = mine_theirs(w_up[0], 1)
    wide_keep = jnp.concatenate([gate_mine, up_mine], axis=1)
    wide_got = swap_cores(jnp.concatenate([gate_theirs, up_theirs], axis=1))
    down_mine, down_theirs = mine_theirs(w_down[0], 0)
    down_keep, down_got = down_mine.T, swap_cores(down_theirs.T)

    def for_sections(keep, got):
        return [jnp.where(first, keep, got), jnp.where(first, got, keep)]

    def gather(shard_part):
        return lax.all_gather(shard_part, "ctx", axis=0, tiled=True)

    attn_parts = for_sections(attn_keep, attn_got)
    wide_parts = for_sections(wide_keep, wide_got)
    down_parts = for_sections(down_keep, down_got)
    wide_low = gather(wide_parts[0])
    attn_pieces, attn_parts[1], wide_parts[1], *down_parts = pin(
        ring_gather(attn_parts[0]), attn_parts[1], wide_parts[1], *down_parts
    )
    attn_low, gains_low = attn_weights(attn_pieces)
    down_low = gather(down_parts[0])
    wide_high = gather(wide_parts[1])
    down_high = gather(down_parts[1])

    pos_row = pick(positions, core)
    cosine, sine = rope_tables(pos_row, HEAD_DIM)
    query_index = jnp.arange(rows, dtype=jnp.int32)
    key_index = jnp.arange(2 * rows, dtype=jnp.int32) - rows
    distance = query_index[:, None] - key_index[None, :]
    allowed = (distance >= 0) & (distance <= pos_row[:, None])
    place = (allowed, cosine, sine, (n_query, n_key))

    stream = pick(inputs, core)
    middle, attn_saved_low, wide_low, attn_part_high = attention_forward(
        stream.astype(f32), gains_low[0], attn_low, place, wide_low, attn_parts[1]
    )
    state_low = ffn_forward_in(middle, gains_low[1], wide_low, half)
    out_low, attn_pieces = ffn_forward_out(state_low, down_low, ring_gather(attn_part_high))
    attn_high, gains_high = attn_weights(attn_pieces)
    middle, attn_saved_high, wide_high = attention_forward(
        out_low.astype(f32), gains_high[0], attn_high, place, wide_high
    )
    state_high = ffn_forward_in(middle, gains_high[1], wide_high, half)

    own_grad = pick(out_grad, core)
    both_grad = jnp.concatenate([own_grad, pick(out_grad, 1 - core)], axis=0)
    mid_grad, ffn_gain_high, wide_share_high, down_share_high = ffn_backward(
        own_grad.astype(f32), both_grad, state_high, gains_high[1], wide_high, down_high
    )
    stream_grad, attn_gain_high, attn_share_high, down_share_high = attention_backward(
        mid_grad, attn_saved_high, gains_high[0], attn_high, place, down_share_high
    )
    boundary_high = stream_grad.astype(bf16)
    both_grad = jnp.concatenate([boundary_high, swap_cores(boundary_high)], axis=0)
    mid_grad, ffn_gain_low, wide_share_low, down_share_low, wide_share_high = ffn_backward(
        boundary_high.astype(f32),
        both_grad,
        state_low,
        gains_low[1],
        wide_low,
        down_low,
        wide_share_high,
    )
    stream_grad, attn_gain_low, attn_share_low, down_share_low, attn_share_high = (
        attention_backward(
            mid_grad, attn_saved_low, gains_low[0], attn_low, place, down_share_low, attn_share_high
        )
    )
    boundary_low = stream_grad.astype(bf16)
    (out_high,) = ffn_forward_out(state_high, down_high)

    def from_other(low, high):
        return swap_cores(jnp.where(first, high, low))

    def to_owner(low, high):
        keep_part = jnp.where(first, low, high)
        got_part = from_other(low, high)
        return jnp.where(first, keep_part, got_part), jnp.where(first, got_part, keep_part)

    section_outputs = jnp.stack(to_owner(out_low, out_high))
    boundary_grads = jnp.stack(to_owner(boundary_low, boundary_high))
    down_pair = (down_share_low, down_share_high)
    down_out = down_outputs(core, *down_pair, from_other(*down_pair))
    wide_pair = (wide_share_low, wide_share_high)
    gate_out, up_out = wide_outputs(core, *wide_pair, from_other(*wide_pair))
    attn_full = jnp.concatenate(to_owner(attn_share_low, attn_share_high), axis=0).astype(f32)
    gains_out = share_gains(
        jnp.stack(
            [jnp.stack([attn_gain_low, ffn_gain_low]), jnp.stack([attn_gain_high, ffn_gain_high])]
        )
    )
    key_at = n_query + n_key
    value_at = key_at + n_key
    return (
        section_outputs[None],
        boundary_grads[None],
        gains_out[:1],
        attn_full[:, :n_query][None],
        attn_full[:, n_query:key_at][None],
        attn_full[:, key_at:value_at][None],
        attn_full[:, value_at:].T[None],
        gains_out[1:],
        gate_out[None],
        up_out[None],
        down_out[None],
    )


def solution(mesh):
    in_specs = (
        P(None, "ctx", None),
        P(None, "ctx", None),
        P(None, "ctx"),
        P("pipe", "ctx"),
        P("pipe", "ctx", "tensor"),
        P("pipe", "ctx", "tensor"),
        P("pipe", "ctx", "tensor"),
        P("pipe", "tensor", "ctx"),
        P("pipe", "ctx"),
        P("pipe", "ctx", "tensor"),
        P("pipe", "ctx", "tensor"),
        P("pipe", "tensor", "ctx"),
    )
    out_specs = (
        P("pipe", None, "ctx", None),
        P("pipe", None, "ctx", None),
        P("pipe", "ctx"),
        P("pipe", "ctx", "tensor"),
        P("pipe", "ctx", "tensor"),
        P("pipe", "ctx", "tensor"),
        P("pipe", "tensor", "ctx"),
        P("pipe", "ctx"),
        P("pipe", "ctx", "tensor"),
        P("pipe", "ctx", "tensor"),
        P("pipe", "tensor", "ctx"),
    )
    return jax.shard_map(
        on_device, mesh=mesh, in_specs=in_specs, out_specs=out_specs, check_vma=False
    )
```

```python
import functools
import math

import jax
import jax.numpy as jnp
from jax import lax
from jax.experimental import pallas as pl
from jax.experimental.pallas import tpu as pltpu
from jax.sharding import PartitionSpec as P

HEADS = 32
KV_HEADS = 8
HEAD_DIM = 64
MAXLEN = 256

epsilon = 1e-05
rope_base = 500000.0
bf16 = jnp.bfloat16
f32 = jnp.float32


def swap_cores(block):
    return lax.ppermute(block, "pipe", [(0, 1), (1, 0)])


def from_behind(block, axis, distance):
    devices = range(lax.axis_size(axis))
    route = [(i - distance, i) for i in devices if i - distance in devices]
    return lax.ppermute(block, axis, route)


def ring_order(count):
    across = 1 << (count.bit_length() - 1) // 2
    down = count // across
    walk = [(0, x) for x in range(across)]
    for y in range(1, down):
        columns = range(1, across)
        walk += [(y, x) for x in (columns if y % 2 == 0 else reversed(columns))]
    walk += [(y, 0) for y in range(down - 1, 0, -1)]
    return [y * across + x for y, x in walk]


def ring_tools():
    count = lax.axis_size("ctx")
    order = ring_order(count)
    place = [order.index(device) for device in range(count)]
    ahead = [(order[i], order[(i + 1) % count]) for i in range(count)]
    behind = [(b, a) for a, b in ahead]
    at = jnp.asarray(place, jnp.int32)[lax.axis_index("ctx")]
    table = jnp.asarray(order * 2, jnp.int32)

    def device_at(distance):
        return table[at + distance % count]

    return count, ahead, behind, device_at


def ring_gather(block):
    count, ahead, behind, device_at = ring_tools()
    half = block.shape[1] // 2
    out = jnp.zeros((count,) + block.shape, block.dtype)

    def put(out, piece, distance, column=0):
        return lax.dynamic_update_slice(out, piece[None], (device_at(distance), 0, column))

    out = put(out, block, 0)
    from_back, from_front = block, block
    for distance in range(1, count // 2):
        from_back = lax.ppermute(from_back, "ctx", ahead)
        from_front = lax.ppermute(from_front, "ctx", behind)
        out = put(out, from_back, -distance)
        out = put(out, from_front, distance)
    left = lax.ppermute(from_back[:, :half], "ctx", ahead)
    right = lax.ppermute(from_front[:, half:], "ctx", behind)
    out = put(out, left, count // 2)
    return put(out, right, count // 2, half)


def ring_scatter(terms):
    count, ahead, behind, device_at = ring_tools()
    half = terms.shape[2] // 2

    def term(distance):
        return lax.dynamic_index_in_dim(terms, device_at(distance), 0, keepdims=False)

    far = term(count // 2)
    to_front = lax.ppermute(far[:, :half], "ctx", ahead)
    to_back = lax.ppermute(far[:, half:], "ctx", behind)
    for distance in range(count // 2 - 1, 0, -1):
        front, back = term(distance), term(-distance)
        if distance == count // 2 - 1:
            front = jnp.concatenate([add_bf16(front[:, :half], to_front), front[:, half:]], axis=1)
            back = jnp.concatenate([back[:, :half], add_bf16(back[:, half:], to_back)], axis=1)
        else:
            front, back = add_bf16(front, to_front), add_bf16(back, to_back)
        to_front = lax.ppermute(front, "ctx", ahead)
        to_back = lax.ppermute(back, "ctx", behind)
    return term(0).astype(f32) + to_front.astype(f32) + to_back.astype(f32)


def add_bf16(a, b):
    return (a.astype(f32) + b.astype(f32)).astype(bf16)


def token_terms_kernel(left_ref, right_ref, out_ref):
    out_ref[...] = lax.dot_general(
        left_ref[...], right_ref[...], (((0,), (0,)), ((), ())), preferred_element_type=f32
    ).astype(bf16)


def token_terms(left, right):
    tokens, width = left.shape
    units = right.shape[1]
    tile, column = min(width, 1024), min(units, 1024)
    return pl.pallas_call(
        token_terms_kernel,
        grid=(units // column, width // tile),
        in_specs=[
            pl.BlockSpec((tokens, tile), lambda j, i: (0, i)),
            pl.BlockSpec((tokens, column), lambda j, i: (0, j)),
        ],
        out_specs=pl.BlockSpec((tile, column), lambda j, i: (i, j)),
        out_shape=jax.ShapeDtypeStruct((width, units), bf16),
        compiler_params=pltpu.CompilerParams(vmem_limit_bytes=40 * 2**20),
        cost_estimate=pl.CostEstimate(
            flops=2 * tokens * width * units,
            bytes_accessed=2 * (width * units + tokens * width + tokens * units),
            transcendentals=0,
        ),
        name="token_terms",
    )(left, right)


def attention_terms_kernel(normed_ref, mid_grad_ref, grads_ref, mixed_ref, out_ref):
    n_grads = grads_ref.shape[1]
    half = out_ref.shape[1]
    rows = (((0,), (0,)), ((), ()))
    inner = lax.dot_general(normed_ref[...], grads_ref[...], rows, preferred_element_type=f32)
    outer = lax.dot_general(mid_grad_ref[...], mixed_ref[...], rows, preferred_element_type=f32)
    for part in range(2):
        part_rows = slice(part * half, (part + 1) * half)
        out_ref[part, :, :n_grads] = inner[part_rows].astype(bf16)
        out_ref[part, :, n_grads:] = outer[part_rows].astype(bf16)


def attention_terms(normed, mid_grad, grads, mixed, count):
    tokens, width = normed.shape
    columns = grads.shape[1] + mixed.shape[1]
    tile = width // count
    return pl.pallas_call(
        attention_terms_kernel,
        grid=(count,),
        in_specs=[
            pl.BlockSpec((tokens, tile), lambda i: (0, i)),
            pl.BlockSpec((tokens, tile), lambda i: (0, i)),
            pl.BlockSpec((tokens, grads.shape[1]), lambda i: (0, 0)),
            pl.BlockSpec((tokens, mixed.shape[1]), lambda i: (0, 0)),
        ],
        out_specs=pl.BlockSpec((2, None, tile // 2, columns), lambda i: (0, i, 0, 0)),
        out_shape=jax.ShapeDtypeStruct((2, count, tile // 2, columns), bf16),
        compiler_params=pltpu.CompilerParams(vmem_limit_bytes=40 * 2**20),
        cost_estimate=pl.CostEstimate(
            flops=2 * tokens * width * columns,
            bytes_accessed=2 * (width * columns + 2 * tokens * width + tokens * columns),
            transcendentals=0,
        ),
        name="attention_terms",
    )(normed, mid_grad, grads, mixed)


def section_stack_kernel(core_ref, low_ref, high_ref, got_ref, out_ref):
    keep = jnp.where(core_ref[0] == 0, low_ref[...], high_ref[...])
    out_ref[...] = jnp.where(core_ref[0] == pl.program_id(0), keep, got_ref[...])


def section_stack(core, low, high, got):
    rows, width = got.shape
    block = pl.BlockSpec((rows, width), lambda i, core: (0, 0))
    return pl.pallas_call(
        section_stack_kernel,
        grid_spec=pltpu.PrefetchScalarGridSpec(
            num_scalar_prefetch=1,
            grid=(2,),
            in_specs=[block, block, block],
            out_specs=pl.BlockSpec((None, rows, width), lambda i, core: (i, 0, 0)),
        ),
        out_shape=jax.ShapeDtypeStruct((2, rows, width), got.dtype),
        compiler_params=pltpu.CompilerParams(vmem_limit_bytes=40 * 2**20),
        cost_estimate=pl.CostEstimate(
            flops=0, bytes_accessed=5 * rows * width * 2, transcendentals=0
        ),
        name="section_stack",
    )(core.reshape(1), low, high, got)


def wide_outputs_kernel(core_ref, low_ref, high_ref, got_ref, gate_ref, up_ref):
    first = core_ref[0] == 0
    units = got_ref.shape[1] // 2
    keep = jnp.where(first, low_ref[...], high_ref[...])
    got = got_ref[...]
    for side in range(2):
        part = jnp.where(first == (side == 0), keep, got).astype(f32)
        gate_ref[:, side * units : (side + 1) * units] = part[:, :units]
        up_ref[:, side * units : (side + 1) * units] = part[:, units:]


def down_outputs_kernel(core_ref, low_ref, high_ref, got_ref, down_ref):
    first = core_ref[0] == 0
    units = got_ref.shape[1]
    keep = jnp.where(first, low_ref[...], high_ref[...])
    got = got_ref[...]
    for side in range(2):
        part = jnp.where(first == (side == 0), keep, got).astype(f32)
        down_ref[side * units : (side + 1) * units, :] = part.T


def section_outputs_call(kernel, core, low, high, got, specs, shapes, name):
    rows, wide = got.shape
    tile = 128
    block = pl.BlockSpec((tile, wide), lambda i, core: (i, 0))
    return pl.pallas_call(
        kernel,
        grid_spec=pltpu.PrefetchScalarGridSpec(
            num_scalar_prefetch=1,
            grid=(rows // tile,),
            in_specs=[block, block, block],
            out_specs=specs(tile),
        ),
        out_shape=shapes,
        compiler_params=pltpu.CompilerParams(vmem_limit_bytes=40 * 2**20),
        cost_estimate=pl.CostEstimate(
            flops=0, bytes_accessed=3 * rows * wide * 2 + 2 * rows * wide * 4, transcendentals=0
        ),
        name=name,
    )(core.reshape(1), low, high, got)


def wide_outputs(core, low, high, got):
    rows, units = got.shape[0], got.shape[1] // 2
    return section_outputs_call(
        wide_outputs_kernel,
        core,
        low,
        high,
        got,
        lambda tile: [pl.BlockSpec((tile, 2 * units), lambda i, core: (i, 0))] * 2,
        [jax.ShapeDtypeStruct((rows, 2 * units), f32)] * 2,
        "wide_outputs",
    )


def down_outputs(core, low, high, got):
    rows, units = got.shape
    return section_outputs_call(
        down_outputs_kernel,
        core,
        low,
        high,
        got,
        lambda tile: pl.BlockSpec((2 * units, tile), lambda i, core: (0, i)),
        jax.ShapeDtypeStruct((2 * units, rows), f32),
        "down_outputs",
    )


def pin(value, *others):
    return lax.optimization_barrier((value, *others))


def share_gains(terms):
    core, shard = lax.axis_index("pipe"), lax.axis_index("ctx")
    count = lax.axis_size("ctx")
    own = lax.dynamic_index_in_dim(terms, core, 0, keepdims=False)
    other = lax.dynamic_index_in_dim(terms, 1 - core, 0, keepdims=False)
    total = own + swap_cores(other)
    blocks = total.reshape(2, count, -1)

    def block(index):
        return lax.dynamic_index_in_dim(blocks, index, 1, keepdims=False)

    result = block(shard)
    for step in range(1, count):
        route = [(i, i ^ step) for i in range(count)]
        result = result + lax.ppermute(block(shard ^ step), "ctx", route)
    return result


def product(left, right):
    return lax.dot_general(
        left, right, (((1,), (0,)), ((), ())), preferred_element_type=f32
    )


def rows_product(left, right):
    return lax.dot_general(
        left, right, (((0,), (0,)), ((), ())), preferred_element_type=f32
    )


def cols_product(left, right):
    return lax.dot_general(
        left, right, (((1,), (1,)), ((), ())), preferred_element_type=f32
    )


def norm_forward(stream, gain_vector):
    inv_rms = lax.rsqrt(jnp.mean(stream * stream, axis=-1) + epsilon)
    return ((stream * inv_rms[:, None] * gain_vector[None, :]).astype(bf16), inv_rms)


def norm_backward(stream, inv_rms, gain_vector, upstream):
    weighted = upstream * gain_vector[None, :]
    gain_grad = jnp.sum(upstream * stream * inv_rms[:, None], axis=0)
    inner_mean = jnp.mean(stream * weighted, axis=-1)
    stream_grad = (
        weighted * inv_rms[:, None] - stream * (inv_rms * inv_rms * inv_rms * inner_mean)[:, None]
    )
    return (stream_grad, gain_grad)


def sum_tensor(partial, *others):
    partial = partial.astype(bf16)
    if others:
        partial, *others = pin(partial, *others)
    return lax.psum(partial, "tensor").astype(f32), *others


def own_share(partial, rows):
    arrived = swap_cores(partial[rows:].astype(bf16))
    return partial[:rows] + arrived.astype(f32)


def half_swap(values):
    lanes = lax.broadcasted_iota(jnp.int32, values.shape, 1)
    count = values.shape[1]
    quarter = HEAD_DIM // 2
    return jnp.where(
        lanes % HEAD_DIM < quarter,
        pltpu.roll(values, count - quarter, 1),
        pltpu.roll(values, quarter, 1),
    )


def wide_table(table, columns):
    return jnp.concatenate([table] * (columns // table.shape[1]), axis=1)


def rope_tables(positions_row, width):
    frequency = jnp.exp(
        jnp.arange(width // 2, dtype=f32) * (-2.0 * math.log(rope_base) / width)
    )
    angles = positions_row.astype(f32)[:, None] * frequency[None, :]
    cosine, sine = jnp.cos(angles), jnp.sin(angles)
    return (
        jnp.concatenate([cosine] * 4, axis=1),
        jnp.concatenate([-sine, sine] * 2, axis=1),
    )


def head_inputs_kernel(sizes, stream_ref, gain_ref, wide_ref, cos_ref, sin_ref,
                       normed_ref, rms_ref, query_ref, own_ref):
    n_query, n_key = sizes
    stream = stream_ref[...].astype(f32)
    inv_rms = lax.rsqrt(jnp.mean(stream * stream, axis=1, keepdims=True) + epsilon)
    normed = (stream * inv_rms * gain_ref[...]).astype(bf16)
    normed_ref[...] = normed
    rms_ref[...] = inv_rms
    raw = jnp.dot(normed, wide_ref[...], preferred_element_type=f32)
    turned = raw[:, : n_query + n_key]
    cosine = wide_table(cos_ref[...], n_query + n_key)
    sine = wide_table(sin_ref[...], n_query + n_key)
    turned = turned * cosine + half_swap(turned) * sine
    query_ref[...] = turned[:, :n_query].astype(bf16)
    own_ref[:, :n_key] = turned[:, n_query:].astype(bf16)
    own_ref[:, n_key:] = raw[:, n_query + n_key :].astype(bf16)


def params(megabytes=48):
    return pltpu.CompilerParams(vmem_limit_bytes=megabytes * 2**20)


def cost(flops, bytes_accessed, transcendentals=0):
    return pl.CostEstimate(
        flops=flops, bytes_accessed=bytes_accessed, transcendentals=transcendentals
    )


def head_inputs(stream, gain, wide, tables, sizes):
    n_query, n_key = sizes
    rows, width = stream.shape
    columns = n_query + 2 * n_key
    whole = lambda *shape: pl.BlockSpec(shape, lambda i: (0,) * len(shape))
    return pl.pallas_call(
        functools.partial(head_inputs_kernel, sizes),
        grid=(1,),
        in_specs=[
            whole(rows, width),
            whole(1, width),
            whole(width, columns),
            whole(rows, 2 * HEAD_DIM),
            whole(rows, 2 * HEAD_DIM),
        ],
        out_specs=[whole(rows, width), whole(rows, 1), whole(rows, n_query), whole(rows, 2 * n_key)],
        out_shape=[
            jax.ShapeDtypeStruct((rows, width), bf16),
            jax.ShapeDtypeStruct((rows, 1), f32),
            jax.ShapeDtypeStruct((rows, n_query), bf16),
            jax.ShapeDtypeStruct((rows, 2 * n_key), bf16),
        ],
        compiler_params=params(),
        cost_estimate=cost(2 * rows * width * columns, 2 * width * (columns + 4 * rows)),
        name="head_inputs",
    )(stream, gain[None], wide, *tables)


def masked_scores(query, keys, allowed):
    raw = lax.dot_general(query, keys, (((1,), (1,)), ((), ())), preferred_element_type=f32)
    return jnp.where(allowed, raw * HEAD_DIM ** (-0.5), -1e30)


def allowed_pairs(pos, rows):
    distance = (
        lax.broadcasted_iota(jnp.int32, (rows, 2 * rows), 0)
        - lax.broadcasted_iota(jnp.int32, (rows, 2 * rows), 1)
        + rows
    )
    return (distance >= 0) & (distance <= pos)


def head_slice(index):
    return slice(index * HEAD_DIM, (index + 1) * HEAD_DIM)


def mix_kernel(n_key, pos_ref, query_ref, tail_ref, own_ref, wide_ref,
               mixed_ref, log_ref, partial_ref, window, mixed_all):
    rows, n_query = query_ref.shape

    @pl.when(pl.program_id(0) == 0)
    def _():
        window[:rows] = tail_ref[...]
        window[rows:] = own_ref[...]
        allowed = allowed_pairs(pos_ref[...], rows)
        group = HEADS // KV_HEADS
        logs, mixed = [], []
        for head in range(n_query // HEAD_DIM):
            keys = window[:, head_slice(head // group)]
            values = window[:, head_slice((n_key // HEAD_DIM) + head // group)]
            masked = masked_scores(query_ref[:, head_slice(head)], keys, allowed)
            top = jnp.max(masked, axis=1, keepdims=True)
            exponent = jnp.exp(masked - top)
            total = jnp.sum(exponent, axis=1, keepdims=True)
            weights = (exponent * (1.0 / total)).astype(bf16)
            mixed.append(jnp.dot(weights, values, preferred_element_type=f32).astype(bf16))
            logs.append(top + jnp.log(total))
        everything = jnp.concatenate(mixed, axis=1)
        mixed_all[...] = everything
        mixed_ref[...] = everything
        log_ref[...] = jnp.concatenate(logs, axis=1)

    partial_ref[...] = lax.dot_general(
        mixed_all[...],
        wide_ref[:, wide_ref.shape[1] - n_query :],
        (((1,), (1,)), ((), ())),
        preferred_element_type=f32,
    ).astype(bf16)


def mix(pos, queries, tail, own, wide, n_key):
    rows, n_query = queries.shape
    width, columns = wide.shape
    tile = 512
    heads = n_query // HEAD_DIM
    whole = lambda *shape: pl.BlockSpec(shape, lambda i: (0,) * len(shape))
    return pl.pallas_call(
        functools.partial(mix_kernel, n_key),
        grid=(width // tile,),
        in_specs=[
            whole(rows, 1),
            whole(rows, n_query),
            whole(rows, 2 * n_key),
            whole(rows, 2 * n_key),
            pl.BlockSpec((tile, columns), lambda i: (i, 0)),
        ],
        out_specs=[
            whole(rows, n_query),
            whole(rows, heads),
            pl.BlockSpec((rows, tile), lambda i: (0, i)),
        ],
        out_shape=[
            jax.ShapeDtypeStruct((rows, n_query), bf16),
            jax.ShapeDtypeStruct((rows, heads), f32),
            jax.ShapeDtypeStruct((rows, width), bf16),
        ],
        scratch_shapes=[pltpu.VMEM((2 * rows, 2 * n_key), bf16), pltpu.VMEM((rows, n_query), bf16)],
        compiler_params=params(),
        cost_estimate=cost(
            2 * rows * n_query * (width + 4 * rows), 2 * width * (columns + rows), 2 * rows * rows * heads
        ),
        name="mix",
    )(pos, queries, tail, own, wide)


def mix_back_kernel(n_key, pos_ref, query_ref, tail_ref, own_ref, mixed_ref, log_ref, cos_ref, sin_ref,
                    mid_grad_ref, wide_ref, query_grad_ref, back_ref, own_grad_ref, mid_b_ref,
                    window, mixed_grad):
    rows, n_query = query_ref.shape
    step = pl.program_id(0)
    mid_b = mid_grad_ref[...].astype(bf16)
    mid_b_ref[...] = mid_b
    part = jnp.dot(mid_b, wide_ref[:, wide_ref.shape[1] - n_query :], preferred_element_type=f32)

    @pl.when(step == 0)
    def _():
        mixed_grad[...] = part

    @pl.when(step > 0)
    def _():
        mixed_grad[...] += part

    @pl.when(step == pl.num_programs(0) - 1)
    def _():
        window[:rows] = tail_ref[...]
        window[rows:] = own_ref[...]
        allowed = allowed_pairs(pos_ref[...], rows)
        group = HEADS // KV_HEADS
        groups = n_key // HEAD_DIM
        scale = HEAD_DIM ** (-0.5)
        grads = mixed_grad[...].astype(bf16)
        over_rows = (((0,), (0,)), ((), ()))
        over_columns = (((1,), (1,)), ((), ()))
        query_grads, key_grads, value_grads = [], [None] * groups, [None] * groups
        for head in range(n_query // HEAD_DIM):
            at = head // group
            keys = window[:, head_slice(at)]
            values = window[:, head_slice(groups + at)]
            query = query_ref[:, head_slice(head)]
            grad = grads[:, head_slice(head)]
            masked = masked_scores(query, keys, allowed)
            prob = jnp.exp(masked - log_ref[:, head : head + 1])
            prob_grad = lax.dot_general(grad, values, over_columns, preferred_element_type=f32)
            delta = jnp.sum(
                grad.astype(f32) * mixed_ref[:, head_slice(head)].astype(f32), axis=1, keepdims=True
            )
            score_grad = (prob * (prob_grad - delta)).astype(bf16)
            query_grads.append(jnp.dot(score_grad, keys, preferred_element_type=f32))
            key_part = lax.dot_general(score_grad, query, over_rows, preferred_element_type=f32)
            value_part = lax.dot_general(
                prob.astype(bf16), grad, over_rows, preferred_element_type=f32
            )
            key_grads[at] = key_part if key_grads[at] is None else key_grads[at] + key_part
            value_grads[at] = value_part if value_grads[at] is None else value_grads[at] + value_part
        query_grad = jnp.concatenate(query_grads, axis=1) * scale
        query_grad = query_grad * wide_table(cos_ref[...], n_query) - half_swap(
            query_grad
        ) * wide_table(sin_ref[...], n_query)
        query_grad_ref[...] = query_grad.astype(bf16)
        key_grad = jnp.concatenate(key_grads, axis=1) * scale
        value_grad = jnp.concatenate(value_grads, axis=1)
        back_ref[:, :n_key] = key_grad[:rows].astype(bf16)
        back_ref[:, n_key:] = value_grad[:rows].astype(bf16)
        own_grad_ref[:, :n_key] = key_grad[rows:]
        own_grad_ref[:, n_key:] = value_grad[rows:]


def mix_back(pos, queries, tail, own, mixed, logs, tables, mid_grad, wide, n_key):
    rows, n_query = queries.shape
    width, columns = wide.shape
    tile = 512
    heads = n_query // HEAD_DIM
    whole = lambda *shape: pl.BlockSpec(shape, lambda i: (0,) * len(shape))
    return pl.pallas_call(
        functools.partial(mix_back_kernel, n_key),
        grid=(width // tile,),
        in_specs=[
            whole(rows, 1),
            whole(rows, n_query),
            whole(rows, 2 * n_key),
            whole(rows, 2 * n_key),
            whole(rows, n_query),
            whole(rows, heads),
            whole(rows, 2 * HEAD_DIM),
            whole(rows, 2 * HEAD_DIM),
            pl.BlockSpec((rows, tile), lambda i: (0, i)),
            pl.BlockSpec((tile, columns), lambda i: (i, 0)),
        ],
        out_specs=[
            whole(rows, n_query),
            whole(rows, 2 * n_key),
            whole(rows, 2 * n_key),
            pl.BlockSpec((rows, tile), lambda i: (0, i)),
        ],
        out_shape=[
            jax.ShapeDtypeStruct((rows, n_query), bf16),
            jax.ShapeDtypeStruct((rows, 2 * n_key), bf16),
            jax.ShapeDtypeStruct((rows, 2 * n_key), f32),
            jax.ShapeDtypeStruct((rows, width), bf16),
        ],
        scratch_shapes=[pltpu.VMEM((2 * rows, 2 * n_key), bf16), pltpu.VMEM((rows, n_query), f32)],
        compiler_params=params(),
        cost_estimate=cost(
            2 * rows * n_query * (width + 10 * rows), 2 * width * (columns + 3 * rows), 2 * rows * rows * heads
        ),
        name="mix_back",
    )(pos, queries, tail, own, mixed, logs, *tables, mid_grad, wide)


def head_grads_kernel(n_key, query_grad_ref, own_grad_ref, back_ref, cos_ref, sin_ref, wide_ref,
                      grads_ref, partial_ref, grads):
    n_query = query_grad_ref.shape[1]

    @pl.when(pl.program_id(0) == 0)
    def _():
        own = own_grad_ref[...] + back_ref[...].astype(f32)
        keys = own[:, :n_key]
        keys = keys * wide_table(cos_ref[...], n_key) - half_swap(keys) * wide_table(
            sin_ref[...], n_key
        )
        grads[:, :n_query] = query_grad_ref[...]
        grads[:, n_query : n_query + n_key] = keys.astype(bf16)
        grads[:, n_query + n_key :] = own[:, n_key:].astype(bf16)
        grads_ref[...] = grads[...]

    partial_ref[...] = lax.dot_general(
        grads[...], wide_ref[...], (((1,), (1,)), ((), ())), preferred_element_type=f32
    ).astype(bf16)


def head_grads(query_grad, own_grad, back, tables, wide, n_key):
    rows, n_query = query_grad.shape
    width = wide.shape[0]
    columns = n_query + 2 * n_key
    tile = 512
    whole = lambda *shape: pl.BlockSpec(shape, lambda i: (0,) * len(shape))
    return pl.pallas_call(
        functools.partial(head_grads_kernel, n_key),
        grid=(width // tile,),
        in_specs=[
            whole(rows, n_query),
            whole(rows, 2 * n_key),
            whole(rows, 2 * n_key),
            whole(rows, 2 * HEAD_DIM),
            whole(rows, 2 * HEAD_DIM),
            pl.BlockSpec((tile, columns), lambda i: (i, 0)),
        ],
        out_specs=[whole(rows, columns), pl.BlockSpec((rows, tile), lambda i: (0, i))],
        out_shape=[
            jax.ShapeDtypeStruct((rows, columns), bf16),
            jax.ShapeDtypeStruct((rows, width), bf16),
        ],
        scratch_shapes=[pltpu.VMEM((rows, columns), bf16)],
        compiler_params=params(),
        cost_estimate=cost(2 * rows * width * columns, 2 * width * (columns + rows)),
        name="head_grads",
    )(query_grad, own_grad, back, *tables, wide)


def attention_forward(stream, gain, wide, place, *others):
    pos, tables, sizes = place
    normed, inv_rms, queries, own = head_inputs(stream, gain, wide, tables, sizes)
    tail = from_behind(own, "ctx", 1)
    mixed, logs, partial = mix(pos, queries, tail, own, wide, sizes[1])
    total, *others = sum_tensor(partial, *others)
    stream = stream.astype(f32)
    saved = (stream, inv_rms[:, 0], normed, queries, tail, own, mixed, logs)
    return stream + total, saved, *others


def ffn_forward_in(middle, gain, wide, hidden_width):
    normed, inv_rms = norm_forward(middle, gain)
    both = jnp.concatenate([normed, swap_cores(normed)], axis=0)
    gate_up = product(both, wide)
    gate = gate_up[:, :hidden_width]
    up = gate_up[:, hidden_width:]
    hidden = (jax.nn.silu(gate) * up).astype(bf16)
    return (middle, inv_rms, both, gate, up, hidden)


def ffn_forward_out(state, down, *others):
    middle, hidden = state[0], state[-1]
    partial = own_share(cols_product(hidden, down), middle.shape[0])
    total, *others = sum_tensor(partial, *others)
    return (middle + total).astype(bf16), *others


def ffn_backward(upstream, upstream_both, state, gain, wide, down, *others):
    middle, inv_rms, both, gate, up, hidden = state
    hidden_grad = product(upstream_both, down)
    sigmoid_gate = jax.nn.sigmoid(gate)
    gate_grad = (hidden_grad * up * sigmoid_gate * (1.0 + gate * (1.0 - sigmoid_gate))).astype(bf16)
    up_grad = (hidden_grad * gate * sigmoid_gate).astype(bf16)
    grads = jnp.concatenate([gate_grad, up_grad], axis=1)
    partial = own_share(cols_product(grads, wide), middle.shape[0])
    normed_grad, *others = sum_tensor(partial, *others)
    down_share = lax.psum_scatter(
        token_terms(upstream_both, hidden), "ctx", scatter_dimension=0, tiled=True
    )
    normed_grad, terms = pin(normed_grad, token_terms(both, grads))
    wide_share = lax.psum_scatter(terms, "ctx", scatter_dimension=0, tiled=True)
    mid_part, gain_term = norm_backward(middle, inv_rms, gain, normed_grad)
    return upstream + mid_part, gain_term, wide_share, down_share, *others


def attention_backward(mid_grad, saved, wide, place, *others):
    pos, tables, sizes = place
    _, _, normed, queries, tail, own, mixed, logs = saved
    query_grad, back, own_grad, mid_grad_b = mix_back(
        pos, queries, tail, own, mixed, logs, tables, mid_grad, wide, sizes[1]
    )
    back = from_behind(back, "ctx", -1)
    grads, partial = head_grads(query_grad, own_grad, back, tables, wide, sizes[1])
    normed_grad, *others = sum_tensor(partial, *others)
    terms = attention_terms(normed, mid_grad_b, grads, mixed, lax.axis_size("ctx"))
    core = lax.axis_index("pipe")
    mine = lax.dynamic_index_in_dim(terms, core, 0, keepdims=False)
    theirs = lax.dynamic_index_in_dim(terms, 1 - core, 0, keepdims=False)
    return normed_grad, add_bf16(mine, swap_cores(theirs)), *others


def attention_backward_out(mid_grad, normed_grad, saved, gain):
    part, gain_term = norm_backward(saved[0], saved[1], gain, normed_grad)
    return (mid_grad + part).astype(bf16), gain_term


def on_device(
    inputs,
    out_grad,
    positions,
    attn_gain,
    w_query,
    w_key,
    w_value,
    w_out,
    ffn_gain,
    w_gate,
    w_up,
    w_down,
):
    core = lax.axis_index("pipe")
    first = core == 0
    shard = lax.axis_index("ctx")
    rows = inputs.shape[1]
    width = inputs.shape[2]
    n_query = w_query.shape[2]
    n_key = w_key.shape[2]
    half = w_gate.shape[2] // 2

    def pick(pair, index):
        return lax.dynamic_index_in_dim(pair, index, 0, keepdims=False)

    def mine_theirs(array, axis):
        size = array.shape[axis] // 2
        mine = lax.dynamic_slice_in_dim(array, core * size, size, axis)
        theirs = lax.dynamic_slice_in_dim(array, (1 - core) * size, size, axis)
        return mine, theirs

    count = lax.axis_size("ctx")
    gain_row = jnp.concatenate([attn_gain, ffn_gain], axis=1)
    attn_shard = jnp.concatenate([w_query[0], w_key[0], w_value[0], w_out[0].T], axis=1)
    wide_columns = attn_shard.shape[1]
    gain_rows = jnp.pad(gain_row, ((0, 15), (0, wide_columns - gain_row.shape[1])))
    rows_mine, rows_theirs = mine_theirs(attn_shard, 0)
    attn_keep = jnp.concatenate([rows_mine, gain_rows], axis=0)
    attn_got = swap_cores(jnp.concatenate([rows_theirs, gain_rows], axis=0))

    def attn_weights(pieces):
        got = swap_cores(pieces)
        both = jnp.stack([jnp.where(first, pieces, got), jnp.where(first, got, pieces)], axis=1)
        part_rows = attn_shard.shape[0] // 2
        wide = both[:, :, :part_rows].reshape(width, wide_columns)
        row = pieces[:, part_rows, : gain_row.shape[1]].astype(f32)
        return wide, row.reshape(count, 2, -1).transpose(1, 0, 2).reshape(2, width)

    gate_mine, gate_theirs = mine_theirs(w_gate[0], 1)
    up_mine, up_theirs = mine_theirs(w_up[0], 1)
    wide_keep = jnp.concatenate([gate_mine, up_mine], axis=1)
    wide_got = swap_cores(jnp.concatenate([gate_theirs, up_theirs], axis=1))
    down_mine, down_theirs = mine_theirs(w_down[0], 0)
    down_keep, down_got = down_mine.T, swap_cores(down_theirs.T)

    def for_sections(keep, got):
        return [jnp.where(first, keep, got), jnp.where(first, got, keep)]

    def gather(shard_part):
        return lax.all_gather(shard_part, "ctx", axis=0, tiled=True)

    attn_parts = for_sections(attn_keep, attn_got)
    wide_parts = for_sections(wide_keep, wide_got)
    down_parts = for_sections(down_keep, down_got)
    wide_low = lax.all_gather(wide_parts[0], ("pipe", "ctx"), axis=0, tiled=True)
    attn_pieces, attn_parts[1], wide_parts[1], *down_parts = pin(
        ring_gather(attn_parts[0]), attn_parts[1], wide_parts[1], *down_parts
    )
    attn_low, gains_low = attn_weights(attn_pieces)
    down_low = gather(down_parts[0])
    wide_high = gather(wide_parts[1])
    down_high = gather(down_parts[1])

    pos_row = pick(positions, core)
    place = (pos_row[:, None], rope_tables(pos_row, HEAD_DIM), (n_query, n_key))

    stream = pick(inputs, core)
    middle, attn_saved_low, wide_low, attn_part_high = attention_forward(
        stream, gains_low[0], attn_low, place, wide_low, attn_parts[1]
    )
    wide_low = pick(wide_low.reshape(2, width, -1), core)
    state_low = ffn_forward_in(middle, gains_low[1], wide_low, half)
    out_low, attn_pieces = ffn_forward_out(state_low, down_low, ring_gather(attn_part_high))
    attn_high, gains_high = attn_weights(attn_pieces)
    middle, attn_saved_high, wide_high = attention_forward(
        out_low, gains_high[0], attn_high, place, wide_high
    )
    state_high = ffn_forward_in(middle, gains_high[1], wide_high, half)

    own_grad = pick(out_grad, core)
    both_grad = jnp.concatenate([own_grad, pick(out_grad, 1 - core)], axis=0)
    mid_grad, ffn_gain_high, wide_share_high, down_share_high = ffn_backward(
        own_grad.astype(f32), both_grad, state_high, gains_high[1], wide_high, down_high
    )
    normed_grad, summed, down_share_high = attention_backward(
        mid_grad, attn_saved_high, attn_high, place, down_share_high
    )
    normed_grad, summed = pin(normed_grad, summed)
    attn_share_high = ring_scatter(summed).astype(bf16)
    boundary_high, attn_gain_high = attention_backward_out(
        mid_grad, normed_grad, attn_saved_high, gains_high[0]
    )
    both_grad = jnp.concatenate([boundary_high, swap_cores(boundary_high)], axis=0)
    mid_grad, ffn_gain_low, wide_share_low, down_share_low, wide_share_high = ffn_backward(
        boundary_high.astype(f32),
        both_grad,
        state_low,
        gains_low[1],
        wide_low,
        down_low,
        wide_share_high,
    )
    normed_grad, summed, down_share_low, attn_share_high = attention_backward(
        mid_grad, attn_saved_low, attn_low, place, down_share_low, attn_share_high
    )
    (out_high,) = ffn_forward_out(state_high, down_high)

    def from_other(low, high):
        return swap_cores(jnp.where(first, high, low))

    def to_owner(low, high):
        keep_part = jnp.where(first, low, high)
        got_part = from_other(low, high)
        return jnp.where(first, keep_part, got_part), jnp.where(first, got_part, keep_part)

    down_pair = (down_share_low, down_share_high)
    down_out = down_outputs(core, *down_pair, from_other(*down_pair))
    attn_share_low = ring_scatter(summed).astype(bf16)
    attn_full = jnp.concatenate(to_owner(attn_share_low, attn_share_high), axis=0).astype(f32)
    normed_grad, down_out, attn_full = pin(normed_grad, down_out, attn_full)

    boundary_low, attn_gain_low = attention_backward_out(
        mid_grad, normed_grad, attn_saved_low, gains_low[0]
    )
    outs = (out_low, out_high)
    section_outputs = section_stack(core, *outs, from_other(*outs))
    boundary = (boundary_low, boundary_high)
    boundary_grads = section_stack(core, *boundary, from_other(*boundary))
    wide_pair = (wide_share_low, wide_share_high)
    gate_out, up_out = wide_outputs(core, *wide_pair, from_other(*wide_pair))
    gains_out = share_gains(
        jnp.stack(
            [jnp.stack([attn_gain_low, ffn_gain_low]), jnp.stack([attn_gain_high, ffn_gain_high])]
        )
    )
    key_at = n_query + n_key
    value_at = key_at + n_key
    return (
        section_outputs[None],
        boundary_grads[None],
        gains_out[:1],
        attn_full[:, :n_query][None],
        attn_full[:, n_query:key_at][None],
        attn_full[:, key_at:value_at][None],
        attn_full[:, value_at:].T[None],
        gains_out[1:],
        gate_out[None],
        up_out[None],
        down_out[None],
    )


def solution(mesh):
    in_specs = (
        P(None, "ctx", None),
        P(None, "ctx", None),
        P(None, "ctx"),
        P("pipe", "ctx"),
        P("pipe", "ctx", "tensor"),
        P("pipe", "ctx", "tensor"),
        P("pipe", "ctx", "tensor"),
        P("pipe", "tensor", "ctx"),
        P("pipe", "ctx"),
        P("pipe", "ctx", "tensor"),
        P("pipe", "ctx", "tensor"),
        P("pipe", "tensor", "ctx"),
    )
    out_specs = (
        P("pipe", None, "ctx", None),
        P("pipe", None, "ctx", None),
        P("pipe", "ctx"),
        P("pipe", "ctx", "tensor"),
        P("pipe", "ctx", "tensor"),
        P("pipe", "ctx", "tensor"),
        P("pipe", "tensor", "ctx"),
        P("pipe", "ctx"),
        P("pipe", "ctx", "tensor"),
        P("pipe", "ctx", "tensor"),
        P("pipe", "tensor", "ctx"),
    )
    return jax.shard_map(
        on_device, mesh=mesh, in_specs=in_specs, out_specs=out_specs, check_vma=False
    )
```

```python
import functools
import math

import jax
import jax.numpy as jnp
from jax import lax
from jax.experimental import pallas as pl
from jax.experimental.pallas import tpu as pltpu
from jax.sharding import PartitionSpec as P

HEADS = 32
KV_HEADS = 8
HEAD_DIM = 64
MAXLEN = 256

epsilon = 1e-05
rope_base = 500000.0
bf16 = jnp.bfloat16
f32 = jnp.float32


def swap_cores(block):
    return lax.ppermute(block, "pipe", [(0, 1), (1, 0)])


def from_behind(block, axis, distance):
    devices = range(lax.axis_size(axis))
    route = [(i - distance, i) for i in devices if i - distance in devices]
    return lax.ppermute(block, axis, route)


def ring_order(count):
    across = 1 << (count.bit_length() - 1) // 2
    down = count // across
    walk = [(0, x) for x in range(across)]
    for y in range(1, down):
        columns = range(1, across)
        walk += [(y, x) for x in (columns if y % 2 == 0 else reversed(columns))]
    walk += [(y, 0) for y in range(down - 1, 0, -1)]
    return [y * across + x for y, x in walk]


def ring_tools():
    count = lax.axis_size("ctx")
    order = ring_order(count)
    place = [order.index(device) for device in range(count)]
    ahead = [(order[i], order[(i + 1) % count]) for i in range(count)]
    behind = [(b, a) for a, b in ahead]
    at = jnp.asarray(place, jnp.int32)[lax.axis_index("ctx")]
    table = jnp.asarray(order * 2, jnp.int32)

    def device_at(distance):
        return table[at + distance % count]

    return count, ahead, behind, device_at


def ring_gather_start(block):
    count, ahead, behind, _ = ring_tools()
    from_back, from_front = [block], [block]
    for _ in range(1, count // 2):
        from_back.append(lax.ppermute(from_back[-1], "ctx", ahead))
        from_front.append(lax.ppermute(from_front[-1], "ctx", behind))
    return from_back, from_front


def ring_gather(from_back, from_front):
    count, ahead, behind, device_at = ring_tools()
    block = from_back[0]
    half = block.shape[1] // 2
    left = lax.ppermute(from_back[-1][:, :half], "ctx", ahead)
    right = lax.ppermute(from_front[-1][:, half:], "ctx", behind)
    out = jnp.zeros((count,) + block.shape, block.dtype)

    def put(out, piece, distance, column=0):
        return lax.dynamic_update_slice(out, piece[None], (device_at(distance), 0, column))

    out = put(out, block, 0)
    for distance in range(1, count // 2):
        out = put(out, from_back[distance], -distance)
        out = put(out, from_front[distance], distance)
    out = put(out, left, count // 2)
    return put(out, right, count // 2, half)


def ring_term(terms, distance):
    return lax.dynamic_index_in_dim(terms, ring_tools()[3](distance), 0, keepdims=False)


def ring_scatter_start(terms):
    count, ahead, behind, _ = ring_tools()
    half = terms.shape[2] // 2
    far = ring_term(terms, count // 2)
    to_front = lax.ppermute(far[:, :half], "ctx", ahead)
    to_back = lax.ppermute(far[:, half:], "ctx", behind)
    for distance in range(count // 2 - 1, 0, -1):
        front, back = ring_term(terms, distance), ring_term(terms, -distance)
        if distance == count // 2 - 1:
            front = jnp.concatenate([add_bf16(front[:, :half], to_front), front[:, half:]], axis=1)
            back = jnp.concatenate([back[:, :half], add_bf16(back[:, half:], to_back)], axis=1)
        else:
            front, back = add_bf16(front, to_front), add_bf16(back, to_back)
        if distance > 1:
            front = lax.ppermute(front, "ctx", ahead)
            back = lax.ppermute(back, "ctx", behind)
        to_front, to_back = front, back
    return ring_term(terms, 0), to_front, to_back


def ring_scatter(own, to_front, to_back):
    _, ahead, behind, _ = ring_tools()
    from_back = lax.ppermute(to_front, "ctx", ahead)
    from_front = lax.ppermute(to_back, "ctx", behind)
    return (own.astype(f32) + from_back.astype(f32) + from_front.astype(f32)).astype(bf16)


def add_bf16(a, b):
    return (a.astype(f32) + b.astype(f32)).astype(bf16)


def params(megabytes=24):
    return pltpu.CompilerParams(vmem_limit_bytes=megabytes * 2**20)


def cost(flops, bytes_accessed, transcendentals=0):
    return pl.CostEstimate(
        flops=flops, bytes_accessed=bytes_accessed, transcendentals=transcendentals
    )


def token_terms_kernel(plan, *refs):
    out_ref = refs[-1]
    lefts, rights = refs[: -1 - len(plan)], refs[-1 - len(plan) : -1]
    rows = (((0,), (0,)), ((), ()))
    column = 0
    for left, right_ref in zip(plan, rights):
        own, got = lefts[2 * left], lefts[2 * left + 1]
        half, columns = own.shape[0], right_ref.shape[1]
        total = lax.dot_general(own[...], right_ref[:half], rows, preferred_element_type=f32)
        total += lax.dot_general(got[...], right_ref[half:], rows, preferred_element_type=f32)
        out_ref[:, column : column + columns] = total.astype(bf16)
        column += columns


def token_terms(lefts, rights):
    tokens, width = lefts[0][0].shape
    tile = 512
    columns = sum(right[2] for right in rights)
    side = pl.BlockSpec((tokens, tile), lambda i: (0, i))

    def right_spec(right):
        return pl.BlockSpec((2 * tokens, right[2]), lambda i: (0, right[3]))

    return pl.pallas_call(
        functools.partial(token_terms_kernel, [right[0] for right in rights]),
        grid=(width // tile,),
        in_specs=[side] * (2 * len(lefts)) + [right_spec(right) for right in rights],
        out_specs=pl.BlockSpec((tile, columns), lambda i: (i, 0)),
        out_shape=jax.ShapeDtypeStruct((width, columns), bf16),
        compiler_params=params(),
        cost_estimate=cost(
            4 * tokens * width * columns,
            2 * (width * columns + 2 * tokens * width * len(lefts) + 2 * tokens * columns),
        ),
        name="token_terms",
    )(*(array for pair in lefts for array in pair), *(right[1] for right in rights))


def attention_terms_kernel(normed_ref, mid_grad_ref, grads_ref, mixed_ref, out_ref):
    n_grads = grads_ref.shape[1]
    half = out_ref.shape[1]
    rows = (((0,), (0,)), ((), ()))
    inner = lax.dot_general(normed_ref[...], grads_ref[...], rows, preferred_element_type=f32)
    outer = lax.dot_general(mid_grad_ref[...], mixed_ref[...], rows, preferred_element_type=f32)
    for part in range(2):
        part_rows = slice(part * half, (part + 1) * half)
        out_ref[part, :, :n_grads] = inner[part_rows].astype(bf16)
        out_ref[part, :, n_grads:] = outer[part_rows].astype(bf16)


def attention_terms(normed, mid_grad, grads, mixed, count):
    tokens, width = normed.shape
    columns = grads.shape[1] + mixed.shape[1]
    tile = width // count
    return pl.pallas_call(
        attention_terms_kernel,
        grid=(count,),
        in_specs=[
            pl.BlockSpec((tokens, tile), lambda i: (0, i)),
            pl.BlockSpec((tokens, tile), lambda i: (0, i)),
            pl.BlockSpec((tokens, grads.shape[1]), lambda i: (0, 0)),
            pl.BlockSpec((tokens, mixed.shape[1]), lambda i: (0, 0)),
        ],
        out_specs=pl.BlockSpec((2, None, tile // 2, columns), lambda i: (0, i, 0, 0)),
        out_shape=jax.ShapeDtypeStruct((2, count, tile // 2, columns), bf16),
        compiler_params=params(),
        cost_estimate=pl.CostEstimate(
            flops=2 * tokens * width * columns,
            bytes_accessed=2 * (width * columns + 2 * tokens * width + tokens * columns),
            transcendentals=0,
        ),
        name="attention_terms",
    )(normed, mid_grad, grads, mixed)


def section_stack_kernel(core_ref, low_ref, high_ref, got_low_ref, got_high_ref, out_ref):
    first = core_ref[0] == 0
    keep = jnp.where(first, low_ref[...], high_ref[...])
    got = jnp.where(first, got_low_ref[...], got_high_ref[...])
    out_ref[...] = jnp.where(core_ref[0] == pl.program_id(0), keep, got)


def section_stack(core, low, high, got_low, got_high):
    rows, width = low.shape
    block = pl.BlockSpec((rows, width), lambda i, core: (0, 0))
    return pl.pallas_call(
        section_stack_kernel,
        grid_spec=pltpu.PrefetchScalarGridSpec(
            num_scalar_prefetch=1,
            grid=(2,),
            in_specs=[block] * 4,
            out_specs=pl.BlockSpec((None, rows, width), lambda i, core: (i, 0, 0)),
        ),
        out_shape=jax.ShapeDtypeStruct((2, rows, width), low.dtype),
        compiler_params=params(),
        cost_estimate=cost(0, 6 * rows * width * 2),
        name="section_stack",
    )(core.reshape(1), low, high, got_low, got_high)


def wide_outputs_kernel(core_ref, *refs):
    first = core_ref[0] == 0
    gate_ref, up_ref = refs[8:]
    parts = []
    for shares in (refs[:4], refs[4:8]):
        keep = jnp.where(first, shares[0][...], shares[1][...])
        got = jnp.where(first, shares[2][...], shares[3][...])
        parts.append([jnp.where(first == (side == 0), keep, got).astype(f32) for side in range(2)])
    quarter = parts[0][0].shape[1]
    units = parts[1][0].shape[1] - quarter
    for side in range(2):
        at = side * units
        gate_ref[:, at : at + quarter] = parts[0][side]
        gate_ref[:, at + quarter : at + units] = parts[1][side][:, :quarter]
        up_ref[:, at : at + units] = parts[1][side][:, quarter:]


def wide_outputs(core, early, late):
    rows, columns = early[0].shape
    quarter = columns // 3
    units = 2 * quarter
    tile = 128
    return pl.pallas_call(
        wide_outputs_kernel,
        grid_spec=pltpu.PrefetchScalarGridSpec(
            num_scalar_prefetch=1,
            grid=(rows // tile,),
            in_specs=[pl.BlockSpec((tile, quarter), lambda i, core: (i, 2))] * 4
            + [pl.BlockSpec((tile, columns), lambda i, core: (i, 0))] * 4,
            out_specs=[pl.BlockSpec((tile, 2 * units), lambda i, core: (i, 0))] * 2,
        ),
        out_shape=[jax.ShapeDtypeStruct((rows, 2 * units), f32)] * 2,
        compiler_params=params(),
        cost_estimate=cost(0, rows * (32 * quarter + 4 * 4 * units)),
        name="wide_outputs",
    )(core.reshape(1), *early, *late)


def down_outputs_kernel(core_ref, low_ref, high_ref, got_low_ref, got_high_ref, down_ref):
    first = core_ref[0] == 0
    units = low_ref.shape[1]
    keep = jnp.where(first, low_ref[...], high_ref[...])
    got = jnp.where(first, got_low_ref[...], got_high_ref[...])
    for side in range(2):
        part = jnp.where(first == (side == 0), keep, got).astype(f32)
        down_ref[side * units : (side + 1) * units, :] = part.T


def down_outputs(core, early):
    rows, columns = early[0].shape
    units = 2 * columns // 3
    tile = 128
    return pl.pallas_call(
        down_outputs_kernel,
        grid_spec=pltpu.PrefetchScalarGridSpec(
            num_scalar_prefetch=1,
            grid=(rows // tile,),
            in_specs=[pl.BlockSpec((tile, units), lambda i, core: (i, 0))] * 4,
            out_specs=pl.BlockSpec((2 * units, tile), lambda i, core: (0, i)),
        ),
        out_shape=jax.ShapeDtypeStruct((2 * units, rows), f32),
        compiler_params=params(),
        cost_estimate=cost(0, rows * units * 16),
        name="down_outputs",
    )(core.reshape(1), *early)


def pin(value, *others):
    return lax.optimization_barrier((value, *others))


def share_gains(terms):
    core, shard = lax.axis_index("pipe"), lax.axis_index("ctx")
    count = lax.axis_size("ctx")
    own = lax.dynamic_index_in_dim(terms, core, 0, keepdims=False)
    other = lax.dynamic_index_in_dim(terms, 1 - core, 0, keepdims=False)
    total = own + swap_cores(other)
    blocks = total.reshape(2, count, -1)

    def block(index):
        return lax.dynamic_index_in_dim(blocks, index, 1, keepdims=False)

    result = block(shard)
    for step in range(1, count):
        route = [(i, i ^ step) for i in range(count)]
        result = result + lax.ppermute(block(shard ^ step), "ctx", route)
    return result


def product(left, right):
    return lax.dot_general(
        left, right, (((1,), (0,)), ((), ())), preferred_element_type=f32
    )


def rows_product(left, right):
    return lax.dot_general(
        left, right, (((0,), (0,)), ((), ())), preferred_element_type=f32
    )


def cols_product(left, right):
    return lax.dot_general(
        left, right, (((1,), (1,)), ((), ())), preferred_element_type=f32
    )


def norm_forward(stream, gain_vector):
    inv_rms = lax.rsqrt(jnp.mean(stream * stream, axis=-1) + epsilon)
    return ((stream * inv_rms[:, None] * gain_vector[None, :]).astype(bf16), inv_rms)


def norm_backward(stream, inv_rms, gain_vector, upstream):
    weighted = upstream * gain_vector[None, :]
    gain_grad = jnp.sum(upstream * stream * inv_rms[:, None], axis=0)
    inner_mean = jnp.mean(stream * weighted, axis=-1)
    stream_grad = (
        weighted * inv_rms[:, None] - stream * (inv_rms * inv_rms * inv_rms * inner_mean)[:, None]
    )
    return (stream_grad, gain_grad)


def sum_tensor(partial, *others):
    partial = partial.astype(bf16)
    if others:
        partial, *others = pin(partial, *others)
    return lax.psum(partial, "tensor"), *others


def own_share(partial, rows):
    arrived = swap_cores(partial[rows:].astype(bf16))
    return partial[:rows] + arrived.astype(f32)


def half_swap(values):
    lanes = lax.broadcasted_iota(jnp.int32, values.shape, 1)
    count = values.shape[1]
    quarter = HEAD_DIM // 2
    return jnp.where(
        lanes % HEAD_DIM < quarter,
        pltpu.roll(values, count - quarter, 1),
        pltpu.roll(values, quarter, 1),
    )


def wide_table(table, columns):
    return jnp.concatenate([table] * (columns // table.shape[1]), axis=1)


def rope_tables(positions_row, width):
    frequency = jnp.exp(
        jnp.arange(width // 2, dtype=f32) * (-2.0 * math.log(rope_base) / width)
    )
    angles = positions_row.astype(f32)[:, None] * frequency[None, :]
    cosine, sine = jnp.cos(angles), jnp.sin(angles)
    return (
        jnp.concatenate([cosine] * 4, axis=1),
        jnp.concatenate([-sine, sine] * 2, axis=1),
    )


def head_inputs_kernel(sizes, stream_ref, gain_ref, wide_ref, cos_ref, sin_ref,
                       normed_ref, rms_ref, query_ref, own_ref):
    n_query, n_key = sizes
    stream = stream_ref[...].astype(f32)
    inv_rms = lax.rsqrt(jnp.mean(stream * stream, axis=1, keepdims=True) + epsilon)
    normed = (stream * inv_rms * gain_ref[...]).astype(bf16)
    normed_ref[...] = normed
    rms_ref[...] = inv_rms
    raw = jnp.dot(normed, wide_ref[...], preferred_element_type=f32)
    turned = raw[:, : n_query + n_key]
    cosine = wide_table(cos_ref[...], n_query + n_key)
    sine = wide_table(sin_ref[...], n_query + n_key)
    turned = turned * cosine + half_swap(turned) * sine
    query_ref[...] = turned[:, :n_query].astype(bf16)
    own_ref[:, :n_key] = turned[:, n_query:].astype(bf16)
    own_ref[:, n_key:] = raw[:, n_query + n_key :].astype(bf16)


def head_inputs(stream, gain, wide, tables, sizes):
    n_query, n_key = sizes
    rows, width = stream.shape
    columns = n_query + 2 * n_key
    whole = lambda *shape: pl.BlockSpec(shape, lambda i: (0,) * len(shape))
    return pl.pallas_call(
        functools.partial(head_inputs_kernel, sizes),
        grid=(1,),
        in_specs=[
            whole(rows, width),
            whole(1, width),
            whole(width, columns),
            whole(rows, 2 * HEAD_DIM),
            whole(rows, 2 * HEAD_DIM),
        ],
        out_specs=[whole(rows, width), whole(rows, 1), whole(rows, n_query), whole(rows, 2 * n_key)],
        out_shape=[
            jax.ShapeDtypeStruct((rows, width), bf16),
            jax.ShapeDtypeStruct((rows, 1), f32),
            jax.ShapeDtypeStruct((rows, n_query), bf16),
            jax.ShapeDtypeStruct((rows, 2 * n_key), bf16),
        ],
        compiler_params=params(),
        cost_estimate=cost(2 * rows * width * columns, 2 * width * (columns + 4 * rows)),
        name="head_inputs",
    )(stream, gain[None], wide, *tables)


def masked_scores(query, keys, allowed):
    raw = lax.dot_general(query, keys, (((1,), (1,)), ((), ())), preferred_element_type=f32)
    return jnp.where(allowed, raw * HEAD_DIM ** (-0.5), -1e30)


def allowed_pairs(pos, rows):
    distance = (
        lax.broadcasted_iota(jnp.int32, (rows, 2 * rows), 0)
        - lax.broadcasted_iota(jnp.int32, (rows, 2 * rows), 1)
        + rows
    )
    return (distance >= 0) & (distance <= pos)


def head_slice(index):
    return slice(index * HEAD_DIM, (index + 1) * HEAD_DIM)


def mix_kernel(n_key, pos_ref, query_ref, tail_ref, own_ref, wide_ref,
               mixed_ref, log_ref, partial_ref, window, mixed_all):
    rows, n_query = query_ref.shape

    @pl.when(pl.program_id(0) == 0)
    def _():
        window[:rows] = tail_ref[...]
        window[rows:] = own_ref[...]
        allowed = allowed_pairs(pos_ref[...], rows)
        group = HEADS // KV_HEADS
        logs, mixed = [], []
        for head in range(n_query // HEAD_DIM):
            keys = window[:, head_slice(head // group)]
            values = window[:, head_slice((n_key // HEAD_DIM) + head // group)]
            masked = masked_scores(query_ref[:, head_slice(head)], keys, allowed)
            top = jnp.max(masked, axis=1, keepdims=True)
            exponent = jnp.exp(masked - top)
            total = jnp.sum(exponent, axis=1, keepdims=True)
            weights = (exponent * (1.0 / total)).astype(bf16)
            mixed.append(jnp.dot(weights, values, preferred_element_type=f32).astype(bf16))
            logs.append(top + jnp.log(total))
        everything = jnp.concatenate(mixed, axis=1)
        mixed_all[...] = everything
        mixed_ref[...] = everything
        log_ref[...] = jnp.concatenate(logs, axis=1)

    partial_ref[...] = lax.dot_general(
        mixed_all[...],
        wide_ref[:, wide_ref.shape[1] - n_query :],
        (((1,), (1,)), ((), ())),
        preferred_element_type=f32,
    ).astype(bf16)


def mix(pos, queries, tail, own, wide, n_key):
    rows, n_query = queries.shape
    width, columns = wide.shape
    tile = 512
    heads = n_query // HEAD_DIM
    whole = lambda *shape: pl.BlockSpec(shape, lambda i: (0,) * len(shape))
    return pl.pallas_call(
        functools.partial(mix_kernel, n_key),
        grid=(width // tile,),
        in_specs=[
            whole(rows, 1),
            whole(rows, n_query),
            whole(rows, 2 * n_key),
            whole(rows, 2 * n_key),
            pl.BlockSpec((tile, columns), lambda i: (i, 0)),
        ],
        out_specs=[
            whole(rows, n_query),
            whole(rows, heads),
            pl.BlockSpec((rows, tile), lambda i: (0, i)),
        ],
        out_shape=[
            jax.ShapeDtypeStruct((rows, n_query), bf16),
            jax.ShapeDtypeStruct((rows, heads), f32),
            jax.ShapeDtypeStruct((rows, width), bf16),
        ],
        scratch_shapes=[pltpu.VMEM((2 * rows, 2 * n_key), bf16), pltpu.VMEM((rows, n_query), bf16)],
        compiler_params=params(),
        cost_estimate=cost(
            2 * rows * n_query * (width + 4 * rows), 2 * width * (columns + rows), 2 * rows * rows * heads
        ),
        name="mix",
    )(pos, queries, tail, own, wide)


def mix_back_kernel(n_key, pos_ref, query_ref, tail_ref, own_ref, mixed_ref, log_ref, cos_ref, sin_ref,
                    mid_grad_ref, wide_ref, query_grad_ref, back_ref, own_grad_ref, mid_b_ref,
                    window, mixed_grad):
    rows, n_query = query_ref.shape
    step = pl.program_id(0)
    mid_b = mid_grad_ref[...].astype(bf16)
    mid_b_ref[...] = mid_b
    part = jnp.dot(mid_b, wide_ref[:, wide_ref.shape[1] - n_query :], preferred_element_type=f32)

    @pl.when(step == 0)
    def _():
        mixed_grad[...] = part

    @pl.when(step > 0)
    def _():
        mixed_grad[...] += part

    @pl.when(step == pl.num_programs(0) - 1)
    def _():
        window[:rows] = tail_ref[...]
        window[rows:] = own_ref[...]
        allowed = allowed_pairs(pos_ref[...], rows)
        group = HEADS // KV_HEADS
        groups = n_key // HEAD_DIM
        scale = HEAD_DIM ** (-0.5)
        grads = mixed_grad[...].astype(bf16)
        over_rows = (((0,), (0,)), ((), ()))
        over_columns = (((1,), (1,)), ((), ()))
        query_grads, key_grads, value_grads = [], [None] * groups, [None] * groups
        for head in range(n_query // HEAD_DIM):
            at = head // group
            keys = window[:, head_slice(at)]
            values = window[:, head_slice(groups + at)]
            query = query_ref[:, head_slice(head)]
            grad = grads[:, head_slice(head)]
            masked = masked_scores(query, keys, allowed)
            prob = jnp.exp(masked - log_ref[:, head : head + 1])
            prob_grad = lax.dot_general(grad, values, over_columns, preferred_element_type=f32)
            delta = jnp.sum(
                grad.astype(f32) * mixed_ref[:, head_slice(head)].astype(f32), axis=1, keepdims=True
            )
            score_grad = (prob * (prob_grad - delta)).astype(bf16)
            query_grads.append(jnp.dot(score_grad, keys, preferred_element_type=f32))
            key_part = lax.dot_general(score_grad, query, over_rows, preferred_element_type=f32)
            value_part = lax.dot_general(
                prob.astype(bf16), grad, over_rows, preferred_element_type=f32
            )
            key_grads[at] = key_part if key_grads[at] is None else key_grads[at] + key_part
            value_grads[at] = value_part if value_grads[at] is None else value_grads[at] + value_part
        query_grad = jnp.concatenate(query_grads, axis=1) * scale
        query_grad = query_grad * wide_table(cos_ref[...], n_query) - half_swap(
            query_grad
        ) * wide_table(sin_ref[...], n_query)
        query_grad_ref[...] = query_grad.astype(bf16)
        key_grad = jnp.concatenate(key_grads, axis=1) * scale
        value_grad = jnp.concatenate(value_grads, axis=1)
        back_ref[:, :n_key] = key_grad[:rows].astype(bf16)
        back_ref[:, n_key:] = value_grad[:rows].astype(bf16)
        own_grad_ref[:, :n_key] = key_grad[rows:]
        own_grad_ref[:, n_key:] = value_grad[rows:]


def mix_back(pos, queries, tail, own, mixed, logs, tables, mid_grad, wide, n_key):
    rows, n_query = queries.shape
    width, columns = wide.shape
    tile = 512
    heads = n_query // HEAD_DIM
    whole = lambda *shape: pl.BlockSpec(shape, lambda i: (0,) * len(shape))
    return pl.pallas_call(
        functools.partial(mix_back_kernel, n_key),
        grid=(width // tile,),
        in_specs=[
            whole(rows, 1),
            whole(rows, n_query),
            whole(rows, 2 * n_key),
            whole(rows, 2 * n_key),
            whole(rows, n_query),
            whole(rows, heads),
            whole(rows, 2 * HEAD_DIM),
            whole(rows, 2 * HEAD_DIM),
            pl.BlockSpec((rows, tile), lambda i: (0, i)),
            pl.BlockSpec((tile, columns), lambda i: (i, 0)),
        ],
        out_specs=[
            whole(rows, n_query),
            whole(rows, 2 * n_key),
            whole(rows, 2 * n_key),
            pl.BlockSpec((rows, tile), lambda i: (0, i)),
        ],
        out_shape=[
            jax.ShapeDtypeStruct((rows, n_query), bf16),
            jax.ShapeDtypeStruct((rows, 2 * n_key), bf16),
            jax.ShapeDtypeStruct((rows, 2 * n_key), f32),
            jax.ShapeDtypeStruct((rows, width), bf16),
        ],
        scratch_shapes=[pltpu.VMEM((2 * rows, 2 * n_key), bf16), pltpu.VMEM((rows, n_query), f32)],
        compiler_params=params(),
        cost_estimate=cost(
            2 * rows * n_query * (width + 10 * rows), 2 * width * (columns + 3 * rows), 2 * rows * rows * heads
        ),
        name="mix_back",
    )(pos, queries, tail, own, mixed, logs, *tables, mid_grad, wide)


def head_grads_kernel(n_key, query_grad_ref, own_grad_ref, back_ref, cos_ref, sin_ref, wide_ref,
                      grads_ref, partial_ref, grads):
    n_query = query_grad_ref.shape[1]

    @pl.when(pl.program_id(0) == 0)
    def _():
        own = own_grad_ref[...] + back_ref[...].astype(f32)
        keys = own[:, :n_key]
        keys = keys * wide_table(cos_ref[...], n_key) - half_swap(keys) * wide_table(
            sin_ref[...], n_key
        )
        grads[:, :n_query] = query_grad_ref[...]
        grads[:, n_query : n_query + n_key] = keys.astype(bf16)
        grads[:, n_query + n_key :] = own[:, n_key:].astype(bf16)
        grads_ref[...] = grads[...]

    partial_ref[...] = lax.dot_general(
        grads[...], wide_ref[...], (((1,), (1,)), ((), ())), preferred_element_type=f32
    ).astype(bf16)


def head_grads(query_grad, own_grad, back, tables, wide, n_key):
    rows, n_query = query_grad.shape
    width = wide.shape[0]
    columns = n_query + 2 * n_key
    tile = 512
    whole = lambda *shape: pl.BlockSpec(shape, lambda i: (0,) * len(shape))
    return pl.pallas_call(
        functools.partial(head_grads_kernel, n_key),
        grid=(width // tile,),
        in_specs=[
            whole(rows, n_query),
            whole(rows, 2 * n_key),
            whole(rows, 2 * n_key),
            whole(rows, 2 * HEAD_DIM),
            whole(rows, 2 * HEAD_DIM),
            pl.BlockSpec((tile, columns), lambda i: (i, 0)),
        ],
        out_specs=[whole(rows, columns), pl.BlockSpec((rows, tile), lambda i: (0, i))],
        out_shape=[
            jax.ShapeDtypeStruct((rows, columns), bf16),
            jax.ShapeDtypeStruct((rows, width), bf16),
        ],
        scratch_shapes=[pltpu.VMEM((rows, columns), bf16)],
        compiler_params=params(),
        cost_estimate=cost(2 * rows * width * columns, 2 * width * (columns + rows)),
        name="head_grads",
    )(query_grad, own_grad, back, *tables, wide)


def attention_forward(stream, gain, wide, place, *others):
    pos, tables, sizes = place
    normed, inv_rms, queries, own = head_inputs(stream, gain, wide, tables, sizes)
    tail = from_behind(own, "ctx", 1)
    mixed, logs, partial = mix(pos, queries, tail, own, wide, sizes[1])
    total, *others = sum_tensor(partial, *others)
    return total, (stream.astype(f32), inv_rms[:, 0], normed, queries, tail, own, mixed, logs), *others


def ffn_forward_in(middle, gain, wide, hidden_width):
    normed, inv_rms = norm_forward(middle, gain)
    got = swap_cores(normed)
    gate_up = product(jnp.concatenate([normed, got], axis=0), wide)
    gate = gate_up[:, :hidden_width]
    up = gate_up[:, hidden_width:]
    hidden = (jax.nn.silu(gate) * up).astype(bf16)
    return (middle, inv_rms, normed, got, gate, up, hidden)


def ffn_share(state, down):
    middle, hidden = state[0], state[-1]
    return own_share(cols_product(hidden, down), middle.shape[0]).astype(bf16)


def ffn_backward(own_grad, other_grad, state, wide, down, *others):
    middle, _, normed, got, gate, up, hidden = state
    hidden_grad = product(jnp.concatenate([own_grad, other_grad], axis=0), down)
    sigmoid_gate = jax.nn.sigmoid(gate)
    gate_grad = (hidden_grad * up * sigmoid_gate * (1.0 + gate * (1.0 - sigmoid_gate))).astype(bf16)
    up_grad = (hidden_grad * gate * sigmoid_gate).astype(bf16)
    units = gate.shape[1]
    partial = cols_product(jnp.concatenate([gate_grad, up_grad], axis=1), wide)
    normed_grad, *others = sum_tensor(own_share(partial, middle.shape[0]), *others)
    own_sides, norm_sides = (own_grad, other_grad), (normed, got)
    early = token_terms(
        [own_sides, norm_sides], [(0, hidden, units, 0), (1, gate_grad, units // 2, 0)]
    )
    early = lax.psum_scatter(early, "ctx", scatter_dimension=0, tiled=True)
    late = token_terms([norm_sides], [(0, gate_grad, units // 2, 1), (0, up_grad, units, 0)])
    return normed_grad, early, late, *others


def ffn_backward_out(upstream, normed_grad, state, gain):
    mid_part, gain_term = norm_backward(state[0], state[1], gain, normed_grad.astype(f32))
    return upstream.astype(f32) + mid_part, gain_term


def attention_backward(mid_grad, saved, wide, place, *others):
    pos, tables, sizes = place
    _, _, normed, queries, tail, own, mixed, logs = saved
    query_grad, back, own_grad, mid_grad_b = mix_back(
        pos, queries, tail, own, mixed, logs, tables, mid_grad, wide, sizes[1]
    )
    back = from_behind(back, "ctx", -1)
    grads, partial = head_grads(query_grad, own_grad, back, tables, wide, sizes[1])
    normed_grad, *others = sum_tensor(partial, *others)
    terms = attention_terms(normed, mid_grad_b, grads, mixed, lax.axis_size("ctx"))
    core = lax.axis_index("pipe")
    mine = lax.dynamic_index_in_dim(terms, core, 0, keepdims=False)
    theirs = lax.dynamic_index_in_dim(terms, 1 - core, 0, keepdims=False)
    return normed_grad, add_bf16(mine, swap_cores(theirs)), *others


def attention_backward_out(mid_grad, normed_grad, saved, gain):
    part, gain_term = norm_backward(saved[0], saved[1], gain, normed_grad.astype(f32))
    return (mid_grad + part).astype(bf16), gain_term


def on_device(
    inputs,
    out_grad,
    positions,
    attn_gain,
    w_query,
    w_key,
    w_value,
    w_out,
    ffn_gain,
    w_gate,
    w_up,
    w_down,
):
    core = lax.axis_index("pipe")
    first = core == 0
    shard = lax.axis_index("ctx")
    rows = inputs.shape[1]
    width = inputs.shape[2]
    n_query = w_query.shape[2]
    n_key = w_key.shape[2]
    half = w_gate.shape[2] // 2

    def pick(pair, index):
        return lax.dynamic_index_in_dim(pair, index, 0, keepdims=False)

    def mine_theirs(array, axis):
        size = array.shape[axis] // 2
        mine = lax.dynamic_slice_in_dim(array, core * size, size, axis)
        theirs = lax.dynamic_slice_in_dim(array, (1 - core) * size, size, axis)
        return mine, theirs

    count = lax.axis_size("ctx")
    gain_row = jnp.concatenate([attn_gain, ffn_gain], axis=1)
    attn_shard = jnp.concatenate([w_query[0], w_key[0], w_value[0], w_out[0].T], axis=1)
    wide_columns = attn_shard.shape[1]
    gain_rows = jnp.pad(gain_row, ((0, 15), (0, wide_columns - gain_row.shape[1])))
    rows_mine, rows_theirs = mine_theirs(attn_shard, 0)
    attn_keep = jnp.concatenate([rows_mine, gain_rows], axis=0)
    attn_got = swap_cores(jnp.concatenate([rows_theirs, gain_rows], axis=0))

    def attn_weights(pieces):
        got = swap_cores(pieces)
        both = jnp.stack([jnp.where(first, pieces, got), jnp.where(first, got, pieces)], axis=1)
        part_rows = attn_shard.shape[0] // 2
        wide = both[:, :, :part_rows].reshape(width, wide_columns)
        row = pieces[:, part_rows, : gain_row.shape[1]].astype(f32)
        return wide, row.reshape(count, 2, -1).transpose(1, 0, 2).reshape(2, width)

    gate_mine, gate_theirs = mine_theirs(w_gate[0], 1)
    up_mine, up_theirs = mine_theirs(w_up[0], 1)
    wide_keep = jnp.concatenate([gate_mine, up_mine], axis=1)
    wide_got = swap_cores(jnp.concatenate([gate_theirs, up_theirs], axis=1))
    down_mine, down_theirs = mine_theirs(w_down[0], 0)
    down_keep, down_got = down_mine.T, swap_cores(down_theirs.T)

    def for_sections(keep, got):
        return [jnp.where(first, keep, got), jnp.where(first, got, keep)]

    def gather(shard_part):
        return lax.all_gather(shard_part, "ctx", axis=0, tiled=True)

    attn_parts = for_sections(attn_keep, attn_got)
    wide_parts = for_sections(wide_keep, wide_got)
    down_parts = for_sections(down_keep, down_got)
    wide_low = lax.all_gather(wide_parts[0], ("pipe", "ctx"), axis=0, tiled=True)
    attn_pieces, attn_parts[1], wide_parts[1], *down_parts = pin(
        ring_gather(*ring_gather_start(attn_parts[0])), attn_parts[1], wide_parts[1], *down_parts
    )
    attn_low, gains_low = attn_weights(attn_pieces)
    down_low = gather(down_parts[0])
    wide_high = gather(wide_parts[1])
    down_high = gather(down_parts[1])

    pos_row = pick(positions, core)
    place = (pos_row[:, None], rope_tables(pos_row, HEAD_DIM), (n_query, n_key))

    def scatter(terms):
        return lax.psum_scatter(terms, "ctx", scatter_dimension=0, tiled=True)

    def give_low(share):
        return lax.ppermute(share, "pipe", [(1, 0)])

    def give_high(share):
        return lax.ppermute(share, "pipe", [(0, 1)])

    stream = pick(inputs, core)
    total, attn_saved_low, wide_low, attn_part_high = attention_forward(
        stream, gains_low[0], attn_low, place, wide_low, attn_parts[1]
    )
    wide_low = pick(wide_low.reshape(2, width, -1), core)
    total, wide_low, attn_ring = pin(total, wide_low, ring_gather_start(attn_part_high))
    middle = attn_saved_low[0] + total.astype(f32)
    state_low = ffn_forward_in(middle, gains_low[1], wide_low, half)
    own_grad, other_grad = pick(out_grad, core), pick(out_grad, 1 - core)
    (total,) = sum_tensor(ffn_share(state_low, down_low))
    total, own_grad, other_grad, (attn_high, gains_high) = pin(
        total, own_grad, other_grad, attn_weights(ring_gather(*attn_ring))
    )
    out_low = (middle + total.astype(f32)).astype(bf16)
    total, attn_saved_high, wide_high = attention_forward(
        out_low, gains_high[0], attn_high, place, wide_high
    )
    total, got_out_low = pin(total, swap_cores(out_low))
    middle = attn_saved_high[0] + total.astype(f32)
    state_high = ffn_forward_in(middle, gains_high[1], wide_high, half)

    normed_grad, early_high, late_high = ffn_backward(
        own_grad, other_grad, state_high, wide_high, down_high
    )
    normed_grad, late_high = pin(normed_grad, late_high)
    mid_grad, ffn_gain_high = ffn_backward_out(own_grad, normed_grad, state_high, gains_high[1])
    late_high = scatter(late_high)
    normed_grad, summed, early_high = attention_backward(
        mid_grad, attn_saved_high, attn_high, place, early_high
    )
    normed_grad, attn_ring, out_share = pin(
        normed_grad, ring_scatter_start(summed), ffn_share(state_high, down_high)
    )
    boundary_high, attn_gain_high = attention_backward_out(
        mid_grad, normed_grad, attn_saved_high, gains_high[0]
    )
    got_boundary_high = swap_cores(boundary_high)
    normed_grad, early_low, late_low, late_high = ffn_backward(
        boundary_high, got_boundary_high, state_low, wide_low, down_low, late_high
    )
    normed_grad, late_low, attn_share_high = pin(normed_grad, late_low, ring_scatter(*attn_ring))
    mid_grad, ffn_gain_low = ffn_backward_out(
        boundary_high, normed_grad, state_low, gains_low[1]
    )
    late_low = scatter(late_low)
    normed_grad, summed, early_low = attention_backward(
        mid_grad, attn_saved_low, attn_low, place, early_low
    )
    (total,) = sum_tensor(out_share)

    def to_owner(low, high):
        keep_part = jnp.where(first, low, high)
        got_part = swap_cores(jnp.where(first, high, low))
        return jnp.where(first, keep_part, got_part), jnp.where(first, got_part, keep_part)

    early = (early_low, early_high, give_low(early_low), give_high(early_high))
    down_out = down_outputs(core, early)
    attn_share_low = ring_scatter(*ring_scatter_start(summed))
    attn_full = jnp.concatenate(to_owner(attn_share_low, attn_share_high), axis=0).astype(f32)
    key_at = n_query + n_key
    value_at = key_at + n_key
    attn_outs = (
        attn_full[:, :n_query],
        attn_full[:, n_query:key_at],
        attn_full[:, key_at:value_at],
        attn_full[:, value_at:].T,
    )
    normed_grad, down_out, attn_outs, got_late_high = pin(
        normed_grad, down_out, attn_outs, give_high(late_high)
    )
    out_high = (middle + total.astype(f32)).astype(bf16)
    section_outputs = section_stack(core, out_low, out_high, got_out_low, swap_cores(out_high))

    boundary_low, attn_gain_low = attention_backward_out(
        mid_grad, normed_grad, attn_saved_low, gains_low[0]
    )
    boundary_grads = section_stack(
        core, boundary_low, boundary_high, swap_cores(boundary_low), got_boundary_high
    )
    late = (late_low, late_high, give_low(late_low), got_late_high)
    gate_out, up_out = wide_outputs(core, early, late)
    gains_out = share_gains(
        jnp.stack(
            [jnp.stack([attn_gain_low, ffn_gain_low]), jnp.stack([attn_gain_high, ffn_gain_high])]
        )
    )
    query_out, key_out, value_out, attn_out = attn_outs
    return (
        section_outputs[None],
        boundary_grads[None],
        gains_out[:1],
        query_out[None],
        key_out[None],
        value_out[None],
        attn_out[None],
        gains_out[1:],
        gate_out[None],
        up_out[None],
        down_out[None],
    )


def solution(mesh):
    in_specs = (
        P(None, "ctx", None),
        P(None, "ctx", None),
        P(None, "ctx"),
        P("pipe", "ctx"),
        P("pipe", "ctx", "tensor"),
        P("pipe", "ctx", "tensor"),
        P("pipe", "ctx", "tensor"),
        P("pipe", "tensor", "ctx"),
        P("pipe", "ctx"),
        P("pipe", "ctx", "tensor"),
        P("pipe", "ctx", "tensor"),
        P("pipe", "tensor", "ctx"),
    )
    out_specs = (
        P("pipe", None, "ctx", None),
        P("pipe", None, "ctx", None),
        P("pipe", "ctx"),
        P("pipe", "ctx", "tensor"),
        P("pipe", "ctx", "tensor"),
        P("pipe", "ctx", "tensor"),
        P("pipe", "tensor", "ctx"),
        P("pipe", "ctx"),
        P("pipe", "ctx", "tensor"),
        P("pipe", "ctx", "tensor"),
        P("pipe", "tensor", "ctx"),
    )
    return jax.shard_map(
        on_device, mesh=mesh, in_specs=in_specs, out_specs=out_specs, check_vma=False
    )
```

```python
import functools
import math

import jax
import jax.numpy as jnp
from jax import lax
from jax.experimental import pallas as pl
from jax.experimental.pallas import tpu as pltpu
from jax.sharding import PartitionSpec as P

HEADS = 32
KV_HEADS = 8
HEAD_DIM = 64
MAXLEN = 256

epsilon = 1e-05
rope_base = 500000.0
bf16 = jnp.bfloat16
f32 = jnp.float32


def swap_cores(block):
    return lax.ppermute(block, "pipe", [(0, 1), (1, 0)])


def from_behind(block, axis, distance):
    devices = range(lax.axis_size(axis))
    route = [(i - distance, i) for i in devices if i - distance in devices]
    return lax.ppermute(block, axis, route)


def ring_order(count):
    across = 1 << (count.bit_length() - 1) // 2
    down = count // across
    walk = [(0, x) for x in range(across)]
    for y in range(1, down):
        columns = range(1, across)
        walk += [(y, x) for x in (columns if y % 2 == 0 else reversed(columns))]
    walk += [(y, 0) for y in range(down - 1, 0, -1)]
    return [y * across + x for y, x in walk]


def ring_tools():
    count = lax.axis_size("ctx")
    order = ring_order(count)
    place = [order.index(device) for device in range(count)]
    ahead = [(order[i], order[(i + 1) % count]) for i in range(count)]
    behind = [(b, a) for a, b in ahead]
    at = jnp.asarray(place, jnp.int32)[lax.axis_index("ctx")]
    table = jnp.asarray(order * 2, jnp.int32)

    def device_at(distance):
        return table[at + distance % count]

    return count, ahead, behind, device_at


def ring_gather_start(block):
    count, ahead, behind, _ = ring_tools()
    from_back, from_front = [block], [block]
    for _ in range(1, count // 2):
        from_back.append(lax.ppermute(from_back[-1], "ctx", ahead))
        from_front.append(lax.ppermute(from_front[-1], "ctx", behind))
    return from_back, from_front


def ring_gather(from_back, from_front):
    count, ahead, behind, device_at = ring_tools()
    block = from_back[0]
    half = block.shape[1] // 2
    left = lax.ppermute(from_back[-1][:, :half], "ctx", ahead)
    right = lax.ppermute(from_front[-1][:, half:], "ctx", behind)
    out = jnp.zeros((count,) + block.shape, block.dtype)

    def put(out, piece, distance, column=0):
        return lax.dynamic_update_slice(out, piece[None], (device_at(distance), 0, column))

    out = put(out, block, 0)
    for distance in range(1, count // 2):
        out = put(out, from_back[distance], -distance)
        out = put(out, from_front[distance], distance)
    out = put(out, left, count // 2)
    return put(out, right, count // 2, half)


def ring_term(terms, distance):
    return lax.dynamic_index_in_dim(terms, ring_tools()[3](distance), 0, keepdims=False)


def ring_scatter_start(terms):
    count, ahead, behind, _ = ring_tools()
    half = terms.shape[2] // 2
    far = ring_term(terms, count // 2)
    to_front = lax.ppermute(far[:, :half], "ctx", ahead)
    to_back = lax.ppermute(far[:, half:], "ctx", behind)
    for distance in range(count // 2 - 1, 0, -1):
        front, back = ring_term(terms, distance), ring_term(terms, -distance)
        if distance == count // 2 - 1:
            front = jnp.concatenate([add_bf16(front[:, :half], to_front), front[:, half:]], axis=1)
            back = jnp.concatenate([back[:, :half], add_bf16(back[:, half:], to_back)], axis=1)
        else:
            front, back = add_bf16(front, to_front), add_bf16(back, to_back)
        if distance > 1:
            front = lax.ppermute(front, "ctx", ahead)
            back = lax.ppermute(back, "ctx", behind)
        to_front, to_back = front, back
    return ring_term(terms, 0), to_front, to_back


def ring_scatter(own, to_front, to_back):
    _, ahead, behind, _ = ring_tools()
    from_back = lax.ppermute(to_front, "ctx", ahead)
    from_front = lax.ppermute(to_back, "ctx", behind)
    return (own.astype(f32) + from_back.astype(f32) + from_front.astype(f32)).astype(bf16)


def add_bf16(a, b):
    return (a.astype(f32) + b.astype(f32)).astype(bf16)


def params(megabytes=24):
    return pltpu.CompilerParams(vmem_limit_bytes=megabytes * 2**20)


def cost(flops, bytes_accessed, transcendentals=0):
    return pl.CostEstimate(
        flops=flops, bytes_accessed=bytes_accessed, transcendentals=transcendentals
    )


def token_terms_kernel(plan, *refs):
    out_ref = refs[-1]
    lefts, rights = refs[: -1 - len(plan)], refs[-1 - len(plan) : -1]
    rows = (((0,), (0,)), ((), ()))
    column = 0
    for (left, start, columns), right_ref in zip(plan, rights):
        own, got = lefts[2 * left], lefts[2 * left + 1]
        half, part = own.shape[0], slice(start, start + columns)
        total = lax.dot_general(own[...], right_ref[:half, part], rows, preferred_element_type=f32)
        total += lax.dot_general(got[...], right_ref[half:, part], rows, preferred_element_type=f32)
        out_ref[:, column : column + columns] = total.astype(bf16)
        column += columns


def token_terms(lefts, rights):
    tokens, width = lefts[0][0].shape
    tile = 512
    columns = sum(right[3] for right in rights)
    side = pl.BlockSpec((tokens, tile), lambda i: (0, i))
    arrays = [right[1] for right in rights]
    plan = [(right[0], right[2], right[3]) for right in rights]
    return pl.pallas_call(
        functools.partial(token_terms_kernel, plan),
        grid=(width // tile,),
        in_specs=[side] * (2 * len(lefts))
        + [pl.BlockSpec(array.shape, lambda i: (0, 0)) for array in arrays],
        out_specs=pl.BlockSpec((tile, columns), lambda i: (i, 0)),
        out_shape=jax.ShapeDtypeStruct((width, columns), bf16),
        compiler_params=params(),
        cost_estimate=cost(
            4 * tokens * width * columns,
            2 * (width * columns + 2 * tokens * width * len(lefts) + 2 * tokens * columns),
        ),
        name="token_terms",
    )(*(array for pair in lefts for array in pair), *arrays)


def attention_terms_kernel(normed_ref, mid_grad_ref, grads_ref, mixed_ref, out_ref):
    n_grads = grads_ref.shape[1]
    half = out_ref.shape[1]
    rows = (((0,), (0,)), ((), ()))
    inner = lax.dot_general(normed_ref[...], grads_ref[...], rows, preferred_element_type=f32)
    outer = lax.dot_general(mid_grad_ref[...], mixed_ref[...], rows, preferred_element_type=f32)
    for part in range(2):
        part_rows = slice(part * half, (part + 1) * half)
        out_ref[part, :, :n_grads] = inner[part_rows].astype(bf16)
        out_ref[part, :, n_grads:] = outer[part_rows].astype(bf16)


def attention_terms(normed, mid_grad, grads, mixed, count):
    tokens, width = normed.shape
    columns = grads.shape[1] + mixed.shape[1]
    tile = width // count
    return pl.pallas_call(
        attention_terms_kernel,
        grid=(count,),
        in_specs=[
            pl.BlockSpec((tokens, tile), lambda i: (0, i)),
            pl.BlockSpec((tokens, tile), lambda i: (0, i)),
            pl.BlockSpec((tokens, grads.shape[1]), lambda i: (0, 0)),
            pl.BlockSpec((tokens, mixed.shape[1]), lambda i: (0, 0)),
        ],
        out_specs=pl.BlockSpec((2, None, tile // 2, columns), lambda i: (0, i, 0, 0)),
        out_shape=jax.ShapeDtypeStruct((2, count, tile // 2, columns), bf16),
        compiler_params=params(),
        cost_estimate=pl.CostEstimate(
            flops=2 * tokens * width * columns,
            bytes_accessed=2 * (width * columns + 2 * tokens * width + tokens * columns),
            transcendentals=0,
        ),
        name="attention_terms",
    )(normed, mid_grad, grads, mixed)


def section_stacks_kernel(core_ref, *refs):
    first = core_ref[0] == 0
    for sources, target in ((refs[:4], refs[8]), (refs[4:8], refs[9])):
        low, high, got_low, got_high = (source[...] for source in sources)
        keep, got = jnp.where(first, low, high), jnp.where(first, got_low, got_high)
        target[...] = jnp.where(core_ref[0] == pl.program_id(0), keep, got)


def section_stacks(core, *sources):
    rows, width = sources[0].shape
    block = pl.BlockSpec((rows, width), lambda i, core: (0, 0))
    return pl.pallas_call(
        section_stacks_kernel,
        grid_spec=pltpu.PrefetchScalarGridSpec(
            num_scalar_prefetch=1,
            grid=(2,),
            in_specs=[block] * 8,
            out_specs=[pl.BlockSpec((None, rows, width), lambda i, core: (i, 0, 0))] * 2,
        ),
        out_shape=[jax.ShapeDtypeStruct((2, rows, width), bf16)] * 2,
        compiler_params=params(40),
        cost_estimate=cost(0, 12 * rows * width * 2),
        name="section_stacks",
    )(core.reshape(1), *sources)


def attention_outputs_kernel(core_ref, low_ref, high_ref, got_ref, query_ref, key_ref, value_ref, out_ref):
    first = core_ref[0] == 0
    keep = jnp.where(first, low_ref[...], high_ref[...])
    got = got_ref[...]
    parts = [jnp.where(first == (side == 0), keep, got).astype(f32) for side in range(2)]
    whole = jnp.concatenate(parts, axis=0)
    column = 0
    for ref in (query_ref, key_ref, value_ref):
        ref[...] = whole[:, column : column + ref.shape[1]]
        column += ref.shape[1]
    out_ref[...] = whole[:, column:].T


def attention_outputs(core, low, high, got, sizes):
    n_query, n_key = sizes
    rows, columns = got.shape
    whole = lambda *shape: pl.BlockSpec(shape, lambda i, core: (0, 0))
    shapes = [(2 * rows, n_query), (2 * rows, n_key), (2 * rows, n_key), (n_query, 2 * rows)]
    return pl.pallas_call(
        attention_outputs_kernel,
        grid_spec=pltpu.PrefetchScalarGridSpec(
            num_scalar_prefetch=1,
            grid=(1,),
            in_specs=[whole(rows, columns)] * 3,
            out_specs=[whole(*shape) for shape in shapes],
        ),
        out_shape=[jax.ShapeDtypeStruct(shape, f32) for shape in shapes],
        compiler_params=params(),
        cost_estimate=cost(0, rows * columns * 14),
        name="attention_outputs",
    )(core.reshape(1), low, high, got)


def wide_outputs_kernel(columns, core_ref, *refs):
    first = core_ref[0] == 0
    gate_ref, up_ref = refs[8:]
    sections = []
    for place in range(4):
        early, late = refs[place][...], refs[4 + place][...]
        head = columns[place % 2]
        rest = gate_ref.shape[1] // 2 - head
        gate = jnp.concatenate([early, late[:, :rest]], axis=1)
        sections.append((gate, late[:, rest:]))
    low, high, got_low, got_high = sections
    for target, part in ((gate_ref, 0), (up_ref, 1)):
        units = target.shape[1] // 2
        keep = jnp.where(first, low[part], high[part])
        got = jnp.where(first, got_low[part], got_high[part])
        target[:, :units] = jnp.where(first, keep, got).astype(f32)
        target[:, units:] = jnp.where(first, got, keep).astype(f32)


def wide_outputs(core, early, late, units):
    rows = early[0].shape[0]
    columns = [share.shape[1] - units for share in early[:2]]
    tile = 128

    def early_spec(head):
        return pl.BlockSpec((tile, head), lambda i, core: (i, units // head))

    return pl.pallas_call(
        functools.partial(wide_outputs_kernel, columns),
        grid_spec=pltpu.PrefetchScalarGridSpec(
            num_scalar_prefetch=1,
            grid=(rows // tile,),
            in_specs=[early_spec(head) for head in columns * 2]
            + [pl.BlockSpec((tile, share.shape[1]), lambda i, core: (i, 0)) for share in late],
            out_specs=[pl.BlockSpec((tile, 2 * units), lambda i, core: (i, 0))] * 2,
        ),
        out_shape=[jax.ShapeDtypeStruct((rows, 2 * units), f32)] * 2,
        compiler_params=params(),
        cost_estimate=cost(0, rows * 32 * units),
        name="wide_outputs",
    )(core.reshape(1), *early, *late)


def down_outputs_kernel(core_ref, low_ref, high_ref, got_low_ref, got_high_ref, down_ref):
    first = core_ref[0] == 0
    units = low_ref.shape[1]
    keep = jnp.where(first, low_ref[...], high_ref[...])
    got = jnp.where(first, got_low_ref[...], got_high_ref[...])
    for side in range(2):
        part = jnp.where(first == (side == 0), keep, got).astype(f32)
        down_ref[side * units : (side + 1) * units, :] = part.T


def down_outputs(core, early, units):
    rows = early[0].shape[0]
    tile = 128
    return pl.pallas_call(
        down_outputs_kernel,
        grid_spec=pltpu.PrefetchScalarGridSpec(
            num_scalar_prefetch=1,
            grid=(rows // tile,),
            in_specs=[pl.BlockSpec((tile, units), lambda i, core: (i, 0))] * 4,
            out_specs=pl.BlockSpec((2 * units, tile), lambda i, core: (0, i)),
        ),
        out_shape=jax.ShapeDtypeStruct((2 * units, rows), f32),
        compiler_params=params(),
        cost_estimate=cost(0, rows * units * 16),
        name="down_outputs",
    )(core.reshape(1), *early)


def pin(value, *others):
    return lax.optimization_barrier((value, *others))


def share_gains(terms):
    core, shard = lax.axis_index("pipe"), lax.axis_index("ctx")
    count = lax.axis_size("ctx")
    own = lax.dynamic_index_in_dim(terms, core, 0, keepdims=False)
    other = lax.dynamic_index_in_dim(terms, 1 - core, 0, keepdims=False)
    total = own + swap_cores(other)
    blocks = total.reshape(2, count, -1)

    def block(index):
        return lax.dynamic_index_in_dim(blocks, index, 1, keepdims=False)

    result = block(shard)
    for step in range(1, count):
        route = [(i, i ^ step) for i in range(count)]
        result = result + lax.ppermute(block(shard ^ step), "ctx", route)
    return result


def product(left, right):
    return lax.dot_general(
        left, right, (((1,), (0,)), ((), ())), preferred_element_type=f32
    )


def rows_product(left, right):
    return lax.dot_general(
        left, right, (((0,), (0,)), ((), ())), preferred_element_type=f32
    )


def cols_product(left, right):
    return lax.dot_general(
        left, right, (((1,), (1,)), ((), ())), preferred_element_type=f32
    )


def norm_forward(stream, gain_vector):
    inv_rms = lax.rsqrt(jnp.mean(stream * stream, axis=-1) + epsilon)
    return ((stream * inv_rms[:, None] * gain_vector[None, :]).astype(bf16), inv_rms)


def norm_backward(stream, inv_rms, gain_vector, upstream):
    weighted = upstream * gain_vector[None, :]
    gain_grad = jnp.sum(upstream * stream * inv_rms[:, None], axis=0)
    inner_mean = jnp.mean(stream * weighted, axis=-1)
    stream_grad = (
        weighted * inv_rms[:, None] - stream * (inv_rms * inv_rms * inv_rms * inner_mean)[:, None]
    )
    return (stream_grad, gain_grad)


def sum_tensor(partial, *others):
    partial = partial.astype(bf16)
    if others:
        partial, *others = pin(partial, *others)
    return lax.psum(partial, "tensor"), *others


def own_share(partial, rows):
    arrived = swap_cores(partial[rows:].astype(bf16))
    return partial[:rows] + arrived.astype(f32)


def half_swap(values):
    lanes = lax.broadcasted_iota(jnp.int32, values.shape, 1)
    count = values.shape[1]
    quarter = HEAD_DIM // 2
    return jnp.where(
        lanes % HEAD_DIM < quarter,
        pltpu.roll(values, count - quarter, 1),
        pltpu.roll(values, quarter, 1),
    )


def wide_table(table, columns):
    return jnp.concatenate([table] * (columns // table.shape[1]), axis=1)


def rope_tables(positions_row, width):
    frequency = jnp.exp(
        jnp.arange(width // 2, dtype=f32) * (-2.0 * math.log(rope_base) / width)
    )
    angles = positions_row.astype(f32)[:, None] * frequency[None, :]
    cosine, sine = jnp.cos(angles), jnp.sin(angles)
    return (
        jnp.concatenate([cosine] * 4, axis=1),
        jnp.concatenate([-sine, sine] * 2, axis=1),
    )


def head_inputs_kernel(sizes, stream_ref, gain_ref, wide_ref, cos_ref, sin_ref,
                       normed_ref, rms_ref, query_ref, own_ref):
    n_query, n_key = sizes
    stream = stream_ref[...].astype(f32)
    inv_rms = lax.rsqrt(jnp.mean(stream * stream, axis=1, keepdims=True) + epsilon)
    normed = (stream * inv_rms * gain_ref[...]).astype(bf16)
    normed_ref[...] = normed
    rms_ref[...] = inv_rms
    raw = jnp.dot(normed, wide_ref[...], preferred_element_type=f32)
    turned = raw[:, : n_query + n_key]
    cosine = wide_table(cos_ref[...], n_query + n_key)
    sine = wide_table(sin_ref[...], n_query + n_key)
    turned = turned * cosine + half_swap(turned) * sine
    query_ref[...] = turned[:, :n_query].astype(bf16)
    own_ref[:, :n_key] = turned[:, n_query:].astype(bf16)
    own_ref[:, n_key:] = raw[:, n_query + n_key :].astype(bf16)


def head_inputs(stream, gain, wide, tables, sizes):
    n_query, n_key = sizes
    rows, width = stream.shape
    columns = n_query + 2 * n_key
    whole = lambda *shape: pl.BlockSpec(shape, lambda i: (0,) * len(shape))
    return pl.pallas_call(
        functools.partial(head_inputs_kernel, sizes),
        grid=(1,),
        in_specs=[
            whole(rows, width),
            whole(1, width),
            whole(width, columns),
            whole(rows, 2 * HEAD_DIM),
            whole(rows, 2 * HEAD_DIM),
        ],
        out_specs=[whole(rows, width), whole(rows, 1), whole(rows, n_query), whole(rows, 2 * n_key)],
        out_shape=[
            jax.ShapeDtypeStruct((rows, width), bf16),
            jax.ShapeDtypeStruct((rows, 1), f32),
            jax.ShapeDtypeStruct((rows, n_query), bf16),
            jax.ShapeDtypeStruct((rows, 2 * n_key), bf16),
        ],
        compiler_params=params(),
        cost_estimate=cost(2 * rows * width * columns, 2 * width * (columns + 4 * rows)),
        name="head_inputs",
    )(stream, gain[None], wide, *tables)


def masked_scores(query, keys, allowed):
    raw = lax.dot_general(query, keys, (((1,), (1,)), ((), ())), preferred_element_type=f32)
    return jnp.where(allowed, raw * HEAD_DIM ** (-0.5), -1e30)


def allowed_pairs(pos, rows):
    distance = (
        lax.broadcasted_iota(jnp.int32, (rows, 2 * rows), 0)
        - lax.broadcasted_iota(jnp.int32, (rows, 2 * rows), 1)
        + rows
    )
    return (distance >= 0) & (distance <= pos)


def head_slice(index):
    return slice(index * HEAD_DIM, (index + 1) * HEAD_DIM)


def mix_kernel(n_key, pos_ref, query_ref, tail_ref, own_ref, wide_ref,
               mixed_ref, log_ref, partial_ref, window, mixed_all):
    rows, n_query = query_ref.shape

    @pl.when(pl.program_id(0) == 0)
    def _():
        window[:rows] = tail_ref[...]
        window[rows:] = own_ref[...]
        allowed = allowed_pairs(pos_ref[...], rows)
        group = HEADS // KV_HEADS
        logs, mixed = [], []
        for head in range(n_query // HEAD_DIM):
            keys = window[:, head_slice(head // group)]
            values = window[:, head_slice((n_key // HEAD_DIM) + head // group)]
            masked = masked_scores(query_ref[:, head_slice(head)], keys, allowed)
            top = jnp.max(masked, axis=1, keepdims=True)
            exponent = jnp.exp(masked - top)
            total = jnp.sum(exponent, axis=1, keepdims=True)
            weights = (exponent * (1.0 / total)).astype(bf16)
            mixed.append(jnp.dot(weights, values, preferred_element_type=f32).astype(bf16))
            logs.append(top + jnp.log(total))
        everything = jnp.concatenate(mixed, axis=1)
        mixed_all[...] = everything
        mixed_ref[...] = everything
        log_ref[...] = jnp.concatenate(logs, axis=1)

    partial_ref[...] = lax.dot_general(
        mixed_all[...],
        wide_ref[...],
        (((1,), (1,)), ((), ())),
        preferred_element_type=f32,
    ).astype(bf16)


def mix(pos, queries, tail, own, wide, n_key):
    rows, n_query = queries.shape
    width, columns = wide.shape
    tile = 512
    heads = n_query // HEAD_DIM
    whole = lambda *shape: pl.BlockSpec(shape, lambda i: (0,) * len(shape))
    return pl.pallas_call(
        functools.partial(mix_kernel, n_key),
        grid=(width // tile,),
        in_specs=[
            whole(rows, 1),
            whole(rows, n_query),
            whole(rows, 2 * n_key),
            whole(rows, 2 * n_key),
            pl.BlockSpec((tile, columns), lambda i: (i, 0)),
        ],
        out_specs=[
            whole(rows, n_query),
            whole(rows, heads),
            pl.BlockSpec((rows, tile), lambda i: (0, i)),
        ],
        out_shape=[
            jax.ShapeDtypeStruct((rows, n_query), bf16),
            jax.ShapeDtypeStruct((rows, heads), f32),
            jax.ShapeDtypeStruct((rows, width), bf16),
        ],
        scratch_shapes=[pltpu.VMEM((2 * rows, 2 * n_key), bf16), pltpu.VMEM((rows, n_query), bf16)],
        compiler_params=params(),
        cost_estimate=cost(
            2 * rows * n_query * (width + 4 * rows), 2 * width * (columns + rows), 2 * rows * rows * heads
        ),
        name="mix",
    )(pos, queries, tail, own, wide)


def mix_back_kernel(n_key, pos_ref, query_ref, tail_ref, own_ref, mixed_ref, log_ref, cos_ref, sin_ref,
                    mid_grad_ref, wide_ref, query_grad_ref, back_ref, own_grad_ref, mid_b_ref,
                    window, mixed_grad):
    rows, n_query = query_ref.shape
    step = pl.program_id(0)
    mid_b = mid_grad_ref[...].astype(bf16)
    mid_b_ref[...] = mid_b
    part = jnp.dot(mid_b, wide_ref[...], preferred_element_type=f32)

    @pl.when(step == 0)
    def _():
        mixed_grad[...] = part

    @pl.when(step > 0)
    def _():
        mixed_grad[...] += part

    @pl.when(step == pl.num_programs(0) - 1)
    def _():
        window[:rows] = tail_ref[...]
        window[rows:] = own_ref[...]
        allowed = allowed_pairs(pos_ref[...], rows)
        group = HEADS // KV_HEADS
        groups = n_key // HEAD_DIM
        scale = HEAD_DIM ** (-0.5)
        grads = mixed_grad[...].astype(bf16)
        over_rows = (((0,), (0,)), ((), ()))
        over_columns = (((1,), (1,)), ((), ()))
        query_grads, key_grads, value_grads = [], [None] * groups, [None] * groups
        for head in range(n_query // HEAD_DIM):
            at = head // group
            keys = window[:, head_slice(at)]
            values = window[:, head_slice(groups + at)]
            query = query_ref[:, head_slice(head)]
            grad = grads[:, head_slice(head)]
            masked = masked_scores(query, keys, allowed)
            prob = jnp.exp(masked - log_ref[:, head : head + 1])
            prob_grad = lax.dot_general(grad, values, over_columns, preferred_element_type=f32)
            delta = jnp.sum(
                grad.astype(f32) * mixed_ref[:, head_slice(head)].astype(f32), axis=1, keepdims=True
            )
            score_grad = (prob * (prob_grad - delta)).astype(bf16)
            query_grads.append(jnp.dot(score_grad, keys, preferred_element_type=f32))
            key_part = lax.dot_general(score_grad, query, over_rows, preferred_element_type=f32)
            value_part = lax.dot_general(
                prob.astype(bf16), grad, over_rows, preferred_element_type=f32
            )
            key_grads[at] = key_part if key_grads[at] is None else key_grads[at] + key_part
            value_grads[at] = value_part if value_grads[at] is None else value_grads[at] + value_part
        query_grad = jnp.concatenate(query_grads, axis=1) * scale
        query_grad = query_grad * wide_table(cos_ref[...], n_query) - half_swap(
            query_grad
        ) * wide_table(sin_ref[...], n_query)
        query_grad_ref[...] = query_grad.astype(bf16)
        key_grad = jnp.concatenate(key_grads, axis=1) * scale
        value_grad = jnp.concatenate(value_grads, axis=1)
        back_ref[:, :n_key] = key_grad[:rows].astype(bf16)
        back_ref[:, n_key:] = value_grad[:rows].astype(bf16)
        own_grad_ref[:, :n_key] = key_grad[rows:]
        own_grad_ref[:, n_key:] = value_grad[rows:]


def mix_back(pos, queries, tail, own, mixed, logs, tables, mid_grad, wide, n_key):
    rows, n_query = queries.shape
    width, columns = wide.shape
    tile = 512
    heads = n_query // HEAD_DIM
    whole = lambda *shape: pl.BlockSpec(shape, lambda i: (0,) * len(shape))
    return pl.pallas_call(
        functools.partial(mix_back_kernel, n_key),
        grid=(width // tile,),
        in_specs=[
            whole(rows, 1),
            whole(rows, n_query),
            whole(rows, 2 * n_key),
            whole(rows, 2 * n_key),
            whole(rows, n_query),
            whole(rows, heads),
            whole(rows, 2 * HEAD_DIM),
            whole(rows, 2 * HEAD_DIM),
            pl.BlockSpec((rows, tile), lambda i: (0, i)),
            pl.BlockSpec((tile, columns), lambda i: (i, 0)),
        ],
        out_specs=[
            whole(rows, n_query),
            whole(rows, 2 * n_key),
            whole(rows, 2 * n_key),
            pl.BlockSpec((rows, tile), lambda i: (0, i)),
        ],
        out_shape=[
            jax.ShapeDtypeStruct((rows, n_query), bf16),
            jax.ShapeDtypeStruct((rows, 2 * n_key), bf16),
            jax.ShapeDtypeStruct((rows, 2 * n_key), f32),
            jax.ShapeDtypeStruct((rows, width), bf16),
        ],
        scratch_shapes=[pltpu.VMEM((2 * rows, 2 * n_key), bf16), pltpu.VMEM((rows, n_query), f32)],
        compiler_params=params(),
        cost_estimate=cost(
            2 * rows * n_query * (width + 10 * rows), 2 * width * (columns + 3 * rows), 2 * rows * rows * heads
        ),
        name="mix_back",
    )(pos, queries, tail, own, mixed, logs, *tables, mid_grad, wide)


def head_grads_kernel(n_key, query_grad_ref, own_grad_ref, back_ref, cos_ref, sin_ref, wide_ref,
                      grads_ref, partial_ref, grads):
    n_query = query_grad_ref.shape[1]

    @pl.when(pl.program_id(0) == 0)
    def _():
        own = own_grad_ref[...] + back_ref[...].astype(f32)
        keys = own[:, :n_key]
        keys = keys * wide_table(cos_ref[...], n_key) - half_swap(keys) * wide_table(
            sin_ref[...], n_key
        )
        grads[:, :n_query] = query_grad_ref[...]
        grads[:, n_query : n_query + n_key] = keys.astype(bf16)
        grads[:, n_query + n_key :] = own[:, n_key:].astype(bf16)
        grads_ref[...] = grads[...]

    partial_ref[...] = lax.dot_general(
        grads[...], wide_ref[...], (((1,), (1,)), ((), ())), preferred_element_type=f32
    ).astype(bf16)


def head_grads(query_grad, own_grad, back, tables, wide, n_key):
    rows, n_query = query_grad.shape
    width = wide.shape[0]
    columns = n_query + 2 * n_key
    tile = 512
    whole = lambda *shape: pl.BlockSpec(shape, lambda i: (0,) * len(shape))
    return pl.pallas_call(
        functools.partial(head_grads_kernel, n_key),
        grid=(width // tile,),
        in_specs=[
            whole(rows, n_query),
            whole(rows, 2 * n_key),
            whole(rows, 2 * n_key),
            whole(rows, 2 * HEAD_DIM),
            whole(rows, 2 * HEAD_DIM),
            pl.BlockSpec((tile, columns), lambda i: (i, 0)),
        ],
        out_specs=[whole(rows, columns), pl.BlockSpec((rows, tile), lambda i: (0, i))],
        out_shape=[
            jax.ShapeDtypeStruct((rows, columns), bf16),
            jax.ShapeDtypeStruct((rows, width), bf16),
        ],
        scratch_shapes=[pltpu.VMEM((rows, columns), bf16)],
        compiler_params=params(),
        cost_estimate=cost(2 * rows * width * columns, 2 * width * (columns + rows)),
        name="head_grads",
    )(query_grad, own_grad, back, *tables, wide)


def attention_forward(stream, gain, wide, place, *others):
    pos, tables, sizes = place
    normed, inv_rms, queries, own = head_inputs(stream, gain, wide[0], tables, sizes)
    tail = from_behind(own, "ctx", 1)
    mixed, logs, partial = mix(pos, queries, tail, own, wide[1], sizes[1])
    total, *others = sum_tensor(partial, *others)
    return total, (stream.astype(f32), inv_rms[:, 0], normed, queries, tail, own, mixed, logs), *others


def ffn_forward_in(middle, gain, wide, hidden_width):
    normed, inv_rms = norm_forward(middle, gain)
    got = swap_cores(normed)
    gate_up = product(jnp.concatenate([normed, got], axis=0), wide)
    gate = gate_up[:, :hidden_width]
    up = gate_up[:, hidden_width:]
    hidden = (jax.nn.silu(gate) * up).astype(bf16)
    return (middle, inv_rms, normed, got, gate, up, hidden)


def ffn_share(state, down):
    middle, hidden = state[0], state[-1]
    return own_share(cols_product(hidden, down), middle.shape[0]).astype(bf16)


def ffn_backward(own_grad, other_grad, state, wide, down, head, *others):
    middle, _, normed, got, gate, up, hidden = state
    hidden_grad = product(jnp.concatenate([own_grad, other_grad], axis=0), down)
    sigmoid_gate = jax.nn.sigmoid(gate)
    gate_grad = (hidden_grad * up * sigmoid_gate * (1.0 + gate * (1.0 - sigmoid_gate))).astype(bf16)
    up_grad = (hidden_grad * gate * sigmoid_gate).astype(bf16)
    units = gate.shape[1]
    partial = cols_product(jnp.concatenate([gate_grad, up_grad], axis=1), wide)
    normed_grad, *others = sum_tensor(own_share(partial, middle.shape[0]), *others)
    own_sides, norm_sides = (own_grad, other_grad), (normed, got)
    early = token_terms([own_sides, norm_sides], [(0, hidden, 0, units), (1, gate_grad, 0, head)])
    early = lax.psum_scatter(early, "ctx", scatter_dimension=0, tiled=True)
    late = token_terms([norm_sides], [(0, gate_grad, head, units - head), (0, up_grad, 0, units)])
    return normed_grad, early, late, *others


def ffn_backward_out(upstream, normed_grad, state, gain):
    mid_part, gain_term = norm_backward(state[0], state[1], gain, normed_grad.astype(f32))
    return upstream.astype(f32) + mid_part, gain_term


def attention_backward(mid_grad, saved, wide, place, *others):
    pos, tables, sizes = place
    _, _, normed, queries, tail, own, mixed, logs = saved
    query_grad, back, own_grad, mid_grad_b = mix_back(
        pos, queries, tail, own, mixed, logs, tables, mid_grad, wide[1], sizes[1]
    )
    back = from_behind(back, "ctx", -1)
    grads, partial = head_grads(query_grad, own_grad, back, tables, wide[0], sizes[1])
    normed_grad, *others = sum_tensor(partial, *others)
    terms = attention_terms(normed, mid_grad_b, grads, mixed, lax.axis_size("ctx"))
    core = lax.axis_index("pipe")
    mine = lax.dynamic_index_in_dim(terms, core, 0, keepdims=False)
    theirs = lax.dynamic_index_in_dim(terms, 1 - core, 0, keepdims=False)
    return normed_grad, add_bf16(mine, swap_cores(theirs)), *others


def attention_backward_out(mid_grad, normed_grad, saved, gain):
    part, gain_term = norm_backward(saved[0], saved[1], gain, normed_grad.astype(f32))
    return (mid_grad + part).astype(bf16), gain_term


def on_device(
    inputs,
    out_grad,
    positions,
    attn_gain,
    w_query,
    w_key,
    w_value,
    w_out,
    ffn_gain,
    w_gate,
    w_up,
    w_down,
):
    core = lax.axis_index("pipe")
    first = core == 0
    shard = lax.axis_index("ctx")
    rows = inputs.shape[1]
    width = inputs.shape[2]
    n_query = w_query.shape[2]
    n_key = w_key.shape[2]
    half = w_gate.shape[2] // 2

    def pick(pair, index):
        return lax.dynamic_index_in_dim(pair, index, 0, keepdims=False)

    def mine_theirs(array, axis):
        size = array.shape[axis] // 2
        mine = lax.dynamic_slice_in_dim(array, core * size, size, axis)
        theirs = lax.dynamic_slice_in_dim(array, (1 - core) * size, size, axis)
        return mine, theirs

    count = lax.axis_size("ctx")
    gain_row = jnp.concatenate([attn_gain, ffn_gain], axis=1)
    attn_shard = jnp.concatenate([w_query[0], w_key[0], w_value[0], w_out[0].T], axis=1)
    wide_columns = attn_shard.shape[1]
    gain_rows = jnp.pad(gain_row, ((0, 15), (0, wide_columns - gain_row.shape[1])))
    rows_mine, rows_theirs = mine_theirs(attn_shard, 0)
    attn_keep = jnp.concatenate([rows_mine, gain_rows], axis=0)
    attn_got = swap_cores(jnp.concatenate([rows_theirs, gain_rows], axis=0))

    inner_columns = n_query + 2 * n_key

    def attn_weights(pieces):
        got = swap_cores(pieces)
        both = jnp.stack([jnp.where(first, pieces, got), jnp.where(first, got, pieces)], axis=1)
        part_rows = attn_shard.shape[0] // 2
        wide = both[:, :, :part_rows].reshape(width, wide_columns)
        wide = (wide[:, :inner_columns], wide[:, inner_columns:])
        row = pieces[:, part_rows, : gain_row.shape[1]].astype(f32)
        return wide, row.reshape(count, 2, -1).transpose(1, 0, 2).reshape(2, width)

    gate_mine, gate_theirs = mine_theirs(w_gate[0], 1)
    up_mine, up_theirs = mine_theirs(w_up[0], 1)
    wide_keep = jnp.concatenate([gate_mine, up_mine], axis=1)
    wide_got = swap_cores(jnp.concatenate([gate_theirs, up_theirs], axis=1))
    down_mine, down_theirs = mine_theirs(w_down[0], 0)
    down_keep, down_got = down_mine.T, swap_cores(down_theirs.T)

    def for_sections(keep, got):
        return [jnp.where(first, keep, got), jnp.where(first, got, keep)]

    def gather(shard_part):
        return lax.all_gather(shard_part, "ctx", axis=0, tiled=True)

    attn_parts = for_sections(attn_keep, attn_got)
    wide_parts = for_sections(wide_keep, wide_got)
    down_parts = for_sections(down_keep, down_got)
    wide_low = lax.all_gather(wide_parts[0], ("pipe", "ctx"), axis=0, tiled=True)
    attn_pieces, attn_parts[1], wide_parts[1], *down_parts = pin(
        ring_gather(*ring_gather_start(attn_parts[0])), attn_parts[1], wide_parts[1], *down_parts
    )
    attn_low, gains_low = attn_weights(attn_pieces)
    down_low = gather(down_parts[0])
    wide_high = gather(wide_parts[1])
    down_high = gather(down_parts[1])

    pos_row = pick(positions, core)
    place = (pos_row[:, None], rope_tables(pos_row, HEAD_DIM), (n_query, n_key))

    def scatter(terms):
        return lax.psum_scatter(terms, "ctx", scatter_dimension=0, tiled=True)

    def give_low(share):
        return lax.ppermute(share, "pipe", [(1, 0)])

    def give_high(share):
        return lax.ppermute(share, "pipe", [(0, 1)])

    stream = pick(inputs, core)
    total, attn_saved_low, wide_low, attn_part_high = attention_forward(
        stream, gains_low[0], attn_low, place, wide_low, attn_parts[1]
    )
    wide_low = pick(wide_low.reshape(2, width, -1), core)
    total, wide_low, attn_ring = pin(total, wide_low, ring_gather_start(attn_part_high))
    middle = attn_saved_low[0] + total.astype(f32)
    state_low = ffn_forward_in(middle, gains_low[1], wide_low, half)
    own_grad, other_grad = pick(out_grad, core), pick(out_grad, 1 - core)
    (total,) = sum_tensor(ffn_share(state_low, down_low))
    total, own_grad, other_grad, (attn_high, gains_high) = pin(
        total, own_grad, other_grad, attn_weights(ring_gather(*attn_ring))
    )
    out_low = (middle + total.astype(f32)).astype(bf16)
    total, attn_saved_high, wide_high = attention_forward(
        out_low, gains_high[0], attn_high, place, wide_high
    )
    total, got_out_low = pin(total, swap_cores(out_low))
    middle = attn_saved_high[0] + total.astype(f32)
    state_high = ffn_forward_in(middle, gains_high[1], wide_high, half)

    normed_grad, early_high, late_high = ffn_backward(
        own_grad, other_grad, state_high, wide_high, down_high, half // 2
    )
    normed_grad, late_high = pin(normed_grad, late_high)
    mid_grad, ffn_gain_high = ffn_backward_out(own_grad, normed_grad, state_high, gains_high[1])
    late_high = scatter(late_high)
    normed_grad, summed, early_high = attention_backward(
        mid_grad, attn_saved_high, attn_high, place, early_high
    )
    normed_grad, attn_ring, out_share = pin(
        normed_grad, ring_scatter_start(summed), ffn_share(state_high, down_high)
    )
    boundary_high, attn_gain_high = attention_backward_out(
        mid_grad, normed_grad, attn_saved_high, gains_high[0]
    )
    got_boundary_high = swap_cores(boundary_high)
    normed_grad, early_low, late_low, late_high = ffn_backward(
        boundary_high, got_boundary_high, state_low, wide_low, down_low, half // 4, late_high
    )
    normed_grad, late_low, attn_share_high = pin(normed_grad, late_low, ring_scatter(*attn_ring))
    mid_grad, ffn_gain_low = ffn_backward_out(
        boundary_high, normed_grad, state_low, gains_low[1]
    )
    late_low = scatter(late_low)
    normed_grad, summed, early_low = attention_backward(
        mid_grad, attn_saved_low, attn_low, place, early_low
    )
    def from_other(low, high):
        return swap_cores(jnp.where(first, high, low))

    (total,) = sum_tensor(out_share)
    attn_pair = (ring_scatter(*ring_scatter_start(summed)), attn_share_high)
    attn_outs = attention_outputs(core, *attn_pair, from_other(*attn_pair), (n_query, n_key))
    early = (early_low, early_high, give_low(early_low), give_high(early_high))
    down_out = down_outputs(core, early, half)
    normed_grad, down_out, attn_outs, got_late_high = pin(
        normed_grad, down_out, attn_outs, give_high(late_high)
    )
    out_high = (middle + total.astype(f32)).astype(bf16)

    boundary_low, attn_gain_low = attention_backward_out(
        mid_grad, normed_grad, attn_saved_low, gains_low[0]
    )
    gains_out = share_gains(
        jnp.stack(
            [jnp.stack([attn_gain_low, ffn_gain_low]), jnp.stack([attn_gain_high, ffn_gain_high])]
        )
    )
    late_low, gains_out, got_out_high, got_boundary_low = pin(
        late_low, gains_out, swap_cores(out_high), swap_cores(boundary_low)
    )
    outs = (out_low, out_high, got_out_low, got_out_high)
    boundaries = (boundary_low, boundary_high, got_boundary_low, got_boundary_high)
    section_outputs, boundary_grads = section_stacks(core, *outs, *boundaries)
    late = (late_low, late_high, give_low(late_low), got_late_high)
    gate_out, up_out = wide_outputs(core, early, late, half)
    query_out, key_out, value_out, attn_out = attn_outs
    return (
        section_outputs[None],
        boundary_grads[None],
        gains_out[:1],
        query_out[None],
        key_out[None],
        value_out[None],
        attn_out[None],
        gains_out[1:],
        gate_out[None],
        up_out[None],
        down_out[None],
    )


def solution(mesh):
    in_specs = (
        P(None, "ctx", None),
        P(None, "ctx", None),
        P(None, "ctx"),
        P("pipe", "ctx"),
        P("pipe", "ctx", "tensor"),
        P("pipe", "ctx", "tensor"),
        P("pipe", "ctx", "tensor"),
        P("pipe", "tensor", "ctx"),
        P("pipe", "ctx"),
        P("pipe", "ctx", "tensor"),
        P("pipe", "ctx", "tensor"),
        P("pipe", "tensor", "ctx"),
    )
    out_specs = (
        P("pipe", None, "ctx", None),
        P("pipe", None, "ctx", None),
        P("pipe", "ctx"),
        P("pipe", "ctx", "tensor"),
        P("pipe", "ctx", "tensor"),
        P("pipe", "ctx", "tensor"),
        P("pipe", "tensor", "ctx"),
        P("pipe", "ctx"),
        P("pipe", "ctx", "tensor"),
        P("pipe", "ctx", "tensor"),
        P("pipe", "tensor", "ctx"),
    )
    return jax.shard_map(
        on_device, mesh=mesh, in_specs=in_specs, out_specs=out_specs, check_vma=False
    )
```

```python
import functools
import math

import jax
import jax.numpy as jnp
from jax import lax
from jax.experimental import pallas as pl
from jax.experimental.pallas import tpu as pltpu
from jax.sharding import PartitionSpec as P

HEADS = 32
KV_HEADS = 8
HEAD_DIM = 64
MAXLEN = 256

epsilon = 1e-05
rope_base = 500000.0
bf16 = jnp.bfloat16
f32 = jnp.float32


def swap_cores(block):
    return lax.ppermute(block, "pipe", [(0, 1), (1, 0)])


def from_behind(block, axis, distance):
    devices = range(lax.axis_size(axis))
    route = [(i - distance, i) for i in devices if i - distance in devices]
    return lax.ppermute(block, axis, route)


def ring_order(count):
    across = 1 << (count.bit_length() - 1) // 2
    down = count // across
    walk = [(0, x) for x in range(across)]
    for y in range(1, down):
        columns = range(1, across)
        walk += [(y, x) for x in (columns if y % 2 == 0 else reversed(columns))]
    walk += [(y, 0) for y in range(down - 1, 0, -1)]
    return [y * across + x for y, x in walk]


def take(array, index, axis=0):
    return lax.dynamic_index_in_dim(
        array, index, axis, keepdims=False, allow_negative_indices=False
    )


def ring_tools():
    count = lax.axis_size("ctx")
    order = ring_order(count)
    ahead = [(order[i], order[(i + 1) % count]) for i in range(count)]
    behind = [(b, a) for a, b in ahead]
    device = lax.axis_index("ctx")

    def device_at(distance):
        if order == [0, 1, 3, 2]:
            place = ((device ^ (device >> 1)) + distance % count) & 3
            return place ^ (place >> 1)
        place = jnp.asarray([order.index(i) for i in range(count)], jnp.int32)
        return take(jnp.asarray(order * 2, jnp.int32), take(place, device) + distance % count)

    return count, ahead, behind, device_at


def ring_gather_start(block):
    count, ahead, behind, _ = ring_tools()
    from_back, from_front = [block], [block]
    for _ in range(1, count // 2):
        from_back.append(lax.ppermute(from_back[-1], "ctx", ahead))
        from_front.append(lax.ppermute(from_front[-1], "ctx", behind))
    return from_back, from_front


def ring_gather(from_back, from_front):
    count, ahead, behind, device_at = ring_tools()
    block = from_back[0]
    half = block.shape[1] // 2
    left = lax.ppermute(from_back[-1][:, :half], "ctx", ahead)
    right = lax.ppermute(from_front[-1][:, half:], "ctx", behind)
    out = jnp.zeros((count,) + block.shape, block.dtype)

    def put(out, piece, distance, column=0):
        return lax.dynamic_update_slice(
            out, piece[None], (device_at(distance), 0, column), allow_negative_indices=False
        )

    out = put(out, block, 0)
    for distance in range(1, count // 2):
        out = put(out, from_back[distance], -distance)
        out = put(out, from_front[distance], distance)
    out = put(out, left, count // 2)
    return put(out, right, count // 2, half)


def ring_term(terms, distance):
    return take(terms, ring_tools()[3](distance))


def ring_scatter_start(terms):
    count, ahead, behind, _ = ring_tools()
    half = terms.shape[2] // 2
    far = ring_term(terms, count // 2)
    to_front = lax.ppermute(far[:, :half], "ctx", ahead)
    to_back = lax.ppermute(far[:, half:], "ctx", behind)
    for distance in range(count // 2 - 1, 0, -1):
        front, back = ring_term(terms, distance), ring_term(terms, -distance)
        if distance == count // 2 - 1:
            front = jnp.concatenate([add_bf16(front[:, :half], to_front), front[:, half:]], axis=1)
            back = jnp.concatenate([back[:, :half], add_bf16(back[:, half:], to_back)], axis=1)
        else:
            front, back = add_bf16(front, to_front), add_bf16(back, to_back)
        if distance > 1:
            front = lax.ppermute(front, "ctx", ahead)
            back = lax.ppermute(back, "ctx", behind)
        to_front, to_back = front, back
    return ring_term(terms, 0), to_front, to_back


def ring_scatter(own, to_front, to_back):
    _, ahead, behind, _ = ring_tools()
    from_back = lax.ppermute(to_front, "ctx", ahead)
    from_front = lax.ppermute(to_back, "ctx", behind)
    return (own.astype(f32) + from_back.astype(f32) + from_front.astype(f32)).astype(bf16)


def add_bf16(a, b):
    return (a.astype(f32) + b.astype(f32)).astype(bf16)


def params(megabytes=24):
    return pltpu.CompilerParams(vmem_limit_bytes=megabytes * 2**20)


def cost(flops, bytes_accessed, transcendentals=0):
    return pl.CostEstimate(
        flops=flops, bytes_accessed=bytes_accessed, transcendentals=transcendentals
    )


def token_terms_kernel(plan, *refs):
    out_ref = refs[-1]
    lefts, rights = refs[: -1 - len(plan)], refs[-1 - len(plan) : -1]
    rows = (((0,), (0,)), ((), ()))
    column = 0
    for (left, start, columns), right_ref in zip(plan, rights):
        own, got = lefts[2 * left], lefts[2 * left + 1]
        half, part = own.shape[0], slice(start, start + columns)
        total = lax.dot_general(own[...], right_ref[:half, part], rows, preferred_element_type=f32)
        total += lax.dot_general(got[...], right_ref[half:, part], rows, preferred_element_type=f32)
        out_ref[:, column : column + columns] = total.astype(bf16)
        column += columns


def token_terms(lefts, rights):
    tokens, width = lefts[0][0].shape
    tile = 512
    columns = sum(right[3] for right in rights)
    side = pl.BlockSpec((tokens, tile), lambda i: (0, i))
    arrays = [right[1] for right in rights]
    plan = [(right[0], right[2], right[3]) for right in rights]
    return pl.pallas_call(
        functools.partial(token_terms_kernel, plan),
        grid=(width // tile,),
        in_specs=[side] * (2 * len(lefts))
        + [pl.BlockSpec(array.shape, lambda i: (0, 0)) for array in arrays],
        out_specs=pl.BlockSpec((tile, columns), lambda i: (i, 0)),
        out_shape=jax.ShapeDtypeStruct((width, columns), bf16),
        compiler_params=params(),
        cost_estimate=cost(
            4 * tokens * width * columns,
            2 * (width * columns + 2 * tokens * width * len(lefts) + 2 * tokens * columns),
        ),
        name="token_terms",
    )(*(array for pair in lefts for array in pair), *arrays)


def attention_terms_kernel(normed_ref, mid_grad_ref, grads_ref, mixed_ref, out_ref):
    n_grads = grads_ref.shape[1]
    half = out_ref.shape[1]
    rows = (((0,), (0,)), ((), ()))
    inner = lax.dot_general(normed_ref[...], grads_ref[...], rows, preferred_element_type=f32)
    outer = lax.dot_general(mid_grad_ref[...], mixed_ref[...], rows, preferred_element_type=f32)
    for part in range(2):
        part_rows = slice(part * half, (part + 1) * half)
        out_ref[part, :, :n_grads] = inner[part_rows].astype(bf16)
        out_ref[part, :, n_grads:] = outer[part_rows].astype(bf16)


def attention_terms(normed, mid_grad, grads, mixed, count):
    tokens, width = normed.shape
    columns = grads.shape[1] + mixed.shape[1]
    tile = width // count
    return pl.pallas_call(
        attention_terms_kernel,
        grid=(count,),
        in_specs=[
            pl.BlockSpec((tokens, tile), lambda i: (0, i)),
            pl.BlockSpec((tokens, tile), lambda i: (0, i)),
            pl.BlockSpec((tokens, grads.shape[1]), lambda i: (0, 0)),
            pl.BlockSpec((tokens, mixed.shape[1]), lambda i: (0, 0)),
        ],
        out_specs=pl.BlockSpec((2, None, tile // 2, columns), lambda i: (0, i, 0, 0)),
        out_shape=jax.ShapeDtypeStruct((2, count, tile // 2, columns), bf16),
        compiler_params=params(),
        cost_estimate=pl.CostEstimate(
            flops=2 * tokens * width * columns,
            bytes_accessed=2 * (width * columns + 2 * tokens * width + tokens * columns),
            transcendentals=0,
        ),
        name="attention_terms",
    )(normed, mid_grad, grads, mixed)


def section_stacks_kernel(core_ref, *refs):
    first = core_ref[0] == 0
    for sources, target in ((refs[:4], refs[8]), (refs[4:8], refs[9])):
        low, high, got_low, got_high = (source[...] for source in sources)
        keep, got = jnp.where(first, low, high), jnp.where(first, got_low, got_high)
        target[...] = jnp.where(core_ref[0] == pl.program_id(0), keep, got)


def section_stacks(core, *sources):
    rows, width = sources[0].shape
    block = pl.BlockSpec((rows, width), lambda i, core: (0, 0))
    return pl.pallas_call(
        section_stacks_kernel,
        grid_spec=pltpu.PrefetchScalarGridSpec(
            num_scalar_prefetch=1,
            grid=(2,),
            in_specs=[block] * 8,
            out_specs=[pl.BlockSpec((None, rows, width), lambda i, core: (i, 0, 0))] * 2,
        ),
        out_shape=[jax.ShapeDtypeStruct((2, rows, width), bf16)] * 2,
        compiler_params=params(40),
        cost_estimate=cost(0, 12 * rows * width * 2),
        name="section_stacks",
    )(core.reshape(1), *sources)


def attention_outputs_kernel(core_ref, low_ref, high_ref, got_ref, query_ref, key_ref, value_ref, out_ref):
    first = core_ref[0] == 0
    keep = jnp.where(first, low_ref[...], high_ref[...])
    got = got_ref[...]
    parts = [jnp.where(first == (side == 0), keep, got).astype(f32) for side in range(2)]
    whole = jnp.concatenate(parts, axis=0)
    column = 0
    for ref in (query_ref, key_ref, value_ref):
        ref[...] = whole[:, column : column + ref.shape[1]]
        column += ref.shape[1]
    out_ref[...] = whole[:, column:].T


def attention_outputs(core, low, high, got, sizes):
    n_query, n_key = sizes
    rows, columns = got.shape
    whole = lambda *shape: pl.BlockSpec(shape, lambda i, core: (0, 0))
    shapes = [(2 * rows, n_query), (2 * rows, n_key), (2 * rows, n_key), (n_query, 2 * rows)]
    return pl.pallas_call(
        attention_outputs_kernel,
        grid_spec=pltpu.PrefetchScalarGridSpec(
            num_scalar_prefetch=1,
            grid=(1,),
            in_specs=[whole(rows, columns)] * 3,
            out_specs=[whole(*shape) for shape in shapes],
        ),
        out_shape=[jax.ShapeDtypeStruct(shape, f32) for shape in shapes],
        compiler_params=params(),
        cost_estimate=cost(0, rows * columns * 14),
        name="attention_outputs",
    )(core.reshape(1), low, high, got)


def wide_outputs_kernel(columns, core_ref, *refs):
    first = core_ref[0] == 0
    gate_ref, up_ref = refs[8:]
    sections = []
    for place in range(4):
        early, late = refs[place][...], refs[4 + place][...]
        head = columns[place % 2]
        rest = gate_ref.shape[1] // 2 - head
        gate = jnp.concatenate([early, late[:, :rest]], axis=1)
        sections.append((gate, late[:, rest:]))
    low, high, got_low, got_high = sections
    for target, part in ((gate_ref, 0), (up_ref, 1)):
        units = target.shape[1] // 2
        keep = jnp.where(first, low[part], high[part])
        got = jnp.where(first, got_low[part], got_high[part])
        target[:, :units] = jnp.where(first, keep, got).astype(f32)
        target[:, units:] = jnp.where(first, got, keep).astype(f32)


def wide_outputs(core, early, late, units):
    rows = early[0].shape[0]
    columns = [share.shape[1] - units for share in early[:2]]
    tile = 128

    def early_spec(head):
        return pl.BlockSpec((tile, head), lambda i, core: (i, units // head))

    return pl.pallas_call(
        functools.partial(wide_outputs_kernel, columns),
        grid_spec=pltpu.PrefetchScalarGridSpec(
            num_scalar_prefetch=1,
            grid=(rows // tile,),
            in_specs=[early_spec(head) for head in columns * 2]
            + [pl.BlockSpec((tile, share.shape[1]), lambda i, core: (i, 0)) for share in late],
            out_specs=[pl.BlockSpec((tile, 2 * units), lambda i, core: (i, 0))] * 2,
        ),
        out_shape=[jax.ShapeDtypeStruct((rows, 2 * units), f32)] * 2,
        compiler_params=params(),
        cost_estimate=cost(0, rows * 32 * units),
        name="wide_outputs",
    )(core.reshape(1), *early, *late)


def down_outputs_kernel(core_ref, low_ref, high_ref, got_low_ref, got_high_ref, down_ref):
    first = core_ref[0] == 0
    units = low_ref.shape[1]
    keep = jnp.where(first, low_ref[...], high_ref[...])
    got = jnp.where(first, got_low_ref[...], got_high_ref[...])
    for side in range(2):
        part = jnp.where(first == (side == 0), keep, got).astype(f32)
        down_ref[side * units : (side + 1) * units, :] = part.T


def down_outputs(core, early, units):
    rows = early[0].shape[0]
    tile = 128
    return pl.pallas_call(
        down_outputs_kernel,
        grid_spec=pltpu.PrefetchScalarGridSpec(
            num_scalar_prefetch=1,
            grid=(rows // tile,),
            in_specs=[pl.BlockSpec((tile, units), lambda i, core: (i, 0))] * 4,
            out_specs=pl.BlockSpec((2 * units, tile), lambda i, core: (0, i)),
        ),
        out_shape=jax.ShapeDtypeStruct((2 * units, rows), f32),
        compiler_params=params(),
        cost_estimate=cost(0, rows * units * 16),
        name="down_outputs",
    )(core.reshape(1), *early)


def pin(value, *others):
    return lax.optimization_barrier((value, *others))


def share_gains(terms):
    core, shard = lax.axis_index("pipe"), lax.axis_index("ctx")
    count = lax.axis_size("ctx")
    own = take(terms, core)
    other = take(terms, 1 - core)
    total = own + swap_cores(other)
    blocks = total.reshape(2, count, -1)

    def block(index):
        return take(blocks, index, 1)

    result = block(shard)
    for step in range(1, count):
        route = [(i, i ^ step) for i in range(count)]
        result = result + lax.ppermute(block(shard ^ step), "ctx", route)
    return result


def product(left, right):
    return lax.dot_general(
        left, right, (((1,), (0,)), ((), ())), preferred_element_type=f32
    )


def rows_product(left, right):
    return lax.dot_general(
        left, right, (((0,), (0,)), ((), ())), preferred_element_type=f32
    )


def cols_product(left, right):
    return lax.dot_general(
        left, right, (((1,), (1,)), ((), ())), preferred_element_type=f32
    )


def norm_forward(stream, gain_vector):
    inv_rms = lax.rsqrt(jnp.mean(stream * stream, axis=-1) + epsilon)
    return ((stream * inv_rms[:, None] * gain_vector[None, :]).astype(bf16), inv_rms)


def norm_backward(stream, inv_rms, gain_vector, upstream):
    weighted = upstream * gain_vector[None, :]
    gain_grad = jnp.sum(upstream * stream * inv_rms[:, None], axis=0)
    inner_mean = jnp.mean(stream * weighted, axis=-1)
    stream_grad = (
        weighted * inv_rms[:, None] - stream * (inv_rms * inv_rms * inv_rms * inner_mean)[:, None]
    )
    return (stream_grad, gain_grad)


def sum_tensor(partial, *others):
    partial = partial.astype(bf16)
    if others:
        partial, *others = pin(partial, *others)
    return lax.psum(partial, "tensor"), *others


def own_share(partial, rows):
    arrived = swap_cores(partial[rows:].astype(bf16))
    return partial[:rows] + arrived.astype(f32)


def half_swap(values):
    lanes = lax.broadcasted_iota(jnp.int32, values.shape, 1)
    count = values.shape[1]
    quarter = HEAD_DIM // 2
    return jnp.where(
        lanes % HEAD_DIM < quarter,
        pltpu.roll(values, count - quarter, 1),
        pltpu.roll(values, quarter, 1),
    )


def wide_table(table, columns):
    return jnp.concatenate([table] * (columns // table.shape[1]), axis=1)


def rope_tables(positions_row, width):
    frequency = jnp.exp(
        jnp.arange(width // 2, dtype=f32) * (-2.0 * math.log(rope_base) / width)
    )
    angles = positions_row.astype(f32)[:, None] * frequency[None, :]
    cosine, sine = jnp.cos(angles), jnp.sin(angles)
    return (
        jnp.concatenate([cosine] * 4, axis=1),
        jnp.concatenate([-sine, sine] * 2, axis=1),
    )


def head_inputs_kernel(sizes, stream_ref, gain_ref, wide_ref, cos_ref, sin_ref,
                       normed_ref, rms_ref, query_ref, own_ref):
    n_query, n_key = sizes
    stream = stream_ref[...].astype(f32)
    inv_rms = lax.rsqrt(jnp.mean(stream * stream, axis=1, keepdims=True) + epsilon)
    normed = (stream * inv_rms * gain_ref[...]).astype(bf16)
    normed_ref[...] = normed
    rms_ref[...] = inv_rms
    raw = jnp.dot(normed, wide_ref[...], preferred_element_type=f32)
    turned = raw[:, : n_query + n_key]
    cosine = wide_table(cos_ref[...], n_query + n_key)
    sine = wide_table(sin_ref[...], n_query + n_key)
    turned = turned * cosine + half_swap(turned) * sine
    query_ref[...] = turned[:, :n_query].astype(bf16)
    own_ref[:, :n_key] = turned[:, n_query:].astype(bf16)
    own_ref[:, n_key:] = raw[:, n_query + n_key :].astype(bf16)


def head_inputs(stream, gain, wide, tables, sizes):
    n_query, n_key = sizes
    rows, width = stream.shape
    columns = n_query + 2 * n_key
    whole = lambda *shape: pl.BlockSpec(shape, lambda i: (0,) * len(shape))
    return pl.pallas_call(
        functools.partial(head_inputs_kernel, sizes),
        grid=(1,),
        in_specs=[
            whole(rows, width),
            whole(1, width),
            whole(width, columns),
            whole(rows, 2 * HEAD_DIM),
            whole(rows, 2 * HEAD_DIM),
        ],
        out_specs=[whole(rows, width), whole(rows, 1), whole(rows, n_query), whole(rows, 2 * n_key)],
        out_shape=[
            jax.ShapeDtypeStruct((rows, width), bf16),
            jax.ShapeDtypeStruct((rows, 1), f32),
            jax.ShapeDtypeStruct((rows, n_query), bf16),
            jax.ShapeDtypeStruct((rows, 2 * n_key), bf16),
        ],
        compiler_params=params(),
        cost_estimate=cost(2 * rows * width * columns, 2 * width * (columns + 4 * rows)),
        name="head_inputs",
    )(stream, gain[None], wide, *tables)


def masked_scores(query, keys, allowed):
    raw = lax.dot_general(query, keys, (((1,), (1,)), ((), ())), preferred_element_type=f32)
    return jnp.where(allowed, raw * HEAD_DIM ** (-0.5), -1e30)


def allowed_pairs(pos, rows):
    distance = (
        lax.broadcasted_iota(jnp.int32, (rows, 2 * rows), 0)
        - lax.broadcasted_iota(jnp.int32, (rows, 2 * rows), 1)
        + rows
    )
    return (distance >= 0) & (distance <= pos)


def head_slice(index):
    return slice(index * HEAD_DIM, (index + 1) * HEAD_DIM)


def mix_kernel(n_key, pos_ref, query_ref, tail_ref, own_ref, wide_ref,
               mixed_ref, log_ref, partial_ref, window, mixed_all):
    rows, n_query = query_ref.shape

    @pl.when(pl.program_id(0) == 0)
    def _():
        window[:rows] = tail_ref[...]
        window[rows:] = own_ref[...]
        allowed = allowed_pairs(pos_ref[...], rows)
        group = HEADS // KV_HEADS
        logs, mixed = [], []
        for head in range(n_query // HEAD_DIM):
            keys = window[:, head_slice(head // group)]
            values = window[:, head_slice((n_key // HEAD_DIM) + head // group)]
            masked = masked_scores(query_ref[:, head_slice(head)], keys, allowed)
            top = jnp.max(masked, axis=1, keepdims=True)
            exponent = jnp.exp(masked - top)
            total = jnp.sum(exponent, axis=1, keepdims=True)
            weights = (exponent * (1.0 / total)).astype(bf16)
            mixed.append(jnp.dot(weights, values, preferred_element_type=f32).astype(bf16))
            logs.append(top + jnp.log(total))
        everything = jnp.concatenate(mixed, axis=1)
        mixed_all[...] = everything
        mixed_ref[...] = everything
        log_ref[...] = jnp.concatenate(logs, axis=1)

    partial_ref[...] = lax.dot_general(
        mixed_all[...],
        wide_ref[...],
        (((1,), (1,)), ((), ())),
        preferred_element_type=f32,
    ).astype(bf16)


def mix(pos, queries, tail, own, wide, n_key):
    rows, n_query = queries.shape
    width, columns = wide.shape
    tile = 512
    heads = n_query // HEAD_DIM
    whole = lambda *shape: pl.BlockSpec(shape, lambda i: (0,) * len(shape))
    return pl.pallas_call(
        functools.partial(mix_kernel, n_key),
        grid=(width // tile,),
        in_specs=[
            whole(rows, 1),
            whole(rows, n_query),
            whole(rows, 2 * n_key),
            whole(rows, 2 * n_key),
            pl.BlockSpec((tile, columns), lambda i: (i, 0)),
        ],
        out_specs=[
            whole(rows, n_query),
            whole(rows, heads),
            pl.BlockSpec((rows, tile), lambda i: (0, i)),
        ],
        out_shape=[
            jax.ShapeDtypeStruct((rows, n_query), bf16),
            jax.ShapeDtypeStruct((rows, heads), f32),
            jax.ShapeDtypeStruct((rows, width), bf16),
        ],
        scratch_shapes=[pltpu.VMEM((2 * rows, 2 * n_key), bf16), pltpu.VMEM((rows, n_query), bf16)],
        compiler_params=params(),
        cost_estimate=cost(
            2 * rows * n_query * (width + 4 * rows), 2 * width * (columns + rows), 2 * rows * rows * heads
        ),
        name="mix",
    )(pos, queries, tail, own, wide)


def mix_back_kernel(n_key, pos_ref, query_ref, tail_ref, own_ref, mixed_ref, log_ref, cos_ref, sin_ref,
                    mid_grad_ref, wide_ref, query_grad_ref, back_ref, own_grad_ref, mid_b_ref,
                    window, mixed_grad):
    rows, n_query = query_ref.shape
    step = pl.program_id(0)
    mid_b = mid_grad_ref[...].astype(bf16)
    mid_b_ref[...] = mid_b
    part = jnp.dot(mid_b, wide_ref[...], preferred_element_type=f32)

    @pl.when(step == 0)
    def _():
        mixed_grad[...] = part

    @pl.when(step > 0)
    def _():
        mixed_grad[...] += part

    @pl.when(step == pl.num_programs(0) - 1)
    def _():
        window[:rows] = tail_ref[...]
        window[rows:] = own_ref[...]
        allowed = allowed_pairs(pos_ref[...], rows)
        group = HEADS // KV_HEADS
        groups = n_key // HEAD_DIM
        scale = HEAD_DIM ** (-0.5)
        grads = mixed_grad[...].astype(bf16)
        over_rows = (((0,), (0,)), ((), ()))
        over_columns = (((1,), (1,)), ((), ()))
        query_grads, key_grads, value_grads = [], [None] * groups, [None] * groups
        for head in range(n_query // HEAD_DIM):
            at = head // group
            keys = window[:, head_slice(at)]
            values = window[:, head_slice(groups + at)]
            query = query_ref[:, head_slice(head)]
            grad = grads[:, head_slice(head)]
            masked = masked_scores(query, keys, allowed)
            prob = jnp.exp(masked - log_ref[:, head : head + 1])
            prob_grad = lax.dot_general(grad, values, over_columns, preferred_element_type=f32)
            delta = jnp.sum(
                grad.astype(f32) * mixed_ref[:, head_slice(head)].astype(f32), axis=1, keepdims=True
            )
            score_grad = (prob * (prob_grad - delta)).astype(bf16)
            query_grads.append(jnp.dot(score_grad, keys, preferred_element_type=f32))
            key_part = lax.dot_general(score_grad, query, over_rows, preferred_element_type=f32)
            value_part = lax.dot_general(
                prob.astype(bf16), grad, over_rows, preferred_element_type=f32
            )
            key_grads[at] = key_part if key_grads[at] is None else key_grads[at] + key_part
            value_grads[at] = value_part if value_grads[at] is None else value_grads[at] + value_part
        query_grad = jnp.concatenate(query_grads, axis=1) * scale
        query_grad = query_grad * wide_table(cos_ref[...], n_query) - half_swap(
            query_grad
        ) * wide_table(sin_ref[...], n_query)
        query_grad_ref[...] = query_grad.astype(bf16)
        key_grad = jnp.concatenate(key_grads, axis=1) * scale
        value_grad = jnp.concatenate(value_grads, axis=1)
        back_ref[:, :n_key] = key_grad[:rows].astype(bf16)
        back_ref[:, n_key:] = value_grad[:rows].astype(bf16)
        own_grad_ref[:, :n_key] = key_grad[rows:]
        own_grad_ref[:, n_key:] = value_grad[rows:]


def mix_back(pos, queries, tail, own, mixed, logs, tables, mid_grad, wide, n_key):
    rows, n_query = queries.shape
    width, columns = wide.shape
    tile = 512
    heads = n_query // HEAD_DIM
    whole = lambda *shape: pl.BlockSpec(shape, lambda i: (0,) * len(shape))
    return pl.pallas_call(
        functools.partial(mix_back_kernel, n_key),
        grid=(width // tile,),
        in_specs=[
            whole(rows, 1),
            whole(rows, n_query),
            whole(rows, 2 * n_key),
            whole(rows, 2 * n_key),
            whole(rows, n_query),
            whole(rows, heads),
            whole(rows, 2 * HEAD_DIM),
            whole(rows, 2 * HEAD_DIM),
            pl.BlockSpec((rows, tile), lambda i: (0, i)),
            pl.BlockSpec((tile, columns), lambda i: (i, 0)),
        ],
        out_specs=[
            whole(rows, n_query),
            whole(rows, 2 * n_key),
            whole(rows, 2 * n_key),
            pl.BlockSpec((rows, tile), lambda i: (0, i)),
        ],
        out_shape=[
            jax.ShapeDtypeStruct((rows, n_query), bf16),
            jax.ShapeDtypeStruct((rows, 2 * n_key), bf16),
            jax.ShapeDtypeStruct((rows, 2 * n_key), f32),
            jax.ShapeDtypeStruct((rows, width), bf16),
        ],
        scratch_shapes=[pltpu.VMEM((2 * rows, 2 * n_key), bf16), pltpu.VMEM((rows, n_query), f32)],
        compiler_params=params(),
        cost_estimate=cost(
            2 * rows * n_query * (width + 10 * rows), 2 * width * (columns + 3 * rows), 2 * rows * rows * heads
        ),
        name="mix_back",
    )(pos, queries, tail, own, mixed, logs, *tables, mid_grad, wide)


def head_grads_kernel(n_key, query_grad_ref, own_grad_ref, back_ref, cos_ref, sin_ref, wide_ref,
                      grads_ref, partial_ref, grads):
    n_query = query_grad_ref.shape[1]

    @pl.when(pl.program_id(0) == 0)
    def _():
        own = own_grad_ref[...] + back_ref[...].astype(f32)
        keys = own[:, :n_key]
        keys = keys * wide_table(cos_ref[...], n_key) - half_swap(keys) * wide_table(
            sin_ref[...], n_key
        )
        grads[:, :n_query] = query_grad_ref[...]
        grads[:, n_query : n_query + n_key] = keys.astype(bf16)
        grads[:, n_query + n_key :] = own[:, n_key:].astype(bf16)
        grads_ref[...] = grads[...]

    partial_ref[...] = lax.dot_general(
        grads[...], wide_ref[...], (((1,), (1,)), ((), ())), preferred_element_type=f32
    ).astype(bf16)


def head_grads(query_grad, own_grad, back, tables, wide, n_key):
    rows, n_query = query_grad.shape
    width = wide.shape[0]
    columns = n_query + 2 * n_key
    tile = 512
    whole = lambda *shape: pl.BlockSpec(shape, lambda i: (0,) * len(shape))
    return pl.pallas_call(
        functools.partial(head_grads_kernel, n_key),
        grid=(width // tile,),
        in_specs=[
            whole(rows, n_query),
            whole(rows, 2 * n_key),
            whole(rows, 2 * n_key),
            whole(rows, 2 * HEAD_DIM),
            whole(rows, 2 * HEAD_DIM),
            pl.BlockSpec((tile, columns), lambda i: (i, 0)),
        ],
        out_specs=[whole(rows, columns), pl.BlockSpec((rows, tile), lambda i: (0, i))],
        out_shape=[
            jax.ShapeDtypeStruct((rows, columns), bf16),
            jax.ShapeDtypeStruct((rows, width), bf16),
        ],
        scratch_shapes=[pltpu.VMEM((rows, columns), bf16)],
        compiler_params=params(),
        cost_estimate=cost(2 * rows * width * columns, 2 * width * (columns + rows)),
        name="head_grads",
    )(query_grad, own_grad, back, *tables, wide)


def attention_forward(stream, gain, wide, place, *others):
    pos, tables, sizes = place
    normed, inv_rms, queries, own = head_inputs(stream, gain, wide[0], tables, sizes)
    tail = from_behind(own, "ctx", 1)
    mixed, logs, partial = mix(pos, queries, tail, own, wide[1], sizes[1])
    total, *others = sum_tensor(partial, *others)
    return total, (stream.astype(f32), inv_rms[:, 0], normed, queries, tail, own, mixed, logs), *others


def ffn_forward_in(middle, gain, wides, hidden_width):
    normed, inv_rms = norm_forward(middle, gain)
    got = swap_cores(normed)
    both = jnp.concatenate([normed, got], axis=0)
    gate_up = [product(both, wide) for wide in wides]
    gate = gate_up[0][:, :hidden_width]
    up = jnp.concatenate([gate_up[0][:, hidden_width:], *gate_up[1:]], axis=1)
    hidden = (jax.nn.silu(gate) * up).astype(bf16)
    return (middle, inv_rms, normed, got, gate, up, hidden)


def ffn_share(state, down):
    middle, hidden = state[0], state[-1]
    return own_share(cols_product(hidden, down), middle.shape[0]).astype(bf16)


def ffn_backward(own_grad, other_grad, state, wide, down, head, *others):
    middle, _, normed, got, gate, up, hidden = state
    hidden_grad = product(jnp.concatenate([own_grad, other_grad], axis=0), down)
    sigmoid_gate = jax.nn.sigmoid(gate)
    gate_grad = (hidden_grad * up * sigmoid_gate * (1.0 + gate * (1.0 - sigmoid_gate))).astype(bf16)
    up_grad = (hidden_grad * gate * sigmoid_gate).astype(bf16)
    units = gate.shape[1]
    partial = cols_product(jnp.concatenate([gate_grad, up_grad], axis=1), wide)
    normed_grad, *others = sum_tensor(own_share(partial, middle.shape[0]), *others)
    own_sides, norm_sides = (own_grad, other_grad), (normed, got)
    early = token_terms([own_sides, norm_sides], [(0, hidden, 0, units), (1, gate_grad, 0, head)])
    early = lax.psum_scatter(early, "ctx", scatter_dimension=0, tiled=True)
    late = token_terms([norm_sides], [(0, gate_grad, head, units - head), (0, up_grad, 0, units)])
    return normed_grad, early, late, *others


def ffn_backward_out(upstream, normed_grad, state, gain):
    mid_part, gain_term = norm_backward(state[0], state[1], gain, normed_grad.astype(f32))
    return upstream.astype(f32) + mid_part, gain_term


def attention_backward(mid_grad, saved, wide, place, *others):
    pos, tables, sizes = place
    _, _, normed, queries, tail, own, mixed, logs = saved
    query_grad, back, own_grad, mid_grad_b = mix_back(
        pos, queries, tail, own, mixed, logs, tables, mid_grad, wide[1], sizes[1]
    )
    back = from_behind(back, "ctx", -1)
    grads, partial = head_grads(query_grad, own_grad, back, tables, wide[0], sizes[1])
    normed_grad, *others = sum_tensor(partial, *others)
    terms = attention_terms(normed, mid_grad_b, grads, mixed, lax.axis_size("ctx"))
    core = lax.axis_index("pipe")
    mine = take(terms, core)
    theirs = take(terms, 1 - core)
    return normed_grad, add_bf16(mine, swap_cores(theirs)), *others


def attention_backward_out(mid_grad, normed_grad, saved, gain):
    part, gain_term = norm_backward(saved[0], saved[1], gain, normed_grad.astype(f32))
    return (mid_grad + part).astype(bf16), gain_term


def on_device(
    inputs,
    out_grad,
    positions,
    attn_gain,
    w_query,
    w_key,
    w_value,
    w_out,
    ffn_gain,
    w_gate,
    w_up,
    w_down,
):
    core = lax.axis_index("pipe")
    first = core == 0
    shard = lax.axis_index("ctx")
    rows = inputs.shape[1]
    width = inputs.shape[2]
    n_query = w_query.shape[2]
    n_key = w_key.shape[2]
    half = w_gate.shape[2] // 2

    def pick(pair, index):
        return take(pair, index)

    def mine_theirs(array, axis):
        size = array.shape[axis] // 2
        mine = lax.dynamic_slice_in_dim(
            array, core * size, size, axis, allow_negative_indices=False
        )
        theirs = lax.dynamic_slice_in_dim(
            array, (1 - core) * size, size, axis, allow_negative_indices=False
        )
        return mine, theirs

    count = lax.axis_size("ctx")
    gain_row = jnp.concatenate([attn_gain, ffn_gain], axis=1)
    attn_shard = jnp.concatenate([w_query[0], w_key[0], w_value[0], w_out[0].T], axis=1)
    wide_columns = attn_shard.shape[1]
    gain_rows = jnp.pad(gain_row, ((0, 15), (0, wide_columns - gain_row.shape[1])))
    rows_mine, rows_theirs = mine_theirs(attn_shard, 0)
    attn_keep = jnp.concatenate([rows_mine, gain_rows], axis=0)
    attn_got = swap_cores(jnp.concatenate([rows_theirs, gain_rows], axis=0))

    inner_columns = n_query + 2 * n_key

    def attn_weights(pieces):
        got = swap_cores(pieces)
        both = jnp.stack([jnp.where(first, pieces, got), jnp.where(first, got, pieces)], axis=1)
        part_rows = attn_shard.shape[0] // 2
        wide = both[:, :, :part_rows].reshape(width, wide_columns)
        wide = (wide[:, :inner_columns], wide[:, inner_columns:])
        row = pieces[:, part_rows, : gain_row.shape[1]].astype(f32)
        return wide, row.reshape(count, 2, -1).transpose(1, 0, 2).reshape(2, width)

    gate_mine, gate_theirs = mine_theirs(w_gate[0], 1)
    up_mine, up_theirs = mine_theirs(w_up[0], 1)
    wide_keep = jnp.concatenate([gate_mine, up_mine], axis=1)
    wide_got = swap_cores(jnp.concatenate([gate_theirs, up_theirs], axis=1))
    down_mine, down_theirs = mine_theirs(w_down[0], 0)
    down_keep, down_got = down_mine.T, swap_cores(down_theirs.T)

    def for_sections(keep, got):
        return [jnp.where(first, keep, got), jnp.where(first, got, keep)]

    def gather(shard_part):
        return lax.all_gather(shard_part, "ctx", axis=0, tiled=True)

    attn_parts = for_sections(attn_keep, attn_got)
    wide_parts = for_sections(wide_keep, wide_got)
    down_parts = for_sections(down_keep, down_got)
    tail_columns = half // 4
    wide_low = lax.all_gather(
        wide_parts[0][:, :-tail_columns], ("pipe", "ctx"), axis=0, tiled=True
    )
    down_parts[0] = jnp.concatenate([down_parts[0], wide_parts[0][:, -tail_columns:]], axis=1)
    attn_pieces, attn_parts[1], wide_parts[1], *down_parts = pin(
        ring_gather(*ring_gather_start(attn_parts[0])), attn_parts[1], wide_parts[1], *down_parts
    )
    attn_low, gains_low = attn_weights(attn_pieces)
    down_and_tail = gather(down_parts[0])
    ring_columns = wide_parts[1].shape[1] // 4
    wide_high = gather(wide_parts[1][:, :-ring_columns])
    down_high = gather(down_parts[1])

    pos_row = pick(positions, core)
    place = (pos_row[:, None], rope_tables(pos_row, HEAD_DIM), (n_query, n_key))

    def scatter(terms):
        return lax.psum_scatter(terms, "ctx", scatter_dimension=0, tiled=True)

    def give_low(share):
        return lax.ppermute(share, "pipe", [(1, 0)])

    def give_high(share):
        return lax.ppermute(share, "pipe", [(0, 1)])

    stream = pick(inputs, core)
    total, attn_saved_low, wide_low, attn_part_high = attention_forward(
        stream, gains_low[0], attn_low, place, wide_low, attn_parts[1]
    )
    wide_low = pick(wide_low.reshape(2, width, -1), core)
    total, wide_low, attn_ring = pin(total, wide_low, ring_gather_start(attn_part_high))
    middle = attn_saved_low[0] + total.astype(f32)
    down_low, wide_tail = down_and_tail[:, :half], down_and_tail[:, half:]
    state_low = ffn_forward_in(middle, gains_low[1], [wide_low, wide_tail], half)
    own_grad, other_grad = pick(out_grad, core), pick(out_grad, 1 - core)
    (total,) = sum_tensor(ffn_share(state_low, down_low))
    wide_low = jnp.concatenate([wide_low, wide_tail], axis=1)
    total, own_grad, other_grad, (attn_high, gains_high), wide_low = pin(
        total, own_grad, other_grad, attn_weights(ring_gather(*attn_ring)), wide_low
    )
    out_low = (middle + total.astype(f32)).astype(bf16)
    total, attn_saved_high, wide_high, wide_part_high = attention_forward(
        out_low, gains_high[0], attn_high, place, wide_high, wide_parts[1][:, -ring_columns:]
    )
    wide_ring = ring_gather_start(wide_part_high)
    wide_high = jnp.concatenate(
        [wide_high, ring_gather(*wide_ring).reshape(width, ring_columns)], axis=1
    )
    total, got_out_low, wide_high = pin(total, swap_cores(out_low), wide_high)
    middle = attn_saved_high[0] + total.astype(f32)
    state_high = ffn_forward_in(middle, gains_high[1], [wide_high], half)

    normed_grad, early_high, late_high = ffn_backward(
        own_grad, other_grad, state_high, wide_high, down_high, half // 2
    )
    normed_grad, late_high = pin(normed_grad, late_high)
    mid_grad, ffn_gain_high = ffn_backward_out(own_grad, normed_grad, state_high, gains_high[1])
    late_high = scatter(late_high)
    normed_grad, summed, early_high = attention_backward(
        mid_grad, attn_saved_high, attn_high, place, early_high
    )
    normed_grad, attn_ring, out_share = pin(
        normed_grad, ring_scatter_start(summed), ffn_share(state_high, down_high)
    )
    boundary_high, attn_gain_high = attention_backward_out(
        mid_grad, normed_grad, attn_saved_high, gains_high[0]
    )
    got_boundary_high = swap_cores(boundary_high)
    normed_grad, early_low, late_low, late_high = ffn_backward(
        boundary_high, got_boundary_high, state_low, wide_low, down_low, half // 4, late_high
    )
    normed_grad, late_low, attn_share_high = pin(normed_grad, late_low, ring_scatter(*attn_ring))
    mid_grad, ffn_gain_low = ffn_backward_out(
        boundary_high, normed_grad, state_low, gains_low[1]
    )
    late_low = scatter(late_low)
    normed_grad, summed, early_low = attention_backward(
        mid_grad, attn_saved_low, attn_low, place, early_low
    )
    def from_other(low, high):
        return swap_cores(jnp.where(first, high, low))

    (total,) = sum_tensor(out_share)
    attn_pair = (ring_scatter(*ring_scatter_start(summed)), attn_share_high)
    attn_outs = attention_outputs(core, *attn_pair, from_other(*attn_pair), (n_query, n_key))
    early = (early_low, early_high, give_low(early_low), give_high(early_high))
    down_out = down_outputs(core, early, half)
    normed_grad, down_out, attn_outs, got_late_high = pin(
        normed_grad, down_out, attn_outs, give_high(late_high)
    )
    out_high = (middle + total.astype(f32)).astype(bf16)

    boundary_low, attn_gain_low = attention_backward_out(
        mid_grad, normed_grad, attn_saved_low, gains_low[0]
    )
    gains_out = share_gains(
        jnp.stack(
            [jnp.stack([attn_gain_low, ffn_gain_low]), jnp.stack([attn_gain_high, ffn_gain_high])]
        )
    )
    late_low, gains_out, got_out_high, got_boundary_low = pin(
        late_low, gains_out, swap_cores(out_high), swap_cores(boundary_low)
    )
    outs = (out_low, out_high, got_out_low, got_out_high)
    boundaries = (boundary_low, boundary_high, got_boundary_low, got_boundary_high)
    section_outputs, boundary_grads = section_stacks(core, *outs, *boundaries)
    late = (late_low, late_high, give_low(late_low), got_late_high)
    gate_out, up_out = wide_outputs(core, early, late, half)
    query_out, key_out, value_out, attn_out = attn_outs
    return (
        section_outputs[None],
        boundary_grads[None],
        gains_out[:1],
        query_out[None],
        key_out[None],
        value_out[None],
        attn_out[None],
        gains_out[1:],
        gate_out[None],
        up_out[None],
        down_out[None],
    )


def solution(mesh):
    in_specs = (
        P(None, "ctx", None),
        P(None, "ctx", None),
        P(None, "ctx"),
        P("pipe", "ctx"),
        P("pipe", "ctx", "tensor"),
        P("pipe", "ctx", "tensor"),
        P("pipe", "ctx", "tensor"),
        P("pipe", "tensor", "ctx"),
        P("pipe", "ctx"),
        P("pipe", "ctx", "tensor"),
        P("pipe", "ctx", "tensor"),
        P("pipe", "tensor", "ctx"),
    )
    out_specs = (
        P("pipe", None, "ctx", None),
        P("pipe", None, "ctx", None),
        P("pipe", "ctx"),
        P("pipe", "ctx", "tensor"),
        P("pipe", "ctx", "tensor"),
        P("pipe", "ctx", "tensor"),
        P("pipe", "tensor", "ctx"),
        P("pipe", "ctx"),
        P("pipe", "ctx", "tensor"),
        P("pipe", "ctx", "tensor"),
        P("pipe", "tensor", "ctx"),
    )
    return jax.shard_map(
        on_device, mesh=mesh, in_specs=in_specs, out_specs=out_specs, check_vma=False
    )
```

```python
import functools
import math

import jax
import jax.numpy as jnp
from jax import lax
from jax.experimental import pallas as pl
from jax.experimental.pallas import tpu as pltpu
from jax.sharding import PartitionSpec as P

HEADS = 32
KV_HEADS = 8
HEAD_DIM = 64
MAXLEN = 256

epsilon = 1e-05
rope_base = 500000.0
bf16 = jnp.bfloat16
f32 = jnp.float32


def swap_cores(block):
    return lax.ppermute(block, "pipe", [(0, 1), (1, 0)])


def from_behind(block, axis, distance):
    devices = range(lax.axis_size(axis))
    route = [(i - distance, i) for i in devices if i - distance in devices]
    return lax.ppermute(block, axis, route)


def ring_order(count):
    across = 1 << (count.bit_length() - 1) // 2
    down = count // across
    walk = [(0, x) for x in range(across)]
    for y in range(1, down):
        columns = range(1, across)
        walk += [(y, x) for x in (columns if y % 2 == 0 else reversed(columns))]
    walk += [(y, 0) for y in range(down - 1, 0, -1)]
    return [y * across + x for y, x in walk]


def take(array, index, axis=0):
    return lax.dynamic_index_in_dim(
        array, index, axis, keepdims=False, allow_negative_indices=False
    )


def ring_tools():
    count = lax.axis_size("ctx")
    order = ring_order(count)
    ahead = [(order[i], order[(i + 1) % count]) for i in range(count)]
    behind = [(b, a) for a, b in ahead]
    device = lax.axis_index("ctx")

    def device_at(distance):
        if order == [0, 1, 3, 2]:
            place = ((device ^ (device >> 1)) + distance % count) & 3
            return place ^ (place >> 1)
        place = jnp.asarray([order.index(i) for i in range(count)], jnp.int32)
        return take(jnp.asarray(order * 2, jnp.int32), take(place, device) + distance % count)

    return count, ahead, behind, device_at


def ring_gather_start(block):
    count, ahead, behind, _ = ring_tools()
    from_back, from_front = [block], [block]
    for _ in range(1, count // 2):
        from_back.append(lax.ppermute(from_back[-1], "ctx", ahead))
        from_front.append(lax.ppermute(from_front[-1], "ctx", behind))
    return from_back, from_front


def ring_gather(from_back, from_front):
    count, ahead, behind, device_at = ring_tools()
    block = from_back[0]
    half = block.shape[1] // 2
    left = lax.ppermute(from_back[-1][:, :half], "ctx", ahead)
    right = lax.ppermute(from_front[-1][:, half:], "ctx", behind)
    out = jnp.zeros((count,) + block.shape, block.dtype)

    def put(out, piece, distance, column=0):
        return lax.dynamic_update_slice(
            out, piece[None], (device_at(distance), 0, column), allow_negative_indices=False
        )

    out = put(out, block, 0)
    for distance in range(1, count // 2):
        out = put(out, from_back[distance], -distance)
        out = put(out, from_front[distance], distance)
    out = put(out, left, count // 2)
    return put(out, right, count // 2, half)


def ring_term(terms, distance):
    return take(terms, ring_tools()[3](distance))


def ring_scatter_start(terms):
    count, ahead, behind, _ = ring_tools()
    half = terms.shape[2] // 2
    far = ring_term(terms, count // 2)
    to_front = lax.ppermute(far[:, :half], "ctx", ahead)
    to_back = lax.ppermute(far[:, half:], "ctx", behind)
    for distance in range(count // 2 - 1, 0, -1):
        front, back = ring_term(terms, distance), ring_term(terms, -distance)
        if distance == count // 2 - 1:
            front = jnp.concatenate([add_bf16(front[:, :half], to_front), front[:, half:]], axis=1)
            back = jnp.concatenate([back[:, :half], add_bf16(back[:, half:], to_back)], axis=1)
        else:
            front, back = add_bf16(front, to_front), add_bf16(back, to_back)
        if distance > 1:
            front = lax.ppermute(front, "ctx", ahead)
            back = lax.ppermute(back, "ctx", behind)
        to_front, to_back = front, back
    return ring_term(terms, 0), to_front, to_back


def ring_scatter(own, to_front, to_back):
    _, ahead, behind, _ = ring_tools()
    from_back = lax.ppermute(to_front, "ctx", ahead)
    from_front = lax.ppermute(to_back, "ctx", behind)
    return (own.astype(f32) + from_back.astype(f32) + from_front.astype(f32)).astype(bf16)


def add_bf16(a, b):
    return (a.astype(f32) + b.astype(f32)).astype(bf16)


def params(megabytes=24):
    return pltpu.CompilerParams(vmem_limit_bytes=megabytes * 2**20)


def cost(flops, bytes_accessed, transcendentals=0):
    return pl.CostEstimate(
        flops=flops, bytes_accessed=bytes_accessed, transcendentals=transcendentals
    )


def token_terms_kernel(plan, *refs):
    out_ref = refs[-1]
    lefts, rights = refs[: -1 - len(plan)], refs[-1 - len(plan) : -1]
    rows = (((0,), (0,)), ((), ()))
    column = 0
    for (left, start, columns), right_ref in zip(plan, rights):
        own, got = lefts[2 * left], lefts[2 * left + 1]
        half, part = own.shape[0], slice(start, start + columns)
        total = lax.dot_general(own[...], right_ref[:half, part], rows, preferred_element_type=f32)
        total += lax.dot_general(got[...], right_ref[half:, part], rows, preferred_element_type=f32)
        out_ref[:, column : column + columns] = total.astype(bf16)
        column += columns


def token_terms(lefts, rights):
    tokens, width = lefts[0][0].shape
    tile = 512
    columns = sum(right[3] for right in rights)
    side = pl.BlockSpec((tokens, tile), lambda i: (0, i))
    arrays = [right[1] for right in rights]
    plan = [(right[0], right[2], right[3]) for right in rights]
    return pl.pallas_call(
        functools.partial(token_terms_kernel, plan),
        grid=(width // tile,),
        in_specs=[side] * (2 * len(lefts))
        + [pl.BlockSpec(array.shape, lambda i: (0, 0)) for array in arrays],
        out_specs=pl.BlockSpec((tile, columns), lambda i: (i, 0)),
        out_shape=jax.ShapeDtypeStruct((width, columns), bf16),
        compiler_params=params(),
        cost_estimate=cost(
            4 * tokens * width * columns,
            2 * (width * columns + 2 * tokens * width * len(lefts) + 2 * tokens * columns),
        ),
        name="token_terms",
    )(*(array for pair in lefts for array in pair), *arrays)


def attention_terms_kernel(normed_ref, mid_grad_ref, grads_ref, mixed_ref, out_ref):
    n_grads = grads_ref.shape[1]
    half = out_ref.shape[1]
    rows = (((0,), (0,)), ((), ()))
    inner = lax.dot_general(normed_ref[...], grads_ref[...], rows, preferred_element_type=f32)
    outer = lax.dot_general(mid_grad_ref[...], mixed_ref[...], rows, preferred_element_type=f32)
    for part in range(2):
        part_rows = slice(part * half, (part + 1) * half)
        out_ref[part, :, :n_grads] = inner[part_rows].astype(bf16)
        out_ref[part, :, n_grads:] = outer[part_rows].astype(bf16)


def attention_terms(normed, mid_grad, grads, mixed, count):
    tokens, width = normed.shape
    columns = grads.shape[1] + mixed.shape[1]
    tile = width // count
    return pl.pallas_call(
        attention_terms_kernel,
        grid=(count,),
        in_specs=[
            pl.BlockSpec((tokens, tile), lambda i: (0, i)),
            pl.BlockSpec((tokens, tile), lambda i: (0, i)),
            pl.BlockSpec((tokens, grads.shape[1]), lambda i: (0, 0)),
            pl.BlockSpec((tokens, mixed.shape[1]), lambda i: (0, 0)),
        ],
        out_specs=pl.BlockSpec((2, None, tile // 2, columns), lambda i: (0, i, 0, 0)),
        out_shape=jax.ShapeDtypeStruct((2, count, tile // 2, columns), bf16),
        compiler_params=params(),
        cost_estimate=pl.CostEstimate(
            flops=2 * tokens * width * columns,
            bytes_accessed=2 * (width * columns + 2 * tokens * width + tokens * columns),
            transcendentals=0,
        ),
        name="attention_terms",
    )(normed, mid_grad, grads, mixed)


def section_stacks_kernel(core_ref, *refs):
    first = core_ref[0] == 0
    for sources, target in ((refs[:4], refs[8]), (refs[4:8], refs[9])):
        low, high, got_low, got_high = (source[...] for source in sources)
        keep, got = jnp.where(first, low, high), jnp.where(first, got_low, got_high)
        target[...] = jnp.where(core_ref[0] == pl.program_id(0), keep, got)


def section_stacks(core, *sources):
    rows, width = sources[0].shape
    block = pl.BlockSpec((rows, width), lambda i, core: (0, 0))
    return pl.pallas_call(
        section_stacks_kernel,
        grid_spec=pltpu.PrefetchScalarGridSpec(
            num_scalar_prefetch=1,
            grid=(2,),
            in_specs=[block] * 8,
            out_specs=[pl.BlockSpec((None, rows, width), lambda i, core: (i, 0, 0))] * 2,
        ),
        out_shape=[jax.ShapeDtypeStruct((2, rows, width), bf16)] * 2,
        compiler_params=params(40),
        cost_estimate=cost(0, 12 * rows * width * 2),
        name="section_stacks",
    )(core.reshape(1), *sources)


def attention_outputs_kernel(core_ref, low_ref, high_ref, got_ref, query_ref, key_ref, value_ref, out_ref):
    first = core_ref[0] == 0
    keep = jnp.where(first, low_ref[...], high_ref[...])
    got = got_ref[...]
    parts = [jnp.where(first == (side == 0), keep, got).astype(f32) for side in range(2)]
    whole = jnp.concatenate(parts, axis=0)
    column = 0
    for ref in (query_ref, key_ref, value_ref):
        ref[...] = whole[:, column : column + ref.shape[1]]
        column += ref.shape[1]
    out_ref[...] = whole[:, column:].T


def attention_outputs(core, low, high, got, sizes):
    n_query, n_key = sizes
    rows, columns = got.shape
    whole = lambda *shape: pl.BlockSpec(shape, lambda i, core: (0, 0))
    shapes = [(2 * rows, n_query), (2 * rows, n_key), (2 * rows, n_key), (n_query, 2 * rows)]
    return pl.pallas_call(
        attention_outputs_kernel,
        grid_spec=pltpu.PrefetchScalarGridSpec(
            num_scalar_prefetch=1,
            grid=(1,),
            in_specs=[whole(rows, columns)] * 3,
            out_specs=[whole(*shape) for shape in shapes],
        ),
        out_shape=[jax.ShapeDtypeStruct(shape, f32) for shape in shapes],
        compiler_params=params(),
        cost_estimate=cost(0, rows * columns * 14),
        name="attention_outputs",
    )(core.reshape(1), low, high, got)


def wide_outputs_kernel(columns, core_ref, *refs):
    first = core_ref[0] == 0
    gate_ref, up_ref = refs[8:]
    sections = []
    for place in range(4):
        early, late = refs[place][...], refs[4 + place][...]
        head = columns[place % 2]
        rest = gate_ref.shape[1] // 2 - head
        gate = jnp.concatenate([early, late[:, :rest]], axis=1)
        sections.append((gate, late[:, rest:]))
    low, high, got_low, got_high = sections
    for target, part in ((gate_ref, 0), (up_ref, 1)):
        units = target.shape[1] // 2
        keep = jnp.where(first, low[part], high[part])
        got = jnp.where(first, got_low[part], got_high[part])
        target[:, :units] = jnp.where(first, keep, got).astype(f32)
        target[:, units:] = jnp.where(first, got, keep).astype(f32)


def wide_outputs(core, early, late, units):
    rows = early[0].shape[0]
    columns = [share.shape[1] - units for share in early[:2]]
    tile = 128

    def early_spec(head):
        return pl.BlockSpec((tile, head), lambda i, core: (i, units // head))

    return pl.pallas_call(
        functools.partial(wide_outputs_kernel, columns),
        grid_spec=pltpu.PrefetchScalarGridSpec(
            num_scalar_prefetch=1,
            grid=(rows // tile,),
            in_specs=[early_spec(head) for head in columns * 2]
            + [pl.BlockSpec((tile, share.shape[1]), lambda i, core: (i, 0)) for share in late],
            out_specs=[pl.BlockSpec((tile, 2 * units), lambda i, core: (i, 0))] * 2,
        ),
        out_shape=[jax.ShapeDtypeStruct((rows, 2 * units), f32)] * 2,
        compiler_params=params(),
        cost_estimate=cost(0, rows * 32 * units),
        name="wide_outputs",
    )(core.reshape(1), *early, *late)


def down_outputs_kernel(core_ref, low_ref, high_ref, got_low_ref, got_high_ref, down_ref):
    first = core_ref[0] == 0
    units = low_ref.shape[1]
    keep = jnp.where(first, low_ref[...], high_ref[...])
    got = jnp.where(first, got_low_ref[...], got_high_ref[...])
    for side in range(2):
        part = jnp.where(first == (side == 0), keep, got).astype(f32)
        down_ref[side * units : (side + 1) * units, :] = part.T


def down_outputs(core, early, units):
    rows = early[0].shape[0]
    tile = 128
    return pl.pallas_call(
        down_outputs_kernel,
        grid_spec=pltpu.PrefetchScalarGridSpec(
            num_scalar_prefetch=1,
            grid=(rows // tile,),
            in_specs=[pl.BlockSpec((tile, units), lambda i, core: (i, 0))] * 4,
            out_specs=pl.BlockSpec((2 * units, tile), lambda i, core: (0, i)),
        ),
        out_shape=jax.ShapeDtypeStruct((2 * units, rows), f32),
        compiler_params=params(),
        cost_estimate=cost(0, rows * units * 16),
        name="down_outputs",
    )(core.reshape(1), *early)


def pin(value, *others):
    return lax.optimization_barrier((value, *others))


def share_gains(terms):
    core, shard = lax.axis_index("pipe"), lax.axis_index("ctx")
    count = lax.axis_size("ctx")
    own = take(terms, core)
    other = take(terms, 1 - core)
    total = own + swap_cores(other)
    blocks = total.reshape(2, count, -1)

    def block(index):
        return take(blocks, index, 1)

    result = block(shard)
    for step in range(1, count):
        route = [(i, i ^ step) for i in range(count)]
        result = result + lax.ppermute(block(shard ^ step), "ctx", route)
    return result


def product(left, right):
    return lax.dot_general(
        left, right, (((1,), (0,)), ((), ())), preferred_element_type=f32
    )


def rows_product(left, right):
    return lax.dot_general(
        left, right, (((0,), (0,)), ((), ())), preferred_element_type=f32
    )


def cols_product(left, right):
    return lax.dot_general(
        left, right, (((1,), (1,)), ((), ())), preferred_element_type=f32
    )


def norm_forward(stream, gain_vector):
    inv_rms = lax.rsqrt(jnp.mean(stream * stream, axis=-1) + epsilon)
    return ((stream * inv_rms[:, None] * gain_vector[None, :]).astype(bf16), inv_rms)


def norm_backward(stream, inv_rms, gain_vector, upstream):
    weighted = upstream * gain_vector[None, :]
    gain_grad = jnp.sum(upstream * stream * inv_rms[:, None], axis=0)
    inner_mean = jnp.mean(stream * weighted, axis=-1)
    stream_grad = (
        weighted * inv_rms[:, None] - stream * (inv_rms * inv_rms * inv_rms * inner_mean)[:, None]
    )
    return (stream_grad, gain_grad)


def sum_tensor(partial, *others):
    partial = partial.astype(bf16)
    if others:
        partial, *others = pin(partial, *others)
    return lax.psum(partial, "tensor"), *others


def own_share(partial, rows):
    arrived = swap_cores(partial[rows:].astype(bf16))
    return partial[:rows] + arrived.astype(f32)


def half_swap(values):
    lanes = lax.broadcasted_iota(jnp.int32, values.shape, 1)
    count = values.shape[1]
    quarter = HEAD_DIM // 2
    return jnp.where(
        lanes % HEAD_DIM < quarter,
        pltpu.roll(values, count - quarter, 1),
        pltpu.roll(values, quarter, 1),
    )


def wide_table(table, columns):
    return jnp.concatenate([table] * (columns // table.shape[1]), axis=1)


def rope_tables(positions_row, width):
    frequency = jnp.exp(
        jnp.arange(width // 2, dtype=f32) * (-2.0 * math.log(rope_base) / width)
    )
    angles = positions_row.astype(f32)[:, None] * frequency[None, :]
    cosine, sine = jnp.cos(angles), jnp.sin(angles)
    return (
        jnp.concatenate([cosine] * 4, axis=1),
        jnp.concatenate([-sine, sine] * 2, axis=1),
    )


def head_inputs_kernel(sizes, stream_ref, gain_ref, wide_ref, cos_ref, sin_ref,
                       normed_ref, rms_ref, query_ref, own_ref):
    n_query, n_key = sizes
    stream = stream_ref[...].astype(f32)
    inv_rms = lax.rsqrt(jnp.mean(stream * stream, axis=1, keepdims=True) + epsilon)
    normed = (stream * inv_rms * gain_ref[...]).astype(bf16)
    normed_ref[...] = normed
    rms_ref[...] = inv_rms
    raw = jnp.dot(normed, wide_ref[...], preferred_element_type=f32)
    turned = raw[:, : n_query + n_key]
    cosine = wide_table(cos_ref[...], n_query + n_key)
    sine = wide_table(sin_ref[...], n_query + n_key)
    turned = turned * cosine + half_swap(turned) * sine
    query_ref[...] = turned[:, :n_query].astype(bf16)
    own_ref[:, :n_key] = turned[:, n_query:].astype(bf16)
    own_ref[:, n_key:] = raw[:, n_query + n_key :].astype(bf16)


def head_inputs(stream, gain, wide, tables, sizes):
    n_query, n_key = sizes
    rows, width = stream.shape
    columns = n_query + 2 * n_key
    whole = lambda *shape: pl.BlockSpec(shape, lambda i: (0,) * len(shape))
    return pl.pallas_call(
        functools.partial(head_inputs_kernel, sizes),
        grid=(1,),
        in_specs=[
            whole(rows, width),
            whole(1, width),
            whole(width, columns),
            whole(rows, 2 * HEAD_DIM),
            whole(rows, 2 * HEAD_DIM),
        ],
        out_specs=[whole(rows, width), whole(rows, 1), whole(rows, n_query), whole(rows, 2 * n_key)],
        out_shape=[
            jax.ShapeDtypeStruct((rows, width), bf16),
            jax.ShapeDtypeStruct((rows, 1), f32),
            jax.ShapeDtypeStruct((rows, n_query), bf16),
            jax.ShapeDtypeStruct((rows, 2 * n_key), bf16),
        ],
        compiler_params=params(),
        cost_estimate=cost(2 * rows * width * columns, 2 * width * (columns + 4 * rows)),
        name="head_inputs",
    )(stream, gain[None], wide, *tables)


def masked_scores(query, keys, allowed):
    raw = lax.dot_general(query, keys, (((1,), (1,)), ((), ())), preferred_element_type=f32)
    return jnp.where(allowed, raw * HEAD_DIM ** (-0.5), -1e30)


def allowed_pairs(pos, rows):
    distance = (
        lax.broadcasted_iota(jnp.int32, (rows, 2 * rows), 0)
        - lax.broadcasted_iota(jnp.int32, (rows, 2 * rows), 1)
        + rows
    )
    return (distance >= 0) & (distance <= pos)


def head_slice(index):
    return slice(index * HEAD_DIM, (index + 1) * HEAD_DIM)


def mix_kernel(n_key, pos_ref, query_ref, tail_ref, own_ref, wide_ref,
               mixed_ref, log_ref, partial_ref, window, mixed_all):
    rows, n_query = query_ref.shape

    @pl.when(pl.program_id(0) == 0)
    def _():
        window[:rows] = tail_ref[...]
        window[rows:] = own_ref[...]
        allowed = allowed_pairs(pos_ref[...], rows)
        group = HEADS // KV_HEADS
        logs, mixed = [], []
        for head in range(n_query // HEAD_DIM):
            keys = window[:, head_slice(head // group)]
            values = window[:, head_slice((n_key // HEAD_DIM) + head // group)]
            masked = masked_scores(query_ref[:, head_slice(head)], keys, allowed)
            top = jnp.max(masked, axis=1, keepdims=True)
            exponent = jnp.exp(masked - top)
            total = jnp.sum(exponent, axis=1, keepdims=True)
            weights = (exponent * (1.0 / total)).astype(bf16)
            mixed.append(jnp.dot(weights, values, preferred_element_type=f32).astype(bf16))
            logs.append(top + jnp.log(total))
        everything = jnp.concatenate(mixed, axis=1)
        mixed_all[...] = everything
        mixed_ref[...] = everything
        log_ref[...] = jnp.concatenate(logs, axis=1)

    partial_ref[...] = lax.dot_general(
        mixed_all[...],
        wide_ref[...],
        (((1,), (1,)), ((), ())),
        preferred_element_type=f32,
    ).astype(bf16)


def mix(pos, queries, tail, own, wide, n_key):
    rows, n_query = queries.shape
    width, columns = wide.shape
    tile = 512
    heads = n_query // HEAD_DIM
    whole = lambda *shape: pl.BlockSpec(shape, lambda i: (0,) * len(shape))
    return pl.pallas_call(
        functools.partial(mix_kernel, n_key),
        grid=(width // tile,),
        in_specs=[
            whole(rows, 1),
            whole(rows, n_query),
            whole(rows, 2 * n_key),
            whole(rows, 2 * n_key),
            pl.BlockSpec((tile, columns), lambda i: (i, 0)),
        ],
        out_specs=[
            whole(rows, n_query),
            whole(rows, heads),
            pl.BlockSpec((rows, tile), lambda i: (0, i)),
        ],
        out_shape=[
            jax.ShapeDtypeStruct((rows, n_query), bf16),
            jax.ShapeDtypeStruct((rows, heads), f32),
            jax.ShapeDtypeStruct((rows, width), bf16),
        ],
        scratch_shapes=[pltpu.VMEM((2 * rows, 2 * n_key), bf16), pltpu.VMEM((rows, n_query), bf16)],
        compiler_params=params(),
        cost_estimate=cost(
            2 * rows * n_query * (width + 4 * rows), 2 * width * (columns + rows), 2 * rows * rows * heads
        ),
        name="mix",
    )(pos, queries, tail, own, wide)


def mix_back_kernel(n_key, pos_ref, query_ref, tail_ref, own_ref, mixed_ref, log_ref, cos_ref, sin_ref,
                    mid_grad_ref, wide_ref, query_grad_ref, back_ref, own_grad_ref, mid_b_ref,
                    window, mixed_grad):
    rows, n_query = query_ref.shape
    step = pl.program_id(0)
    mid_b = mid_grad_ref[...].astype(bf16)
    mid_b_ref[...] = mid_b
    part = jnp.dot(mid_b, wide_ref[...], preferred_element_type=f32)

    @pl.when(step == 0)
    def _():
        mixed_grad[...] = part

    @pl.when(step > 0)
    def _():
        mixed_grad[...] += part

    @pl.when(step == pl.num_programs(0) - 1)
    def _():
        window[:rows] = tail_ref[...]
        window[rows:] = own_ref[...]
        allowed = allowed_pairs(pos_ref[...], rows)
        group = HEADS // KV_HEADS
        groups = n_key // HEAD_DIM
        scale = HEAD_DIM ** (-0.5)
        grads = mixed_grad[...].astype(bf16)
        over_rows = (((0,), (0,)), ((), ()))
        over_columns = (((1,), (1,)), ((), ()))
        query_grads, key_grads, value_grads = [], [None] * groups, [None] * groups
        for head in range(n_query // HEAD_DIM):
            at = head // group
            keys = window[:, head_slice(at)]
            values = window[:, head_slice(groups + at)]
            query = query_ref[:, head_slice(head)]
            grad = grads[:, head_slice(head)]
            masked = masked_scores(query, keys, allowed)
            prob = jnp.exp(masked - log_ref[:, head : head + 1])
            prob_grad = lax.dot_general(grad, values, over_columns, preferred_element_type=f32)
            delta = jnp.sum(
                grad.astype(f32) * mixed_ref[:, head_slice(head)].astype(f32), axis=1, keepdims=True
            )
            score_grad = (prob * (prob_grad - delta)).astype(bf16)
            query_grads.append(jnp.dot(score_grad, keys, preferred_element_type=f32))
            key_part = lax.dot_general(score_grad, query, over_rows, preferred_element_type=f32)
            value_part = lax.dot_general(
                prob.astype(bf16), grad, over_rows, preferred_element_type=f32
            )
            key_grads[at] = key_part if key_grads[at] is None else key_grads[at] + key_part
            value_grads[at] = value_part if value_grads[at] is None else value_grads[at] + value_part
        query_grad = jnp.concatenate(query_grads, axis=1) * scale
        query_grad = query_grad * wide_table(cos_ref[...], n_query) - half_swap(
            query_grad
        ) * wide_table(sin_ref[...], n_query)
        query_grad_ref[...] = query_grad.astype(bf16)
        key_grad = jnp.concatenate(key_grads, axis=1) * scale
        value_grad = jnp.concatenate(value_grads, axis=1)
        back_ref[:, :n_key] = key_grad[:rows].astype(bf16)
        back_ref[:, n_key:] = value_grad[:rows].astype(bf16)
        own_grad_ref[:, :n_key] = key_grad[rows:]
        own_grad_ref[:, n_key:] = value_grad[rows:]


def mix_back(pos, queries, tail, own, mixed, logs, tables, mid_grad, wide, n_key):
    rows, n_query = queries.shape
    width, columns = wide.shape
    tile = 512
    heads = n_query // HEAD_DIM
    whole = lambda *shape: pl.BlockSpec(shape, lambda i: (0,) * len(shape))
    return pl.pallas_call(
        functools.partial(mix_back_kernel, n_key),
        grid=(width // tile,),
        in_specs=[
            whole(rows, 1),
            whole(rows, n_query),
            whole(rows, 2 * n_key),
            whole(rows, 2 * n_key),
            whole(rows, n_query),
            whole(rows, heads),
            whole(rows, 2 * HEAD_DIM),
            whole(rows, 2 * HEAD_DIM),
            pl.BlockSpec((rows, tile), lambda i: (0, i)),
            pl.BlockSpec((tile, columns), lambda i: (i, 0)),
        ],
        out_specs=[
            whole(rows, n_query),
            whole(rows, 2 * n_key),
            whole(rows, 2 * n_key),
            pl.BlockSpec((rows, tile), lambda i: (0, i)),
        ],
        out_shape=[
            jax.ShapeDtypeStruct((rows, n_query), bf16),
            jax.ShapeDtypeStruct((rows, 2 * n_key), bf16),
            jax.ShapeDtypeStruct((rows, 2 * n_key), f32),
            jax.ShapeDtypeStruct((rows, width), bf16),
        ],
        scratch_shapes=[pltpu.VMEM((2 * rows, 2 * n_key), bf16), pltpu.VMEM((rows, n_query), f32)],
        compiler_params=params(),
        cost_estimate=cost(
            2 * rows * n_query * (width + 10 * rows), 2 * width * (columns + 3 * rows), 2 * rows * rows * heads
        ),
        name="mix_back",
    )(pos, queries, tail, own, mixed, logs, *tables, mid_grad, wide)


def head_grads_kernel(n_key, query_grad_ref, own_grad_ref, back_ref, cos_ref, sin_ref, wide_ref,
                      grads_ref, partial_ref, grads):
    n_query = query_grad_ref.shape[1]

    @pl.when(pl.program_id(0) == 0)
    def _():
        own = own_grad_ref[...] + back_ref[...].astype(f32)
        keys = own[:, :n_key]
        keys = keys * wide_table(cos_ref[...], n_key) - half_swap(keys) * wide_table(
            sin_ref[...], n_key
        )
        grads[:, :n_query] = query_grad_ref[...]
        grads[:, n_query : n_query + n_key] = keys.astype(bf16)
        grads[:, n_query + n_key :] = own[:, n_key:].astype(bf16)
        grads_ref[...] = grads[...]

    partial_ref[...] = lax.dot_general(
        grads[...], wide_ref[...], (((1,), (1,)), ((), ())), preferred_element_type=f32
    ).astype(bf16)


def head_grads(query_grad, own_grad, back, tables, wide, n_key):
    rows, n_query = query_grad.shape
    width = wide.shape[0]
    columns = n_query + 2 * n_key
    tile = 512
    whole = lambda *shape: pl.BlockSpec(shape, lambda i: (0,) * len(shape))
    return pl.pallas_call(
        functools.partial(head_grads_kernel, n_key),
        grid=(width // tile,),
        in_specs=[
            whole(rows, n_query),
            whole(rows, 2 * n_key),
            whole(rows, 2 * n_key),
            whole(rows, 2 * HEAD_DIM),
            whole(rows, 2 * HEAD_DIM),
            pl.BlockSpec((tile, columns), lambda i: (i, 0)),
        ],
        out_specs=[whole(rows, columns), pl.BlockSpec((rows, tile), lambda i: (0, i))],
        out_shape=[
            jax.ShapeDtypeStruct((rows, columns), bf16),
            jax.ShapeDtypeStruct((rows, width), bf16),
        ],
        scratch_shapes=[pltpu.VMEM((rows, columns), bf16)],
        compiler_params=params(),
        cost_estimate=cost(2 * rows * width * columns, 2 * width * (columns + rows)),
        name="head_grads",
    )(query_grad, own_grad, back, *tables, wide)


def attention_forward(stream, gain, wide, place, *others):
    pos, tables, sizes = place
    normed, inv_rms, queries, own = head_inputs(stream, gain, wide[0], tables, sizes)
    tail = from_behind(own, "ctx", 1)
    mixed, logs, partial = mix(pos, queries, tail, own, wide[1], sizes[1])
    total, *others = sum_tensor(partial, *others)
    return total, (stream.astype(f32), inv_rms[:, 0], normed, queries, tail, own, mixed, logs), *others


def ffn_forward_in(middle, gain, wides, hidden_width):
    normed, inv_rms = norm_forward(middle, gain)
    got = swap_cores(normed)
    both = jnp.concatenate([normed, got], axis=0)
    gate_up = [product(both, wide) for wide in wides]
    gate = gate_up[0][:, :hidden_width]
    if gate_up[0].shape[1] > hidden_width:
        gate_up.insert(1, gate_up[0][:, hidden_width:])
    up = jnp.concatenate(gate_up[1:], axis=1)
    hidden = (jax.nn.silu(gate) * up).astype(bf16)
    return (middle, inv_rms, normed, got, gate, up, hidden)


def ffn_share(state, down):
    middle, hidden = state[0], state[-1]
    return own_share(cols_product(hidden, down), middle.shape[0]).astype(bf16)


def ffn_backward(own_grad, other_grad, state, wides, down, head, *others):
    middle, _, normed, got, gate, up, hidden = state
    hidden_grad = product(jnp.concatenate([own_grad, other_grad], axis=0), down)
    sigmoid_gate = jax.nn.sigmoid(gate)
    gate_grad = (hidden_grad * up * sigmoid_gate * (1.0 + gate * (1.0 - sigmoid_gate))).astype(bf16)
    up_grad = (hidden_grad * gate * sigmoid_gate).astype(bf16)
    units = gate.shape[1]
    if len(wides) == 1:
        partial = cols_product(jnp.concatenate([gate_grad, up_grad], axis=1), wides[0])
    else:
        partial = cols_product(gate_grad, wides[0]) + cols_product(up_grad, wides[1])
    normed_grad, *others = sum_tensor(own_share(partial, middle.shape[0]), *others)
    own_sides, norm_sides = (own_grad, other_grad), (normed, got)
    early = token_terms([own_sides, norm_sides], [(0, hidden, 0, units), (1, gate_grad, 0, head)])
    early = lax.psum_scatter(early, "ctx", scatter_dimension=0, tiled=True)
    late = token_terms([norm_sides], [(0, gate_grad, head, units - head), (0, up_grad, 0, units)])
    return normed_grad, early, late, *others


def ffn_backward_out(upstream, normed_grad, state, gain):
    mid_part, gain_term = norm_backward(state[0], state[1], gain, normed_grad.astype(f32))
    return upstream.astype(f32) + mid_part, gain_term


def attention_backward(mid_grad, saved, wide, place, *others):
    pos, tables, sizes = place
    _, _, normed, queries, tail, own, mixed, logs = saved
    query_grad, back, own_grad, mid_grad_b = mix_back(
        pos, queries, tail, own, mixed, logs, tables, mid_grad, wide[1], sizes[1]
    )
    back = from_behind(back, "ctx", -1)
    grads, partial = head_grads(query_grad, own_grad, back, tables, wide[0], sizes[1])
    normed_grad, *others = sum_tensor(partial, *others)
    terms = attention_terms(normed, mid_grad_b, grads, mixed, lax.axis_size("ctx"))
    core = lax.axis_index("pipe")
    mine = take(terms, core)
    theirs = take(terms, 1 - core)
    return normed_grad, add_bf16(mine, swap_cores(theirs)), *others


def attention_backward_out(mid_grad, normed_grad, saved, gain):
    part, gain_term = norm_backward(saved[0], saved[1], gain, normed_grad.astype(f32))
    return (mid_grad + part).astype(bf16), gain_term


def on_device(
    inputs,
    out_grad,
    positions,
    attn_gain,
    w_query,
    w_key,
    w_value,
    w_out,
    ffn_gain,
    w_gate,
    w_up,
    w_down,
):
    core = lax.axis_index("pipe")
    first = core == 0
    shard = lax.axis_index("ctx")
    rows = inputs.shape[1]
    width = inputs.shape[2]
    n_query = w_query.shape[2]
    n_key = w_key.shape[2]
    half = w_gate.shape[2] // 2

    def pick(pair, index):
        return take(pair, index)

    def mine_theirs(array, axis):
        size = array.shape[axis] // 2
        mine = lax.dynamic_slice_in_dim(
            array, core * size, size, axis, allow_negative_indices=False
        )
        theirs = lax.dynamic_slice_in_dim(
            array, (1 - core) * size, size, axis, allow_negative_indices=False
        )
        return mine, theirs

    count = lax.axis_size("ctx")
    gain_row = jnp.concatenate([attn_gain, ffn_gain], axis=1)
    attn_shard = jnp.concatenate([w_query[0], w_key[0], w_value[0], w_out[0].T], axis=1)
    wide_columns = attn_shard.shape[1]
    gain_rows = jnp.pad(gain_row, ((0, 15), (0, wide_columns - gain_row.shape[1])))
    rows_mine, rows_theirs = mine_theirs(attn_shard, 0)
    attn_keep = jnp.concatenate([rows_mine, gain_rows], axis=0)
    attn_got = swap_cores(jnp.concatenate([rows_theirs, gain_rows], axis=0))

    inner_columns = n_query + 2 * n_key

    def attn_weights(pieces):
        got = swap_cores(pieces)
        both = jnp.stack([jnp.where(first, pieces, got), jnp.where(first, got, pieces)], axis=1)
        part_rows = attn_shard.shape[0] // 2
        wide = both[:, :, :part_rows].reshape(width, wide_columns)
        wide = (wide[:, :inner_columns], wide[:, inner_columns:])
        row = pieces[:, part_rows, : gain_row.shape[1]].astype(f32)
        return wide, row.reshape(count, 2, -1).transpose(1, 0, 2).reshape(2, width)

    gate_mine, gate_theirs = mine_theirs(w_gate[0], 1)
    up_mine, up_theirs = mine_theirs(w_up[0], 1)
    wide_keep = jnp.concatenate([gate_mine, up_mine], axis=1)
    wide_got = swap_cores(jnp.concatenate([gate_theirs, up_theirs], axis=1))
    down_mine, down_theirs = mine_theirs(w_down[0], 0)
    down_keep, down_got = down_mine.T, swap_cores(down_theirs.T)

    def for_sections(keep, got):
        return [jnp.where(first, keep, got), jnp.where(first, got, keep)]

    def gather(shard_part):
        return lax.all_gather(shard_part, "ctx", axis=0, tiled=True)

    attn_parts = for_sections(attn_keep, attn_got)
    wide_parts = for_sections(wide_keep, wide_got)
    down_parts = for_sections(down_keep, down_got)
    tail_columns = half // 4
    wide_low = lax.all_gather(
        wide_parts[0][:, :-tail_columns], ("pipe", "ctx"), axis=0, tiled=True
    )
    down_parts[0] = jnp.concatenate([down_parts[0], wide_parts[0][:, -tail_columns:]], axis=1)
    attn_pieces, attn_parts[1], wide_parts[1], *down_parts = pin(
        ring_gather(*ring_gather_start(attn_parts[0])), attn_parts[1], wide_parts[1], *down_parts
    )
    attn_low, gains_low = attn_weights(attn_pieces)
    down_and_tail = gather(down_parts[0])
    ring_columns = wide_parts[1].shape[1] // 4
    wide_high = gather(wide_parts[1][:, :-ring_columns])
    down_high = gather(down_parts[1])

    pos_row = pick(positions, core)
    place = (pos_row[:, None], rope_tables(pos_row, HEAD_DIM), (n_query, n_key))

    def scatter(terms):
        return lax.psum_scatter(terms, "ctx", scatter_dimension=0, tiled=True)

    def give_low(share):
        return lax.ppermute(share, "pipe", [(1, 0)])

    def give_high(share):
        return lax.ppermute(share, "pipe", [(0, 1)])

    stream = pick(inputs, core)
    total, attn_saved_low, wide_low, attn_part_high = attention_forward(
        stream, gains_low[0], attn_low, place, wide_low, attn_parts[1]
    )
    wide_low = pick(wide_low.reshape(2, width, -1), core)
    total, wide_low, attn_ring = pin(total, wide_low, ring_gather_start(attn_part_high))
    middle = attn_saved_low[0] + total.astype(f32)
    down_low, wide_tail = down_and_tail[:, :half], down_and_tail[:, half:]
    state_low = ffn_forward_in(middle, gains_low[1], [wide_low, wide_tail], half)
    own_grad, other_grad = pick(out_grad, core), pick(out_grad, 1 - core)
    (total,) = sum_tensor(ffn_share(state_low, down_low))
    wide_low = jnp.concatenate([wide_low, wide_tail], axis=1)
    total, own_grad, other_grad, (attn_high, gains_high), wide_low = pin(
        total, own_grad, other_grad, attn_weights(ring_gather(*attn_ring)), wide_low
    )
    out_low = (middle + total.astype(f32)).astype(bf16)
    total, attn_saved_high, wide_high, wide_part_high = attention_forward(
        out_low, gains_high[0], attn_high, place, wide_high, wide_parts[1][:, -ring_columns:]
    )
    wide_ring = ring_gather_start(wide_part_high)
    up_high = jnp.concatenate(
        [wide_high[:, half:], ring_gather(*wide_ring).reshape(width, ring_columns)], axis=1
    )
    wide_high = [wide_high[:, :half], up_high]
    total, got_out_low, wide_high = pin(total, swap_cores(out_low), wide_high)
    middle = attn_saved_high[0] + total.astype(f32)
    state_high = ffn_forward_in(middle, gains_high[1], wide_high, half)

    gate, up, down_high = pin(state_high[4], state_high[5], down_high)
    hidden = (jax.nn.silu(gate) * up).astype(bf16)
    state_high = (*state_high[:4], gate, up, hidden)
    normed_grad, early_high, late_high = ffn_backward(
        own_grad, other_grad, state_high, wide_high, down_high, half // 2
    )
    normed_grad, late_high = pin(normed_grad, late_high)
    mid_grad, ffn_gain_high = ffn_backward_out(own_grad, normed_grad, state_high, gains_high[1])
    late_high = scatter(late_high)
    normed_grad, summed, early_high = attention_backward(
        mid_grad, attn_saved_high, attn_high, place, early_high
    )
    normed_grad, attn_ring, out_share = pin(
        normed_grad, ring_scatter_start(summed), ffn_share(state_high, down_high)
    )
    boundary_high, attn_gain_high = attention_backward_out(
        mid_grad, normed_grad, attn_saved_high, gains_high[0]
    )
    got_boundary_high = swap_cores(boundary_high)
    normed_grad, early_low, late_low, late_high = ffn_backward(
        boundary_high, got_boundary_high, state_low, [wide_low], down_low, half // 4, late_high
    )
    normed_grad, late_low, attn_share_high = pin(normed_grad, late_low, ring_scatter(*attn_ring))
    mid_grad, ffn_gain_low = ffn_backward_out(
        boundary_high, normed_grad, state_low, gains_low[1]
    )
    late_low = scatter(late_low)
    normed_grad, summed, early_low = attention_backward(
        mid_grad, attn_saved_low, attn_low, place, early_low
    )
    def from_other(low, high):
        return swap_cores(jnp.where(first, high, low))

    (total,) = sum_tensor(out_share)
    attn_pair = (ring_scatter(*ring_scatter_start(summed)), attn_share_high)
    attn_outs = attention_outputs(core, *attn_pair, from_other(*attn_pair), (n_query, n_key))
    early = (early_low, early_high, give_low(early_low), give_high(early_high))
    down_out = down_outputs(core, early, half)
    normed_grad, down_out, attn_outs, got_late_high = pin(
        normed_grad, down_out, attn_outs, give_high(late_high)
    )
    out_high = (middle + total.astype(f32)).astype(bf16)

    boundary_low, attn_gain_low = attention_backward_out(
        mid_grad, normed_grad, attn_saved_low, gains_low[0]
    )
    gains_out = share_gains(
        jnp.stack(
            [jnp.stack([attn_gain_low, ffn_gain_low]), jnp.stack([attn_gain_high, ffn_gain_high])]
        )
    )
    late_low, gains_out, got_out_high, got_boundary_low = pin(
        late_low, gains_out, swap_cores(out_high), swap_cores(boundary_low)
    )
    outs = (out_low, out_high, got_out_low, got_out_high)
    boundaries = (boundary_low, boundary_high, got_boundary_low, got_boundary_high)
    section_outputs, boundary_grads = section_stacks(core, *outs, *boundaries)
    late = (late_low, late_high, give_low(late_low), got_late_high)
    gate_out, up_out = wide_outputs(core, early, late, half)
    query_out, key_out, value_out, attn_out = attn_outs
    return (
        section_outputs[None],
        boundary_grads[None],
        gains_out[:1],
        query_out[None],
        key_out[None],
        value_out[None],
        attn_out[None],
        gains_out[1:],
        gate_out[None],
        up_out[None],
        down_out[None],
    )


def solution(mesh):
    in_specs = (
        P(None, "ctx", None),
        P(None, "ctx", None),
        P(None, "ctx"),
        P("pipe", "ctx"),
        P("pipe", "ctx", "tensor"),
        P("pipe", "ctx", "tensor"),
        P("pipe", "ctx", "tensor"),
        P("pipe", "tensor", "ctx"),
        P("pipe", "ctx"),
        P("pipe", "ctx", "tensor"),
        P("pipe", "ctx", "tensor"),
        P("pipe", "tensor", "ctx"),
    )
    out_specs = (
        P("pipe", None, "ctx", None),
        P("pipe", None, "ctx", None),
        P("pipe", "ctx"),
        P("pipe", "ctx", "tensor"),
        P("pipe", "ctx", "tensor"),
        P("pipe", "ctx", "tensor"),
        P("pipe", "tensor", "ctx"),
        P("pipe", "ctx"),
        P("pipe", "ctx", "tensor"),
        P("pipe", "ctx", "tensor"),
        P("pipe", "tensor", "ctx"),
    )
    return jax.shard_map(
        on_device, mesh=mesh, in_specs=in_specs, out_specs=out_specs, check_vma=False
    )
```

```python
import functools
import math

import jax
import jax.numpy as jnp
from jax import lax
from jax.experimental import pallas as pl
from jax.experimental.pallas import tpu as pltpu
from jax.sharding import PartitionSpec as P

HEADS = 32
KV_HEADS = 8
HEAD_DIM = 64
MAXLEN = 256

epsilon = 1e-05
rope_base = 500000.0
bf16 = jnp.bfloat16
f32 = jnp.float32


def swap_cores(block):
    return lax.ppermute(block, "pipe", [(0, 1), (1, 0)])


def from_behind(block, axis, distance):
    devices = range(lax.axis_size(axis))
    route = [(i - distance, i) for i in devices if i - distance in devices]
    return lax.ppermute(block, axis, route)


def ring_order(count):
    across = 1 << (count.bit_length() - 1) // 2
    down = count // across
    walk = [(0, x) for x in range(across)]
    for y in range(1, down):
        columns = range(1, across)
        walk += [(y, x) for x in (columns if y % 2 == 0 else reversed(columns))]
    walk += [(y, 0) for y in range(down - 1, 0, -1)]
    return [y * across + x for y, x in walk]


def take(array, index, axis=0):
    return lax.dynamic_index_in_dim(
        array, index, axis, keepdims=False, allow_negative_indices=False
    )


def ring_tools():
    count = lax.axis_size("ctx")
    order = ring_order(count)
    ahead = [(order[i], order[(i + 1) % count]) for i in range(count)]
    behind = [(b, a) for a, b in ahead]
    device = lax.axis_index("ctx")

    def device_at(distance):
        if order == [0, 1, 3, 2]:
            place = ((device ^ (device >> 1)) + distance % count) & 3
            return place ^ (place >> 1)
        place = jnp.asarray([order.index(i) for i in range(count)], jnp.int32)
        return take(jnp.asarray(order * 2, jnp.int32), take(place, device) + distance % count)

    return count, ahead, behind, device_at


def ring_gather_start(block):
    count, ahead, behind, _ = ring_tools()
    from_back, from_front = [block], [block]
    for _ in range(1, count // 2):
        from_back.append(lax.ppermute(from_back[-1], "ctx", ahead))
        from_front.append(lax.ppermute(from_front[-1], "ctx", behind))
    return from_back, from_front


def ring_gather(from_back, from_front):
    count, ahead, behind, device_at = ring_tools()
    block = from_back[0]
    half = block.shape[1] // 2
    left = lax.ppermute(from_back[-1][:, :half], "ctx", ahead)
    right = lax.ppermute(from_front[-1][:, half:], "ctx", behind)
    out = jnp.zeros((count,) + block.shape, block.dtype)

    def put(out, piece, distance, column=0):
        return lax.dynamic_update_slice(
            out, piece[None], (device_at(distance), 0, column), allow_negative_indices=False
        )

    out = put(out, block, 0)
    for distance in range(1, count // 2):
        out = put(out, from_back[distance], -distance)
        out = put(out, from_front[distance], distance)
    out = put(out, left, count // 2)
    return put(out, right, count // 2, half)


def ring_term(terms, distance):
    return take(terms, ring_tools()[3](distance))


def ring_scatter_start(terms):
    count, ahead, behind, _ = ring_tools()
    half = terms.shape[2] // 2
    far = ring_term(terms, count // 2)
    to_front = lax.ppermute(far[:, :half], "ctx", ahead)
    to_back = lax.ppermute(far[:, half:], "ctx", behind)
    for distance in range(count // 2 - 1, 0, -1):
        front, back = ring_term(terms, distance), ring_term(terms, -distance)
        if distance == count // 2 - 1:
            front = jnp.concatenate([add_bf16(front[:, :half], to_front), front[:, half:]], axis=1)
            back = jnp.concatenate([back[:, :half], add_bf16(back[:, half:], to_back)], axis=1)
        else:
            front, back = add_bf16(front, to_front), add_bf16(back, to_back)
        if distance > 1:
            front = lax.ppermute(front, "ctx", ahead)
            back = lax.ppermute(back, "ctx", behind)
        to_front, to_back = front, back
    return ring_term(terms, 0), to_front, to_back


def ring_scatter(own, to_front, to_back):
    _, ahead, behind, _ = ring_tools()
    from_back = lax.ppermute(to_front, "ctx", ahead)
    from_front = lax.ppermute(to_back, "ctx", behind)
    return (own.astype(f32) + from_back.astype(f32) + from_front.astype(f32)).astype(bf16)


def add_bf16(a, b):
    return (a.astype(f32) + b.astype(f32)).astype(bf16)


def params(megabytes=24):
    return pltpu.CompilerParams(vmem_limit_bytes=megabytes * 2**20)


def cost(flops, bytes_accessed, transcendentals=0):
    return pl.CostEstimate(
        flops=flops, bytes_accessed=bytes_accessed, transcendentals=transcendentals
    )


def token_terms_kernel(plan, *refs):
    out_ref = refs[-1]
    lefts, rights = refs[: -1 - len(plan)], refs[-1 - len(plan) : -1]
    rows = (((0,), (0,)), ((), ()))
    column = 0
    for (left, start, columns), right_ref in zip(plan, rights):
        own, got = lefts[2 * left], lefts[2 * left + 1]
        half, part = own.shape[0], slice(start, start + columns)
        total = lax.dot_general(own[...], right_ref[:half, part], rows, preferred_element_type=f32)
        total += lax.dot_general(got[...], right_ref[half:, part], rows, preferred_element_type=f32)
        out_ref[:, column : column + columns] = total.astype(bf16)
        column += columns


def token_terms(lefts, rights):
    tokens, width = lefts[0][0].shape
    tile = 512
    columns = sum(right[3] for right in rights)
    side = pl.BlockSpec((tokens, tile), lambda i: (0, i))
    arrays = [right[1] for right in rights]
    plan = [(right[0], right[2], right[3]) for right in rights]
    return pl.pallas_call(
        functools.partial(token_terms_kernel, plan),
        grid=(width // tile,),
        in_specs=[side] * (2 * len(lefts))
        + [pl.BlockSpec(array.shape, lambda i: (0, 0)) for array in arrays],
        out_specs=pl.BlockSpec((tile, columns), lambda i: (i, 0)),
        out_shape=jax.ShapeDtypeStruct((width, columns), bf16),
        compiler_params=params(),
        cost_estimate=cost(
            4 * tokens * width * columns,
            2 * (width * columns + 2 * tokens * width * len(lefts) + 2 * tokens * columns),
        ),
        name="token_terms",
    )(*(array for pair in lefts for array in pair), *arrays)


def attention_terms_kernel(normed_ref, mid_grad_ref, grads_ref, mixed_ref, out_ref):
    n_grads = grads_ref.shape[1]
    half = out_ref.shape[1]
    rows = (((0,), (0,)), ((), ()))
    inner = lax.dot_general(normed_ref[...], grads_ref[...], rows, preferred_element_type=f32)
    outer = lax.dot_general(mid_grad_ref[...], mixed_ref[...], rows, preferred_element_type=f32)
    for part in range(2):
        part_rows = slice(part * half, (part + 1) * half)
        out_ref[part, :, :n_grads] = inner[part_rows].astype(bf16)
        out_ref[part, :, n_grads:] = outer[part_rows].astype(bf16)


def attention_terms(normed, mid_grad, grads, mixed, count):
    tokens, width = normed.shape
    columns = grads.shape[1] + mixed.shape[1]
    tile = width // count
    return pl.pallas_call(
        attention_terms_kernel,
        grid=(count,),
        in_specs=[
            pl.BlockSpec((tokens, tile), lambda i: (0, i)),
            pl.BlockSpec((tokens, tile), lambda i: (0, i)),
            pl.BlockSpec((tokens, grads.shape[1]), lambda i: (0, 0)),
            pl.BlockSpec((tokens, mixed.shape[1]), lambda i: (0, 0)),
        ],
        out_specs=pl.BlockSpec((2, None, tile // 2, columns), lambda i: (0, i, 0, 0)),
        out_shape=jax.ShapeDtypeStruct((2, count, tile // 2, columns), bf16),
        compiler_params=params(),
        cost_estimate=pl.CostEstimate(
            flops=2 * tokens * width * columns,
            bytes_accessed=2 * (width * columns + 2 * tokens * width + tokens * columns),
            transcendentals=0,
        ),
        name="attention_terms",
    )(normed, mid_grad, grads, mixed)


def section_stacks_kernel(core_ref, *refs):
    first = core_ref[0] == 0
    for sources, target in ((refs[:4], refs[8]), (refs[4:8], refs[9])):
        low, high, got_low, got_high = (source[...] for source in sources)
        keep, got = jnp.where(first, low, high), jnp.where(first, got_low, got_high)
        target[...] = jnp.where(core_ref[0] == pl.program_id(0), keep, got)


def section_stacks(core, *sources):
    rows, width = sources[0].shape
    block = pl.BlockSpec((rows, width), lambda i, core: (0, 0))
    return pl.pallas_call(
        section_stacks_kernel,
        grid_spec=pltpu.PrefetchScalarGridSpec(
            num_scalar_prefetch=1,
            grid=(2,),
            in_specs=[block] * 8,
            out_specs=[pl.BlockSpec((None, rows, width), lambda i, core: (i, 0, 0))] * 2,
        ),
        out_shape=[jax.ShapeDtypeStruct((2, rows, width), bf16)] * 2,
        compiler_params=params(40),
        cost_estimate=cost(0, 12 * rows * width * 2),
        name="section_stacks",
    )(core.reshape(1), *sources)


def attention_outputs_kernel(core_ref, low_ref, high_ref, got_ref, query_ref, key_ref, value_ref, out_ref):
    first = core_ref[0] == 0
    keep = jnp.where(first, low_ref[...], high_ref[...])
    got = got_ref[...]
    parts = [jnp.where(first == (side == 0), keep, got).astype(f32) for side in range(2)]
    whole = jnp.concatenate(parts, axis=0)
    column = 0
    for ref in (query_ref, key_ref, value_ref):
        ref[...] = whole[:, column : column + ref.shape[1]]
        column += ref.shape[1]
    out_ref[...] = whole[:, column:].T


def attention_outputs(core, low, high, got, sizes):
    n_query, n_key = sizes
    rows, columns = got.shape
    whole = lambda *shape: pl.BlockSpec(shape, lambda i, core: (0, 0))
    shapes = [(2 * rows, n_query), (2 * rows, n_key), (2 * rows, n_key), (n_query, 2 * rows)]
    return pl.pallas_call(
        attention_outputs_kernel,
        grid_spec=pltpu.PrefetchScalarGridSpec(
            num_scalar_prefetch=1,
            grid=(1,),
            in_specs=[whole(rows, columns)] * 3,
            out_specs=[whole(*shape) for shape in shapes],
        ),
        out_shape=[jax.ShapeDtypeStruct(shape, f32) for shape in shapes],
        compiler_params=params(),
        cost_estimate=cost(0, rows * columns * 14),
        name="attention_outputs",
    )(core.reshape(1), low, high, got)


def wide_outputs_kernel(columns, core_ref, *refs):
    first = core_ref[0] == 0
    gate_ref, up_ref = refs[8:]
    sections = []
    for place in range(4):
        early, late = refs[place][...], refs[4 + place][...]
        head = columns[place % 2]
        rest = gate_ref.shape[1] // 2 - head
        gate = jnp.concatenate([early, late[:, :rest]], axis=1)
        sections.append((gate, late[:, rest:]))
    low, high, got_low, got_high = sections
    for target, part in ((gate_ref, 0), (up_ref, 1)):
        units = target.shape[1] // 2
        keep = jnp.where(first, low[part], high[part])
        got = jnp.where(first, got_low[part], got_high[part])
        target[:, :units] = jnp.where(first, keep, got).astype(f32)
        target[:, units:] = jnp.where(first, got, keep).astype(f32)


def wide_outputs(core, early, late, units):
    rows = early[0].shape[0]
    columns = [share.shape[1] - units for share in early[:2]]
    tile = 128

    def early_spec(head):
        return pl.BlockSpec((tile, head), lambda i, core: (i, units // head))

    return pl.pallas_call(
        functools.partial(wide_outputs_kernel, columns),
        grid_spec=pltpu.PrefetchScalarGridSpec(
            num_scalar_prefetch=1,
            grid=(rows // tile,),
            in_specs=[early_spec(head) for head in columns * 2]
            + [pl.BlockSpec((tile, share.shape[1]), lambda i, core: (i, 0)) for share in late],
            out_specs=[pl.BlockSpec((tile, 2 * units), lambda i, core: (i, 0))] * 2,
        ),
        out_shape=[jax.ShapeDtypeStruct((rows, 2 * units), f32)] * 2,
        compiler_params=params(),
        cost_estimate=cost(0, rows * 32 * units),
        name="wide_outputs",
    )(core.reshape(1), *early, *late)


def down_outputs_kernel(core_ref, low_ref, high_ref, got_low_ref, got_high_ref, down_ref):
    first = core_ref[0] == 0
    units = low_ref.shape[1]
    keep = jnp.where(first, low_ref[...], high_ref[...])
    got = jnp.where(first, got_low_ref[...], got_high_ref[...])
    for side in range(2):
        part = jnp.where(first == (side == 0), keep, got).astype(f32)
        down_ref[side * units : (side + 1) * units, :] = part.T


def down_outputs(core, early, units):
    rows = early[0].shape[0]
    tile = 128
    return pl.pallas_call(
        down_outputs_kernel,
        grid_spec=pltpu.PrefetchScalarGridSpec(
            num_scalar_prefetch=1,
            grid=(rows // tile,),
            in_specs=[pl.BlockSpec((tile, units), lambda i, core: (i, 0))] * 4,
            out_specs=pl.BlockSpec((2 * units, tile), lambda i, core: (0, i)),
        ),
        out_shape=jax.ShapeDtypeStruct((2 * units, rows), f32),
        compiler_params=params(),
        cost_estimate=cost(0, rows * units * 16),
        name="down_outputs",
    )(core.reshape(1), *early)


def pin(value, *others):
    return lax.optimization_barrier((value, *others))


def share_gains(terms):
    core, shard = lax.axis_index("pipe"), lax.axis_index("ctx")
    count = lax.axis_size("ctx")
    own = take(terms, core)
    other = take(terms, 1 - core)
    total = own + swap_cores(other)
    blocks = total.reshape(2, count, -1)

    def block(index):
        return take(blocks, index, 1)

    result = block(shard)
    for step in range(1, count):
        route = [(i, i ^ step) for i in range(count)]
        result = result + lax.ppermute(block(shard ^ step), "ctx", route)
    return result


def product(left, right):
    return lax.dot_general(
        left, right, (((1,), (0,)), ((), ())), preferred_element_type=f32
    )


def rows_product(left, right):
    return lax.dot_general(
        left, right, (((0,), (0,)), ((), ())), preferred_element_type=f32
    )


def cols_product(left, right):
    return lax.dot_general(
        left, right, (((1,), (1,)), ((), ())), preferred_element_type=f32
    )


def norm_forward(stream, gain_vector):
    inv_rms = lax.rsqrt(jnp.mean(stream * stream, axis=-1) + epsilon)
    return ((stream * inv_rms[:, None] * gain_vector[None, :]).astype(bf16), inv_rms)


def norm_backward(stream, inv_rms, gain_vector, upstream):
    weighted = upstream * gain_vector[None, :]
    gain_grad = jnp.sum(upstream * stream * inv_rms[:, None], axis=0)
    inner_mean = jnp.mean(stream * weighted, axis=-1)
    stream_grad = (
        weighted * inv_rms[:, None] - stream * (inv_rms * inv_rms * inv_rms * inner_mean)[:, None]
    )
    return (stream_grad, gain_grad)


def sum_tensor(partial, *others):
    partial = partial.astype(bf16)
    if others:
        partial, *others = pin(partial, *others)
    return lax.psum(partial, "tensor"), *others


def own_share(partial, rows):
    arrived = swap_cores(partial[rows:].astype(bf16))
    return partial[:rows] + arrived.astype(f32)


def half_swap(values):
    lanes = lax.broadcasted_iota(jnp.int32, values.shape, 1)
    count = values.shape[1]
    quarter = HEAD_DIM // 2
    return jnp.where(
        lanes % HEAD_DIM < quarter,
        pltpu.roll(values, count - quarter, 1),
        pltpu.roll(values, quarter, 1),
    )


def wide_table(table, columns):
    return jnp.concatenate([table] * (columns // table.shape[1]), axis=1)


def rope_tables(positions_row, width):
    frequency = jnp.exp(
        jnp.arange(width // 2, dtype=f32) * (-2.0 * math.log(rope_base) / width)
    )
    angles = positions_row.astype(f32)[:, None] * frequency[None, :]
    cosine, sine = jnp.cos(angles), jnp.sin(angles)
    return (
        jnp.concatenate([cosine] * 4, axis=1),
        jnp.concatenate([-sine, sine] * 2, axis=1),
    )


def head_inputs_kernel(sizes, stream_ref, gain_ref, wide_ref, cos_ref, sin_ref,
                       normed_ref, rms_ref, query_ref, own_ref):
    n_query, n_key = sizes
    stream = stream_ref[...].astype(f32)
    inv_rms = lax.rsqrt(jnp.mean(stream * stream, axis=1, keepdims=True) + epsilon)
    normed = (stream * inv_rms * gain_ref[...]).astype(bf16)
    normed_ref[...] = normed
    rms_ref[...] = inv_rms
    raw = jnp.dot(normed, wide_ref[...], preferred_element_type=f32)
    turned = raw[:, : n_query + n_key]
    cosine = wide_table(cos_ref[...], n_query + n_key)
    sine = wide_table(sin_ref[...], n_query + n_key)
    turned = turned * cosine + half_swap(turned) * sine
    query_ref[...] = turned[:, :n_query].astype(bf16)
    own_ref[:, :n_key] = turned[:, n_query:].astype(bf16)
    own_ref[:, n_key:] = raw[:, n_query + n_key :].astype(bf16)


def head_inputs(stream, gain, wide, tables, sizes):
    n_query, n_key = sizes
    rows, width = stream.shape
    columns = n_query + 2 * n_key
    whole = lambda *shape: pl.BlockSpec(shape, lambda i: (0,) * len(shape))
    return pl.pallas_call(
        functools.partial(head_inputs_kernel, sizes),
        grid=(1,),
        in_specs=[
            whole(rows, width),
            whole(1, width),
            whole(width, columns),
            whole(rows, 2 * HEAD_DIM),
            whole(rows, 2 * HEAD_DIM),
        ],
        out_specs=[whole(rows, width), whole(rows, 1), whole(rows, n_query), whole(rows, 2 * n_key)],
        out_shape=[
            jax.ShapeDtypeStruct((rows, width), bf16),
            jax.ShapeDtypeStruct((rows, 1), f32),
            jax.ShapeDtypeStruct((rows, n_query), bf16),
            jax.ShapeDtypeStruct((rows, 2 * n_key), bf16),
        ],
        compiler_params=params(),
        cost_estimate=cost(2 * rows * width * columns, 2 * width * (columns + 4 * rows)),
        name="head_inputs",
    )(stream, gain[None], wide, *tables)


def masked_scores(query, keys, allowed):
    raw = lax.dot_general(query, keys, (((1,), (1,)), ((), ())), preferred_element_type=f32)
    return jnp.where(allowed, raw * HEAD_DIM ** (-0.5), -1e30)


def allowed_pairs(pos, rows):
    distance = (
        lax.broadcasted_iota(jnp.int32, (rows, 2 * rows), 0)
        - lax.broadcasted_iota(jnp.int32, (rows, 2 * rows), 1)
        + rows
    )
    return (distance >= 0) & (distance <= pos)


def head_slice(index):
    return slice(index * HEAD_DIM, (index + 1) * HEAD_DIM)


def mix_kernel(n_key, pos_ref, query_ref, tail_ref, own_ref, wide_ref,
               mixed_ref, log_ref, partial_ref, window, mixed_all):
    rows, n_query = query_ref.shape

    @pl.when(pl.program_id(0) == 0)
    def _():
        window[:rows] = tail_ref[...]
        window[rows:] = own_ref[...]
        allowed = allowed_pairs(pos_ref[...], rows)
        group = HEADS // KV_HEADS
        logs, mixed = [], []
        for head in range(n_query // HEAD_DIM):
            keys = window[:, head_slice(head // group)]
            values = window[:, head_slice((n_key // HEAD_DIM) + head // group)]
            masked = masked_scores(query_ref[:, head_slice(head)], keys, allowed)
            top = jnp.max(masked, axis=1, keepdims=True)
            exponent = jnp.exp(masked - top)
            total = jnp.sum(exponent, axis=1, keepdims=True)
            weights = (exponent * (1.0 / total)).astype(bf16)
            mixed.append(jnp.dot(weights, values, preferred_element_type=f32).astype(bf16))
            logs.append(top + jnp.log(total))
        everything = jnp.concatenate(mixed, axis=1)
        mixed_all[...] = everything
        mixed_ref[...] = everything
        log_ref[...] = jnp.concatenate(logs, axis=1)

    partial_ref[...] = lax.dot_general(
        mixed_all[...],
        wide_ref[...],
        (((1,), (1,)), ((), ())),
        preferred_element_type=f32,
    ).astype(bf16)


def mix(pos, queries, tail, own, wide, n_key):
    rows, n_query = queries.shape
    width, columns = wide.shape
    tile = 512
    heads = n_query // HEAD_DIM
    whole = lambda *shape: pl.BlockSpec(shape, lambda i: (0,) * len(shape))
    return pl.pallas_call(
        functools.partial(mix_kernel, n_key),
        grid=(width // tile,),
        in_specs=[
            whole(rows, 1),
            whole(rows, n_query),
            whole(rows, 2 * n_key),
            whole(rows, 2 * n_key),
            pl.BlockSpec((tile, columns), lambda i: (i, 0)),
        ],
        out_specs=[
            whole(rows, n_query),
            whole(rows, heads),
            pl.BlockSpec((rows, tile), lambda i: (0, i)),
        ],
        out_shape=[
            jax.ShapeDtypeStruct((rows, n_query), bf16),
            jax.ShapeDtypeStruct((rows, heads), f32),
            jax.ShapeDtypeStruct((rows, width), bf16),
        ],
        scratch_shapes=[pltpu.VMEM((2 * rows, 2 * n_key), bf16), pltpu.VMEM((rows, n_query), bf16)],
        compiler_params=params(),
        cost_estimate=cost(
            2 * rows * n_query * (width + 4 * rows), 2 * width * (columns + rows), 2 * rows * rows * heads
        ),
        name="mix",
    )(pos, queries, tail, own, wide)


def mix_back_kernel(n_key, pos_ref, query_ref, tail_ref, own_ref, mixed_ref, log_ref, cos_ref, sin_ref,
                    mid_grad_ref, wide_ref, query_grad_ref, back_ref, own_grad_ref, mid_b_ref,
                    window, mixed_grad):
    rows, n_query = query_ref.shape
    step = pl.program_id(0)
    mid_b = mid_grad_ref[...].astype(bf16)
    mid_b_ref[...] = mid_b
    part = jnp.dot(mid_b, wide_ref[...], preferred_element_type=f32)

    @pl.when(step == 0)
    def _():
        mixed_grad[...] = part

    @pl.when(step > 0)
    def _():
        mixed_grad[...] += part

    @pl.when(step == pl.num_programs(0) - 1)
    def _():
        window[:rows] = tail_ref[...]
        window[rows:] = own_ref[...]
        allowed = allowed_pairs(pos_ref[...], rows)
        group = HEADS // KV_HEADS
        groups = n_key // HEAD_DIM
        scale = HEAD_DIM ** (-0.5)
        grads = mixed_grad[...].astype(bf16)
        over_rows = (((0,), (0,)), ((), ()))
        over_columns = (((1,), (1,)), ((), ()))
        query_grads, key_grads, value_grads = [], [None] * groups, [None] * groups
        for head in range(n_query // HEAD_DIM):
            at = head // group
            keys = window[:, head_slice(at)]
            values = window[:, head_slice(groups + at)]
            query = query_ref[:, head_slice(head)]
            grad = grads[:, head_slice(head)]
            masked = masked_scores(query, keys, allowed)
            prob = jnp.exp(masked - log_ref[:, head : head + 1])
            prob_grad = lax.dot_general(grad, values, over_columns, preferred_element_type=f32)
            delta = jnp.sum(
                grad.astype(f32) * mixed_ref[:, head_slice(head)].astype(f32), axis=1, keepdims=True
            )
            score_grad = (prob * (prob_grad - delta)).astype(bf16)
            query_grads.append(jnp.dot(score_grad, keys, preferred_element_type=f32))
            key_part = lax.dot_general(score_grad, query, over_rows, preferred_element_type=f32)
            value_part = lax.dot_general(
                prob.astype(bf16), grad, over_rows, preferred_element_type=f32
            )
            key_grads[at] = key_part if key_grads[at] is None else key_grads[at] + key_part
            value_grads[at] = value_part if value_grads[at] is None else value_grads[at] + value_part
        query_grad = jnp.concatenate(query_grads, axis=1) * scale
        query_grad = query_grad * wide_table(cos_ref[...], n_query) - half_swap(
            query_grad
        ) * wide_table(sin_ref[...], n_query)
        query_grad_ref[...] = query_grad.astype(bf16)
        key_grad = jnp.concatenate(key_grads, axis=1) * scale
        value_grad = jnp.concatenate(value_grads, axis=1)
        back_ref[:, :n_key] = key_grad[:rows].astype(bf16)
        back_ref[:, n_key:] = value_grad[:rows].astype(bf16)
        own_grad_ref[:, :n_key] = key_grad[rows:]
        own_grad_ref[:, n_key:] = value_grad[rows:]


def mix_back(pos, queries, tail, own, mixed, logs, tables, mid_grad, wide, n_key):
    rows, n_query = queries.shape
    width, columns = wide.shape
    tile = 512
    heads = n_query // HEAD_DIM
    whole = lambda *shape: pl.BlockSpec(shape, lambda i: (0,) * len(shape))
    return pl.pallas_call(
        functools.partial(mix_back_kernel, n_key),
        grid=(width // tile,),
        in_specs=[
            whole(rows, 1),
            whole(rows, n_query),
            whole(rows, 2 * n_key),
            whole(rows, 2 * n_key),
            whole(rows, n_query),
            whole(rows, heads),
            whole(rows, 2 * HEAD_DIM),
            whole(rows, 2 * HEAD_DIM),
            pl.BlockSpec((rows, tile), lambda i: (0, i)),
            pl.BlockSpec((tile, columns), lambda i: (i, 0)),
        ],
        out_specs=[
            whole(rows, n_query),
            whole(rows, 2 * n_key),
            whole(rows, 2 * n_key),
            pl.BlockSpec((rows, tile), lambda i: (0, i)),
        ],
        out_shape=[
            jax.ShapeDtypeStruct((rows, n_query), bf16),
            jax.ShapeDtypeStruct((rows, 2 * n_key), bf16),
            jax.ShapeDtypeStruct((rows, 2 * n_key), f32),
            jax.ShapeDtypeStruct((rows, width), bf16),
        ],
        scratch_shapes=[pltpu.VMEM((2 * rows, 2 * n_key), bf16), pltpu.VMEM((rows, n_query), f32)],
        compiler_params=params(),
        cost_estimate=cost(
            2 * rows * n_query * (width + 10 * rows), 2 * width * (columns + 3 * rows), 2 * rows * rows * heads
        ),
        name="mix_back",
    )(pos, queries, tail, own, mixed, logs, *tables, mid_grad, wide)


def head_grads_kernel(n_key, query_grad_ref, own_grad_ref, back_ref, cos_ref, sin_ref, wide_ref,
                      grads_ref, partial_ref, grads):
    n_query = query_grad_ref.shape[1]

    @pl.when(pl.program_id(0) == 0)
    def _():
        own = own_grad_ref[...] + back_ref[...].astype(f32)
        keys = own[:, :n_key]
        keys = keys * wide_table(cos_ref[...], n_key) - half_swap(keys) * wide_table(
            sin_ref[...], n_key
        )
        grads[:, :n_query] = query_grad_ref[...]
        grads[:, n_query : n_query + n_key] = keys.astype(bf16)
        grads[:, n_query + n_key :] = own[:, n_key:].astype(bf16)
        grads_ref[...] = grads[...]

    partial_ref[...] = lax.dot_general(
        grads[...], wide_ref[...], (((1,), (1,)), ((), ())), preferred_element_type=f32
    ).astype(bf16)


def head_grads(query_grad, own_grad, back, tables, wide, n_key):
    rows, n_query = query_grad.shape
    width = wide.shape[0]
    columns = n_query + 2 * n_key
    tile = 512
    whole = lambda *shape: pl.BlockSpec(shape, lambda i: (0,) * len(shape))
    return pl.pallas_call(
        functools.partial(head_grads_kernel, n_key),
        grid=(width // tile,),
        in_specs=[
            whole(rows, n_query),
            whole(rows, 2 * n_key),
            whole(rows, 2 * n_key),
            whole(rows, 2 * HEAD_DIM),
            whole(rows, 2 * HEAD_DIM),
            pl.BlockSpec((tile, columns), lambda i: (i, 0)),
        ],
        out_specs=[whole(rows, columns), pl.BlockSpec((rows, tile), lambda i: (0, i))],
        out_shape=[
            jax.ShapeDtypeStruct((rows, columns), bf16),
            jax.ShapeDtypeStruct((rows, width), bf16),
        ],
        scratch_shapes=[pltpu.VMEM((rows, columns), bf16)],
        compiler_params=params(),
        cost_estimate=cost(2 * rows * width * columns, 2 * width * (columns + rows)),
        name="head_grads",
    )(query_grad, own_grad, back, *tables, wide)


def attention_forward(stream, gain, wide, place, *others):
    pos, tables, sizes = place
    normed, inv_rms, queries, own = head_inputs(stream, gain, wide[0], tables, sizes)
    tail = from_behind(own, "ctx", 1)
    mixed, logs, partial = mix(pos, queries, tail, own, wide[1], sizes[1])
    total, *others = sum_tensor(partial, *others)
    return total, (stream.astype(f32), inv_rms[:, 0], normed, queries, tail, own, mixed, logs), *others


def ffn_forward_in(middle, gain, wides, hidden_width):
    normed, inv_rms = norm_forward(middle, gain)
    got = swap_cores(normed)
    both = jnp.concatenate([normed, got], axis=0)
    gate_up = [product(both, wide) for wide in wides]
    gate = gate_up[0][:, :hidden_width]
    if gate_up[0].shape[1] > hidden_width:
        gate_up.insert(1, gate_up[0][:, hidden_width:])
    up = jnp.concatenate(gate_up[1:], axis=1)
    hidden = (jax.nn.silu(gate) * up).astype(bf16)
    return (middle, inv_rms, normed, got, gate, up, hidden)


def ffn_share(state, down):
    middle, hidden = state[0], state[-1]
    return own_share(cols_product(hidden, down), middle.shape[0]).astype(bf16)


def ffn_backward(own_grad, other_grad, state, wides, down, head, *others):
    middle, _, normed, got, gate, up, hidden = state
    hidden_grad = product(jnp.concatenate([own_grad, other_grad], axis=0), down)
    sigmoid_gate = jax.nn.sigmoid(gate)
    gate_grad = (hidden_grad * up * sigmoid_gate * (1.0 + gate * (1.0 - sigmoid_gate))).astype(bf16)
    up_grad = (hidden_grad * gate * sigmoid_gate).astype(bf16)
    units = gate.shape[1]
    if len(wides) == 1:
        partial = cols_product(jnp.concatenate([gate_grad, up_grad], axis=1), wides[0])
    else:
        partial = cols_product(gate_grad, wides[0]) + cols_product(up_grad, wides[1])
    normed_grad, *others = sum_tensor(own_share(partial, middle.shape[0]), *others)
    own_sides, norm_sides = (own_grad, other_grad), (normed, got)
    early = token_terms([own_sides, norm_sides], [(0, hidden, 0, units), (1, gate_grad, 0, head)])
    early = lax.psum_scatter(early, "ctx", scatter_dimension=0, tiled=True)
    late = token_terms([norm_sides], [(0, gate_grad, head, units - head), (0, up_grad, 0, units)])
    return normed_grad, early, late, *others


def ffn_backward_out(upstream, normed_grad, state, gain):
    mid_part, gain_term = norm_backward(state[0], state[1], gain, normed_grad.astype(f32))
    return upstream.astype(f32) + mid_part, gain_term


def attention_backward(mid_grad, saved, wide, place, *others):
    pos, tables, sizes = place
    _, _, normed, queries, tail, own, mixed, logs = saved
    query_grad, back, own_grad, mid_grad_b = mix_back(
        pos, queries, tail, own, mixed, logs, tables, mid_grad, wide[1], sizes[1]
    )
    back = from_behind(back, "ctx", -1)
    grads, partial = head_grads(query_grad, own_grad, back, tables, wide[0], sizes[1])
    normed_grad, *others = sum_tensor(partial, *others)
    terms = attention_terms(normed, mid_grad_b, grads, mixed, lax.axis_size("ctx"))
    core = lax.axis_index("pipe")
    mine = take(terms, core)
    theirs = take(terms, 1 - core)
    return normed_grad, add_bf16(mine, swap_cores(theirs)), *others


def attention_backward_out(mid_grad, normed_grad, saved, gain):
    part, gain_term = norm_backward(saved[0], saved[1], gain, normed_grad.astype(f32))
    return (mid_grad + part).astype(bf16), gain_term


def on_device(
    inputs,
    out_grad,
    positions,
    attn_gain,
    w_query,
    w_key,
    w_value,
    w_out,
    ffn_gain,
    w_gate,
    w_up,
    w_down,
):
    core = lax.axis_index("pipe")
    first = core == 0
    shard = lax.axis_index("ctx")
    rows = inputs.shape[1]
    width = inputs.shape[2]
    n_query = w_query.shape[2]
    n_key = w_key.shape[2]
    half = w_gate.shape[2] // 2

    def pick(pair, index):
        return take(pair, index)

    def mine_theirs(array, axis):
        size = array.shape[axis] // 2
        mine = lax.dynamic_slice_in_dim(
            array, core * size, size, axis, allow_negative_indices=False
        )
        theirs = lax.dynamic_slice_in_dim(
            array, (1 - core) * size, size, axis, allow_negative_indices=False
        )
        return mine, theirs

    count = lax.axis_size("ctx")
    gain_row = jnp.concatenate([attn_gain, ffn_gain], axis=1)
    attn_shard = jnp.concatenate([w_query[0], w_key[0], w_value[0], w_out[0].T], axis=1)
    wide_columns = attn_shard.shape[1]
    gain_rows = jnp.pad(gain_row, ((0, 15), (0, wide_columns - gain_row.shape[1])))
    rows_mine, rows_theirs = mine_theirs(attn_shard, 0)
    attn_keep = jnp.concatenate([rows_mine, gain_rows], axis=0)
    attn_got = swap_cores(jnp.concatenate([rows_theirs, gain_rows], axis=0))

    inner_columns = n_query + 2 * n_key

    def attn_weights(pieces):
        got = swap_cores(pieces)
        both = jnp.stack([jnp.where(first, pieces, got), jnp.where(first, got, pieces)], axis=1)
        part_rows = attn_shard.shape[0] // 2
        wide = both[:, :, :part_rows].reshape(width, wide_columns)
        wide = (wide[:, :inner_columns], wide[:, inner_columns:])
        row = pieces[:, part_rows, : gain_row.shape[1]].astype(f32)
        return wide, row.reshape(count, 2, -1).transpose(1, 0, 2).reshape(2, width)

    gate_mine, gate_theirs = mine_theirs(w_gate[0], 1)
    up_mine, up_theirs = mine_theirs(w_up[0], 1)
    wide_keep = jnp.concatenate([gate_mine, up_mine], axis=1)
    wide_got = swap_cores(jnp.concatenate([gate_theirs, up_theirs], axis=1))
    down_mine, down_theirs = mine_theirs(w_down[0], 0)
    down_keep, down_got = down_mine.T, swap_cores(down_theirs.T)

    def for_sections(keep, got):
        return [jnp.where(first, keep, got), jnp.where(first, got, keep)]

    def gather(shard_part):
        return lax.all_gather(shard_part, "ctx", axis=0, tiled=True)

    attn_parts = for_sections(attn_keep, attn_got)
    wide_parts = for_sections(wide_keep, wide_got)
    down_parts = for_sections(down_keep, down_got)
    tail_columns = 3 * half // 8
    wide_low = lax.all_gather(
        wide_parts[0][:, :-tail_columns], ("pipe", "ctx"), axis=0, tiled=True
    )
    down_parts[0] = jnp.concatenate([down_parts[0], wide_parts[0][:, -tail_columns:]], axis=1)
    attn_pieces, attn_parts[1], wide_parts[1], *down_parts = pin(
        ring_gather(*ring_gather_start(attn_parts[0])), attn_parts[1], wide_parts[1], *down_parts
    )
    attn_low, gains_low = attn_weights(attn_pieces)
    down_and_tail = gather(down_parts[0])
    ring_columns = 3 * wide_parts[1].shape[1] // 8
    wide_high = gather(wide_parts[1][:, :-ring_columns])
    down_high = gather(down_parts[1])

    pos_row = pick(positions, core)
    place = (pos_row[:, None], rope_tables(pos_row, HEAD_DIM), (n_query, n_key))

    def scatter(terms):
        return lax.psum_scatter(terms, "ctx", scatter_dimension=0, tiled=True)

    def give_low(share):
        return lax.ppermute(share, "pipe", [(1, 0)])

    def give_high(share):
        return lax.ppermute(share, "pipe", [(0, 1)])

    stream = pick(inputs, core)
    total, attn_saved_low, wide_low, attn_part_high = attention_forward(
        stream, gains_low[0], attn_low, place, wide_low, attn_parts[1]
    )
    wide_low = pick(wide_low.reshape(2, width, -1), core)
    total, wide_low = pin(total, wide_low)
    middle = attn_saved_low[0] + total.astype(f32)
    down_low, wide_tail = down_and_tail[:, :half], down_and_tail[:, half:]
    state_low = ffn_forward_in(middle, gains_low[1], [wide_low, wide_tail], half)
    own_grad, other_grad = pick(out_grad, core), pick(out_grad, 1 - core)
    total, attn_part_high = sum_tensor(ffn_share(state_low, down_low), attn_part_high)
    attn_ring = ring_gather_start(attn_part_high)
    wide_low = jnp.concatenate([wide_low, wide_tail], axis=1)
    total, own_grad, other_grad, (attn_high, gains_high), wide_low = pin(
        total, own_grad, other_grad, attn_weights(ring_gather(*attn_ring)), wide_low
    )
    out_low = (middle + total.astype(f32)).astype(bf16)
    total, attn_saved_high, wide_high, wide_part_high = attention_forward(
        out_low, gains_high[0], attn_high, place, wide_high, wide_parts[1][:, -ring_columns:]
    )
    wide_ring = ring_gather_start(wide_part_high)
    up_high = jnp.concatenate(
        [wide_high[:, half:], ring_gather(*wide_ring).reshape(width, ring_columns)], axis=1
    )
    wide_high = [wide_high[:, :half], up_high]
    total, got_out_low, wide_high = pin(total, swap_cores(out_low), wide_high)
    middle = attn_saved_high[0] + total.astype(f32)
    state_high = ffn_forward_in(middle, gains_high[1], wide_high, half)

    gate, up, down_high = pin(state_high[4], state_high[5], down_high)
    hidden = (jax.nn.silu(gate) * up).astype(bf16)
    state_high = (*state_high[:4], gate, up, hidden)
    normed_grad, early_high, late_high = ffn_backward(
        own_grad, other_grad, state_high, wide_high, down_high, half // 2
    )
    normed_grad, late_high = pin(normed_grad, late_high)
    mid_grad, ffn_gain_high = ffn_backward_out(own_grad, normed_grad, state_high, gains_high[1])
    late_high = scatter(late_high)
    normed_grad, summed, early_high = attention_backward(
        mid_grad, attn_saved_high, attn_high, place, early_high
    )
    normed_grad, attn_ring, out_share = pin(
        normed_grad, ring_scatter_start(summed), ffn_share(state_high, down_high)
    )
    boundary_high, attn_gain_high = attention_backward_out(
        mid_grad, normed_grad, attn_saved_high, gains_high[0]
    )
    got_boundary_high = swap_cores(boundary_high)
    normed_grad, early_low, late_low, late_high = ffn_backward(
        boundary_high, got_boundary_high, state_low, [wide_low], down_low, half // 4, late_high
    )
    normed_grad, late_low, attn_share_high = pin(normed_grad, late_low, ring_scatter(*attn_ring))
    mid_grad, ffn_gain_low = ffn_backward_out(
        boundary_high, normed_grad, state_low, gains_low[1]
    )
    late_low = scatter(late_low)
    normed_grad, summed, early_low = attention_backward(
        mid_grad, attn_saved_low, attn_low, place, early_low
    )
    def from_other(low, high):
        return swap_cores(jnp.where(first, high, low))

    (total,) = sum_tensor(out_share)
    attn_pair = (ring_scatter(*ring_scatter_start(summed)), attn_share_high)
    attn_outs = attention_outputs(core, *attn_pair, from_other(*attn_pair), (n_query, n_key))
    early = (early_low, early_high, give_low(early_low), give_high(early_high))
    down_out = down_outputs(core, early, half)
    normed_grad, down_out, attn_outs, got_late_high = pin(
        normed_grad, down_out, attn_outs, give_high(late_high)
    )
    out_high = (middle + total.astype(f32)).astype(bf16)

    boundary_low, attn_gain_low = attention_backward_out(
        mid_grad, normed_grad, attn_saved_low, gains_low[0]
    )
    gains_out = share_gains(
        jnp.stack(
            [jnp.stack([attn_gain_low, ffn_gain_low]), jnp.stack([attn_gain_high, ffn_gain_high])]
        )
    )
    late_low, gains_out, got_out_high, got_boundary_low = pin(
        late_low, gains_out, swap_cores(out_high), swap_cores(boundary_low)
    )
    outs = (out_low, out_high, got_out_low, got_out_high)
    boundaries = (boundary_low, boundary_high, got_boundary_low, got_boundary_high)
    section_outputs, boundary_grads = section_stacks(core, *outs, *boundaries)
    late = (late_low, late_high, give_low(late_low), got_late_high)
    gate_out, up_out = wide_outputs(core, early, late, half)
    query_out, key_out, value_out, attn_out = attn_outs
    return (
        section_outputs[None],
        boundary_grads[None],
        gains_out[:1],
        query_out[None],
        key_out[None],
        value_out[None],
        attn_out[None],
        gains_out[1:],
        gate_out[None],
        up_out[None],
        down_out[None],
    )


def solution(mesh):
    in_specs = (
        P(None, "ctx", None),
        P(None, "ctx", None),
        P(None, "ctx"),
        P("pipe", "ctx"),
        P("pipe", "ctx", "tensor"),
        P("pipe", "ctx", "tensor"),
        P("pipe", "ctx", "tensor"),
        P("pipe", "tensor", "ctx"),
        P("pipe", "ctx"),
        P("pipe", "ctx", "tensor"),
        P("pipe", "ctx", "tensor"),
        P("pipe", "tensor", "ctx"),
    )
    out_specs = (
        P("pipe", None, "ctx", None),
        P("pipe", None, "ctx", None),
        P("pipe", "ctx"),
        P("pipe", "ctx", "tensor"),
        P("pipe", "ctx", "tensor"),
        P("pipe", "ctx", "tensor"),
        P("pipe", "tensor", "ctx"),
        P("pipe", "ctx"),
        P("pipe", "ctx", "tensor"),
        P("pipe", "ctx", "tensor"),
        P("pipe", "tensor", "ctx"),
    )
    return jax.shard_map(
        on_device, mesh=mesh, in_specs=in_specs, out_specs=out_specs, check_vma=False
    )
```

```python
import functools
import math

import jax
import jax.numpy as jnp
from jax import lax
from jax.experimental import pallas as pl
from jax.experimental.pallas import tpu as pltpu
from jax.sharding import PartitionSpec as P

HEADS = 32
KV_HEADS = 8
HEAD_DIM = 64
MAXLEN = 256

epsilon = 1e-05
rope_base = 500000.0
bf16 = jnp.bfloat16
f32 = jnp.float32


def swap_cores(block):
    return lax.ppermute(block, "pipe", [(0, 1), (1, 0)])


def from_behind(block, axis, distance):
    devices = range(lax.axis_size(axis))
    route = [(i - distance, i) for i in devices if i - distance in devices]
    return lax.ppermute(block, axis, route)


def ring_order(count):
    across = 1 << (count.bit_length() - 1) // 2
    down = count // across
    walk = [(0, x) for x in range(across)]
    for y in range(1, down):
        columns = range(1, across)
        walk += [(y, x) for x in (columns if y % 2 == 0 else reversed(columns))]
    walk += [(y, 0) for y in range(down - 1, 0, -1)]
    return [y * across + x for y, x in walk]


def take(array, index, axis=0):
    return lax.dynamic_index_in_dim(
        array, index, axis, keepdims=False, allow_negative_indices=False
    )


def ring_tools():
    count = lax.axis_size("ctx")
    order = ring_order(count)
    ahead = [(order[i], order[(i + 1) % count]) for i in range(count)]
    behind = [(b, a) for a, b in ahead]
    device = lax.axis_index("ctx")

    def device_at(distance):
        if order == [0, 1, 3, 2]:
            place = ((device ^ (device >> 1)) + distance % count) & 3
            return place ^ (place >> 1)
        place = jnp.asarray([order.index(i) for i in range(count)], jnp.int32)
        return take(jnp.asarray(order * 2, jnp.int32), take(place, device) + distance % count)

    return count, ahead, behind, device_at


def ring_gather_start(block):
    count, ahead, behind, _ = ring_tools()
    from_back, from_front = [block], [block]
    for _ in range(1, count // 2):
        from_back.append(lax.ppermute(from_back[-1], "ctx", ahead))
        from_front.append(lax.ppermute(from_front[-1], "ctx", behind))
    return from_back, from_front


def ring_gather(from_back, from_front):
    count, ahead, behind, device_at = ring_tools()
    block = from_back[0]
    half = block.shape[1] // 2
    left = lax.ppermute(from_back[-1][:, :half], "ctx", ahead)
    right = lax.ppermute(from_front[-1][:, half:], "ctx", behind)
    out = jnp.zeros((count,) + block.shape, block.dtype)

    def put(out, piece, distance, column=0):
        return lax.dynamic_update_slice(
            out, piece[None], (device_at(distance), 0, column), allow_negative_indices=False
        )

    out = put(out, block, 0)
    for distance in range(1, count // 2):
        out = put(out, from_back[distance], -distance)
        out = put(out, from_front[distance], distance)
    out = put(out, left, count // 2)
    return put(out, right, count // 2, half)


def ring_term(terms, distance):
    return take(terms, ring_tools()[3](distance))


def ring_scatter_start(terms):
    count, ahead, behind, _ = ring_tools()
    half = terms.shape[2] // 2
    far = ring_term(terms, count // 2)
    to_front = lax.ppermute(far[:, :half], "ctx", ahead)
    to_back = lax.ppermute(far[:, half:], "ctx", behind)
    for distance in range(count // 2 - 1, 0, -1):
        front, back = ring_term(terms, distance), ring_term(terms, -distance)
        if distance == count // 2 - 1:
            front = jnp.concatenate([add_bf16(front[:, :half], to_front), front[:, half:]], axis=1)
            back = jnp.concatenate([back[:, :half], add_bf16(back[:, half:], to_back)], axis=1)
        else:
            front, back = add_bf16(front, to_front), add_bf16(back, to_back)
        if distance > 1:
            front = lax.ppermute(front, "ctx", ahead)
            back = lax.ppermute(back, "ctx", behind)
        to_front, to_back = front, back
    return ring_term(terms, 0), to_front, to_back


def ring_scatter(own, to_front, to_back):
    _, ahead, behind, _ = ring_tools()
    from_back = lax.ppermute(to_front, "ctx", ahead)
    from_front = lax.ppermute(to_back, "ctx", behind)
    return (own.astype(f32) + from_back.astype(f32) + from_front.astype(f32)).astype(bf16)


def add_bf16(a, b):
    return (a.astype(f32) + b.astype(f32)).astype(bf16)


def params(megabytes=24):
    return pltpu.CompilerParams(vmem_limit_bytes=megabytes * 2**20)


def cost(flops, bytes_accessed, transcendentals=0):
    return pl.CostEstimate(
        flops=flops, bytes_accessed=bytes_accessed, transcendentals=transcendentals
    )


def token_terms_kernel(plan, *refs):
    out_ref = refs[-1]
    lefts, rights = refs[: -1 - len(plan)], refs[-1 - len(plan) : -1]
    rows = (((0,), (0,)), ((), ()))
    column = 0
    for (left, start, columns), right_ref in zip(plan, rights):
        own, got = lefts[2 * left], lefts[2 * left + 1]
        half, part = own.shape[0], slice(start, start + columns)
        total = lax.dot_general(own[...], right_ref[:half, part], rows, preferred_element_type=f32)
        total += lax.dot_general(got[...], right_ref[half:, part], rows, preferred_element_type=f32)
        out_ref[:, column : column + columns] = total.astype(bf16)
        column += columns


def token_terms(lefts, rights):
    tokens, width = lefts[0][0].shape
    tile = 512
    columns = sum(right[3] for right in rights)
    side = pl.BlockSpec((tokens, tile), lambda i: (0, i))
    arrays = [right[1] for right in rights]
    plan = [(right[0], right[2], right[3]) for right in rights]
    return pl.pallas_call(
        functools.partial(token_terms_kernel, plan),
        grid=(width // tile,),
        in_specs=[side] * (2 * len(lefts))
        + [pl.BlockSpec(array.shape, lambda i: (0, 0)) for array in arrays],
        out_specs=pl.BlockSpec((tile, columns), lambda i: (i, 0)),
        out_shape=jax.ShapeDtypeStruct((width, columns), bf16),
        compiler_params=params(58),
        cost_estimate=cost(
            4 * tokens * width * columns,
            2 * (width * columns + 2 * tokens * width * len(lefts) + 2 * tokens * columns),
        ),
        name="token_terms",
    )(*(array for pair in lefts for array in pair), *arrays)


def attention_terms_kernel(normed_ref, mid_grad_ref, grads_ref, mixed_ref, out_ref):
    n_grads = grads_ref.shape[1]
    half = out_ref.shape[1]
    rows = (((0,), (0,)), ((), ()))
    inner = lax.dot_general(normed_ref[...], grads_ref[...], rows, preferred_element_type=f32)
    outer = lax.dot_general(mid_grad_ref[...], mixed_ref[...], rows, preferred_element_type=f32)
    for part in range(2):
        part_rows = slice(part * half, (part + 1) * half)
        out_ref[part, :, :n_grads] = inner[part_rows].astype(bf16)
        out_ref[part, :, n_grads:] = outer[part_rows].astype(bf16)


def attention_terms(normed, mid_grad, grads, mixed, count):
    tokens, width = normed.shape
    columns = grads.shape[1] + mixed.shape[1]
    tile = width // count
    return pl.pallas_call(
        attention_terms_kernel,
        grid=(count,),
        in_specs=[
            pl.BlockSpec((tokens, tile), lambda i: (0, i)),
            pl.BlockSpec((tokens, tile), lambda i: (0, i)),
            pl.BlockSpec((tokens, grads.shape[1]), lambda i: (0, 0)),
            pl.BlockSpec((tokens, mixed.shape[1]), lambda i: (0, 0)),
        ],
        out_specs=pl.BlockSpec((2, None, tile // 2, columns), lambda i: (0, i, 0, 0)),
        out_shape=jax.ShapeDtypeStruct((2, count, tile // 2, columns), bf16),
        compiler_params=params(),
        cost_estimate=pl.CostEstimate(
            flops=2 * tokens * width * columns,
            bytes_accessed=2 * (width * columns + 2 * tokens * width + tokens * columns),
            transcendentals=0,
        ),
        name="attention_terms",
    )(normed, mid_grad, grads, mixed)


def section_stacks_kernel(core_ref, *refs):
    first = core_ref[0] == 0
    for sources, target in ((refs[:4], refs[8]), (refs[4:8], refs[9])):
        low, high, got_low, got_high = (source[...] for source in sources)
        keep, got = jnp.where(first, low, high), jnp.where(first, got_low, got_high)
        target[...] = jnp.where(core_ref[0] == pl.program_id(0), keep, got)


def section_stacks(core, *sources):
    rows, width = sources[0].shape
    block = pl.BlockSpec((rows, width), lambda i, core: (0, 0))
    return pl.pallas_call(
        section_stacks_kernel,
        grid_spec=pltpu.PrefetchScalarGridSpec(
            num_scalar_prefetch=1,
            grid=(2,),
            in_specs=[block] * 8,
            out_specs=[pl.BlockSpec((None, rows, width), lambda i, core: (i, 0, 0))] * 2,
        ),
        out_shape=[jax.ShapeDtypeStruct((2, rows, width), bf16)] * 2,
        compiler_params=params(40),
        cost_estimate=cost(0, 12 * rows * width * 2),
        name="section_stacks",
    )(core.reshape(1), *sources)


def attention_outputs_kernel(core_ref, low_ref, high_ref, got_ref, query_ref, key_ref, value_ref, out_ref):
    first = core_ref[0] == 0
    keep = jnp.where(first, low_ref[...], high_ref[...])
    got = got_ref[...]
    parts = [jnp.where(first == (side == 0), keep, got).astype(f32) for side in range(2)]
    whole = jnp.concatenate(parts, axis=0)
    column = 0
    for ref in (query_ref, key_ref, value_ref):
        ref[...] = whole[:, column : column + ref.shape[1]]
        column += ref.shape[1]
    out_ref[...] = whole[:, column:].T


def attention_outputs(core, low, high, got, sizes):
    n_query, n_key = sizes
    rows, columns = got.shape
    whole = lambda *shape: pl.BlockSpec(shape, lambda i, core: (0, 0))
    shapes = [(2 * rows, n_query), (2 * rows, n_key), (2 * rows, n_key), (n_query, 2 * rows)]
    return pl.pallas_call(
        attention_outputs_kernel,
        grid_spec=pltpu.PrefetchScalarGridSpec(
            num_scalar_prefetch=1,
            grid=(1,),
            in_specs=[whole(rows, columns)] * 3,
            out_specs=[whole(*shape) for shape in shapes],
        ),
        out_shape=[jax.ShapeDtypeStruct(shape, f32) for shape in shapes],
        compiler_params=params(),
        cost_estimate=cost(0, rows * columns * 14),
        name="attention_outputs",
    )(core.reshape(1), low, high, got)


def wide_outputs_kernel(columns, core_ref, *refs):
    first = core_ref[0] == 0
    gate_ref, up_ref = refs[8:]
    sections = []
    for place in range(4):
        early, late = refs[place][...], refs[4 + place][...]
        head = columns[place % 2]
        rest = gate_ref.shape[1] // 2 - head
        gate = jnp.concatenate([early, late[:, :rest]], axis=1)
        sections.append((gate, late[:, rest:]))
    low, high, got_low, got_high = sections
    for target, part in ((gate_ref, 0), (up_ref, 1)):
        units = target.shape[1] // 2
        keep = jnp.where(first, low[part], high[part])
        got = jnp.where(first, got_low[part], got_high[part])
        target[:, :units] = jnp.where(first, keep, got).astype(f32)
        target[:, units:] = jnp.where(first, got, keep).astype(f32)


def wide_outputs(core, early, late, units):
    rows = early[0].shape[0]
    columns = [share.shape[1] - units for share in early[:2]]
    tile = 128

    def early_spec(head):
        return pl.BlockSpec((tile, head), lambda i, core: (i, units // head))

    return pl.pallas_call(
        functools.partial(wide_outputs_kernel, columns),
        grid_spec=pltpu.PrefetchScalarGridSpec(
            num_scalar_prefetch=1,
            grid=(rows // tile,),
            in_specs=[early_spec(head) for head in columns * 2]
            + [pl.BlockSpec((tile, share.shape[1]), lambda i, core: (i, 0)) for share in late],
            out_specs=[pl.BlockSpec((tile, 2 * units), lambda i, core: (i, 0))] * 2,
        ),
        out_shape=[jax.ShapeDtypeStruct((rows, 2 * units), f32)] * 2,
        compiler_params=params(),
        cost_estimate=cost(0, rows * 32 * units),
        name="wide_outputs",
    )(core.reshape(1), *early, *late)


def down_outputs_kernel(core_ref, low_ref, high_ref, got_low_ref, got_high_ref, down_ref):
    first = core_ref[0] == 0
    units = low_ref.shape[1]
    keep = jnp.where(first, low_ref[...], high_ref[...])
    got = jnp.where(first, got_low_ref[...], got_high_ref[...])
    for side in range(2):
        part = jnp.where(first == (side == 0), keep, got).astype(f32)
        down_ref[side * units : (side + 1) * units, :] = part.T


def down_outputs(core, early, units):
    rows = early[0].shape[0]
    tile = 128
    return pl.pallas_call(
        down_outputs_kernel,
        grid_spec=pltpu.PrefetchScalarGridSpec(
            num_scalar_prefetch=1,
            grid=(rows // tile,),
            in_specs=[pl.BlockSpec((tile, units), lambda i, core: (i, 0))] * 4,
            out_specs=pl.BlockSpec((2 * units, tile), lambda i, core: (0, i)),
        ),
        out_shape=jax.ShapeDtypeStruct((2 * units, rows), f32),
        compiler_params=params(),
        cost_estimate=cost(0, rows * units * 16),
        name="down_outputs",
    )(core.reshape(1), *early)


def pin(value, *others):
    return lax.optimization_barrier((value, *others))


def share_gains(terms):
    core, shard = lax.axis_index("pipe"), lax.axis_index("ctx")
    count = lax.axis_size("ctx")
    own = take(terms, core)
    other = take(terms, 1 - core)
    total = own + swap_cores(other)
    blocks = total.reshape(2, count, -1)

    def block(index):
        return take(blocks, index, 1)

    result = block(shard)
    for step in range(1, count):
        route = [(i, i ^ step) for i in range(count)]
        result = result + lax.ppermute(block(shard ^ step), "ctx", route)
    return result


def product(left, right):
    return lax.dot_general(
        left, right, (((1,), (0,)), ((), ())), preferred_element_type=f32
    )


def rows_product(left, right):
    return lax.dot_general(
        left, right, (((0,), (0,)), ((), ())), preferred_element_type=f32
    )


def cols_product(left, right):
    return lax.dot_general(
        left, right, (((1,), (1,)), ((), ())), preferred_element_type=f32
    )


def norm_forward(stream, gain_vector):
    inv_rms = lax.rsqrt(jnp.mean(stream * stream, axis=-1) + epsilon)
    return ((stream * inv_rms[:, None] * gain_vector[None, :]).astype(bf16), inv_rms)


def norm_backward(stream, inv_rms, gain_vector, upstream):
    weighted = upstream * gain_vector[None, :]
    gain_grad = jnp.sum(upstream * stream * inv_rms[:, None], axis=0)
    inner_mean = jnp.mean(stream * weighted, axis=-1)
    stream_grad = (
        weighted * inv_rms[:, None] - stream * (inv_rms * inv_rms * inv_rms * inner_mean)[:, None]
    )
    return (stream_grad, gain_grad)


def sum_tensor(partial, *others):
    partial = partial.astype(bf16)
    if others:
        partial, *others = pin(partial, *others)
    return lax.psum(partial, "tensor"), *others


def own_share(partial, rows):
    arrived = swap_cores(partial[rows:].astype(bf16))
    return partial[:rows] + arrived.astype(f32)


def half_swap(values):
    lanes = lax.broadcasted_iota(jnp.int32, values.shape, 1)
    count = values.shape[1]
    quarter = HEAD_DIM // 2
    return jnp.where(
        lanes % HEAD_DIM < quarter,
        pltpu.roll(values, count - quarter, 1),
        pltpu.roll(values, quarter, 1),
    )


def wide_table(table, columns):
    return jnp.concatenate([table] * (columns // table.shape[1]), axis=1)


def rope_tables(positions_row, width):
    frequency = jnp.exp(
        jnp.arange(width // 2, dtype=f32) * (-2.0 * math.log(rope_base) / width)
    )
    angles = positions_row.astype(f32)[:, None] * frequency[None, :]
    cosine, sine = jnp.cos(angles), jnp.sin(angles)
    return (
        jnp.concatenate([cosine] * 4, axis=1),
        jnp.concatenate([-sine, sine] * 2, axis=1),
    )


def head_inputs_kernel(sizes, stream_ref, gain_ref, wide_ref, cos_ref, sin_ref,
                       normed_ref, rms_ref, query_ref, own_ref):
    n_query, n_key = sizes
    stream = stream_ref[...].astype(f32)
    inv_rms = lax.rsqrt(jnp.mean(stream * stream, axis=1, keepdims=True) + epsilon)
    normed = (stream * inv_rms * gain_ref[...]).astype(bf16)
    normed_ref[...] = normed
    rms_ref[...] = inv_rms
    raw = jnp.dot(normed, wide_ref[...], preferred_element_type=f32)
    turned = raw[:, : n_query + n_key]
    cosine = wide_table(cos_ref[...], n_query + n_key)
    sine = wide_table(sin_ref[...], n_query + n_key)
    turned = turned * cosine + half_swap(turned) * sine
    query_ref[...] = turned[:, :n_query].astype(bf16)
    own_ref[:, :n_key] = turned[:, n_query:].astype(bf16)
    own_ref[:, n_key:] = raw[:, n_query + n_key :].astype(bf16)


def head_inputs(stream, gain, wide, tables, sizes):
    n_query, n_key = sizes
    rows, width = stream.shape
    columns = n_query + 2 * n_key
    whole = lambda *shape: pl.BlockSpec(shape, lambda i: (0,) * len(shape))
    return pl.pallas_call(
        functools.partial(head_inputs_kernel, sizes),
        grid=(1,),
        in_specs=[
            whole(rows, width),
            whole(1, width),
            whole(width, columns),
            whole(rows, 2 * HEAD_DIM),
            whole(rows, 2 * HEAD_DIM),
        ],
        out_specs=[whole(rows, width), whole(rows, 1), whole(rows, n_query), whole(rows, 2 * n_key)],
        out_shape=[
            jax.ShapeDtypeStruct((rows, width), bf16),
            jax.ShapeDtypeStruct((rows, 1), f32),
            jax.ShapeDtypeStruct((rows, n_query), bf16),
            jax.ShapeDtypeStruct((rows, 2 * n_key), bf16),
        ],
        compiler_params=params(),
        cost_estimate=cost(2 * rows * width * columns, 2 * width * (columns + 4 * rows)),
        name="head_inputs",
    )(stream, gain[None], wide, *tables)


def masked_scores(query, keys, allowed):
    raw = lax.dot_general(query, keys, (((1,), (1,)), ((), ())), preferred_element_type=f32)
    return jnp.where(allowed, raw * HEAD_DIM ** (-0.5), -1e30)


def allowed_pairs(pos, rows):
    distance = (
        lax.broadcasted_iota(jnp.int32, (rows, 2 * rows), 0)
        - lax.broadcasted_iota(jnp.int32, (rows, 2 * rows), 1)
        + rows
    )
    return (distance >= 0) & (distance <= pos)


def head_slice(index):
    return slice(index * HEAD_DIM, (index + 1) * HEAD_DIM)


def mix_kernel(n_key, pos_ref, query_ref, tail_ref, own_ref, wide_ref,
               mixed_ref, log_ref, partial_ref, window, mixed_all):
    rows, n_query = query_ref.shape

    @pl.when(pl.program_id(0) == 0)
    def _():
        window[:rows] = tail_ref[...]
        window[rows:] = own_ref[...]
        allowed = allowed_pairs(pos_ref[...], rows)
        group = HEADS // KV_HEADS
        logs, mixed = [], []
        for head in range(n_query // HEAD_DIM):
            keys = window[:, head_slice(head // group)]
            values = window[:, head_slice((n_key // HEAD_DIM) + head // group)]
            masked = masked_scores(query_ref[:, head_slice(head)], keys, allowed)
            top = jnp.max(masked, axis=1, keepdims=True)
            exponent = jnp.exp(masked - top)
            total = jnp.sum(exponent, axis=1, keepdims=True)
            weights = (exponent * (1.0 / total)).astype(bf16)
            mixed.append(jnp.dot(weights, values, preferred_element_type=f32).astype(bf16))
            logs.append(top + jnp.log(total))
        everything = jnp.concatenate(mixed, axis=1)
        mixed_all[...] = everything
        mixed_ref[...] = everything
        log_ref[...] = jnp.concatenate(logs, axis=1)

    partial_ref[...] = lax.dot_general(
        mixed_all[...],
        wide_ref[...],
        (((1,), (1,)), ((), ())),
        preferred_element_type=f32,
    ).astype(bf16)


def mix(pos, queries, tail, own, wide, n_key):
    rows, n_query = queries.shape
    width, columns = wide.shape
    tile = 512
    heads = n_query // HEAD_DIM
    whole = lambda *shape: pl.BlockSpec(shape, lambda i: (0,) * len(shape))
    return pl.pallas_call(
        functools.partial(mix_kernel, n_key),
        grid=(width // tile,),
        in_specs=[
            whole(rows, 1),
            whole(rows, n_query),
            whole(rows, 2 * n_key),
            whole(rows, 2 * n_key),
            pl.BlockSpec((tile, columns), lambda i: (i, 0)),
        ],
        out_specs=[
            whole(rows, n_query),
            whole(rows, heads),
            pl.BlockSpec((rows, tile), lambda i: (0, i)),
        ],
        out_shape=[
            jax.ShapeDtypeStruct((rows, n_query), bf16),
            jax.ShapeDtypeStruct((rows, heads), f32),
            jax.ShapeDtypeStruct((rows, width), bf16),
        ],
        scratch_shapes=[pltpu.VMEM((2 * rows, 2 * n_key), bf16), pltpu.VMEM((rows, n_query), bf16)],
        compiler_params=params(),
        cost_estimate=cost(
            2 * rows * n_query * (width + 4 * rows), 2 * width * (columns + rows), 2 * rows * rows * heads
        ),
        name="mix",
    )(pos, queries, tail, own, wide)


def mix_back_kernel(n_key, pos_ref, query_ref, tail_ref, own_ref, mixed_ref, log_ref, cos_ref, sin_ref,
                    mid_grad_ref, wide_ref, query_grad_ref, back_ref, own_grad_ref, mid_b_ref,
                    window, mixed_grad):
    rows, n_query = query_ref.shape
    step = pl.program_id(0)
    mid_b = mid_grad_ref[...].astype(bf16)
    mid_b_ref[...] = mid_b
    part = jnp.dot(mid_b, wide_ref[...], preferred_element_type=f32)

    @pl.when(step == 0)
    def _():
        mixed_grad[...] = part

    @pl.when(step > 0)
    def _():
        mixed_grad[...] += part

    @pl.when(step == pl.num_programs(0) - 1)
    def _():
        window[:rows] = tail_ref[...]
        window[rows:] = own_ref[...]
        allowed = allowed_pairs(pos_ref[...], rows)
        group = HEADS // KV_HEADS
        groups = n_key // HEAD_DIM
        scale = HEAD_DIM ** (-0.5)
        grads = mixed_grad[...].astype(bf16)
        over_rows = (((0,), (0,)), ((), ()))
        over_columns = (((1,), (1,)), ((), ()))
        query_grads, key_grads, value_grads = [], [None] * groups, [None] * groups
        for head in range(n_query // HEAD_DIM):
            at = head // group
            keys = window[:, head_slice(at)]
            values = window[:, head_slice(groups + at)]
            query = query_ref[:, head_slice(head)]
            grad = grads[:, head_slice(head)]
            masked = masked_scores(query, keys, allowed)
            prob = jnp.exp(masked - log_ref[:, head : head + 1])
            prob_grad = lax.dot_general(grad, values, over_columns, preferred_element_type=f32)
            delta = jnp.sum(
                grad.astype(f32) * mixed_ref[:, head_slice(head)].astype(f32), axis=1, keepdims=True
            )
            score_grad = (prob * (prob_grad - delta)).astype(bf16)
            query_grads.append(jnp.dot(score_grad, keys, preferred_element_type=f32))
            key_part = lax.dot_general(score_grad, query, over_rows, preferred_element_type=f32)
            value_part = lax.dot_general(
                prob.astype(bf16), grad, over_rows, preferred_element_type=f32
            )
            key_grads[at] = key_part if key_grads[at] is None else key_grads[at] + key_part
            value_grads[at] = value_part if value_grads[at] is None else value_grads[at] + value_part
        query_grad = jnp.concatenate(query_grads, axis=1) * scale
        query_grad = query_grad * wide_table(cos_ref[...], n_query) - half_swap(
            query_grad
        ) * wide_table(sin_ref[...], n_query)
        query_grad_ref[...] = query_grad.astype(bf16)
        key_grad = jnp.concatenate(key_grads, axis=1) * scale
        value_grad = jnp.concatenate(value_grads, axis=1)
        back_ref[:, :n_key] = key_grad[:rows].astype(bf16)
        back_ref[:, n_key:] = value_grad[:rows].astype(bf16)
        own_grad_ref[:, :n_key] = key_grad[rows:]
        own_grad_ref[:, n_key:] = value_grad[rows:]


def mix_back(pos, queries, tail, own, mixed, logs, tables, mid_grad, wide, n_key):
    rows, n_query = queries.shape
    width, columns = wide.shape
    tile = 512
    heads = n_query // HEAD_DIM
    whole = lambda *shape: pl.BlockSpec(shape, lambda i: (0,) * len(shape))
    return pl.pallas_call(
        functools.partial(mix_back_kernel, n_key),
        grid=(width // tile,),
        in_specs=[
            whole(rows, 1),
            whole(rows, n_query),
            whole(rows, 2 * n_key),
            whole(rows, 2 * n_key),
            whole(rows, n_query),
            whole(rows, heads),
            whole(rows, 2 * HEAD_DIM),
            whole(rows, 2 * HEAD_DIM),
            pl.BlockSpec((rows, tile), lambda i: (0, i)),
            pl.BlockSpec((tile, columns), lambda i: (i, 0)),
        ],
        out_specs=[
            whole(rows, n_query),
            whole(rows, 2 * n_key),
            whole(rows, 2 * n_key),
            pl.BlockSpec((rows, tile), lambda i: (0, i)),
        ],
        out_shape=[
            jax.ShapeDtypeStruct((rows, n_query), bf16),
            jax.ShapeDtypeStruct((rows, 2 * n_key), bf16),
            jax.ShapeDtypeStruct((rows, 2 * n_key), f32),
            jax.ShapeDtypeStruct((rows, width), bf16),
        ],
        scratch_shapes=[pltpu.VMEM((2 * rows, 2 * n_key), bf16), pltpu.VMEM((rows, n_query), f32)],
        compiler_params=params(),
        cost_estimate=cost(
            2 * rows * n_query * (width + 10 * rows), 2 * width * (columns + 3 * rows), 2 * rows * rows * heads
        ),
        name="mix_back",
    )(pos, queries, tail, own, mixed, logs, *tables, mid_grad, wide)


def head_grads_kernel(n_key, query_grad_ref, own_grad_ref, back_ref, cos_ref, sin_ref, wide_ref,
                      grads_ref, partial_ref, grads):
    n_query = query_grad_ref.shape[1]

    @pl.when(pl.program_id(0) == 0)
    def _():
        own = own_grad_ref[...] + back_ref[...].astype(f32)
        keys = own[:, :n_key]
        keys = keys * wide_table(cos_ref[...], n_key) - half_swap(keys) * wide_table(
            sin_ref[...], n_key
        )
        grads[:, :n_query] = query_grad_ref[...]
        grads[:, n_query : n_query + n_key] = keys.astype(bf16)
        grads[:, n_query + n_key :] = own[:, n_key:].astype(bf16)
        grads_ref[...] = grads[...]

    partial_ref[...] = lax.dot_general(
        grads[...], wide_ref[...], (((1,), (1,)), ((), ())), preferred_element_type=f32
    ).astype(bf16)


def head_grads(query_grad, own_grad, back, tables, wide, n_key):
    rows, n_query = query_grad.shape
    width = wide.shape[0]
    columns = n_query + 2 * n_key
    tile = 512
    whole = lambda *shape: pl.BlockSpec(shape, lambda i: (0,) * len(shape))
    return pl.pallas_call(
        functools.partial(head_grads_kernel, n_key),
        grid=(width // tile,),
        in_specs=[
            whole(rows, n_query),
            whole(rows, 2 * n_key),
            whole(rows, 2 * n_key),
            whole(rows, 2 * HEAD_DIM),
            whole(rows, 2 * HEAD_DIM),
            pl.BlockSpec((tile, columns), lambda i: (i, 0)),
        ],
        out_specs=[whole(rows, columns), pl.BlockSpec((rows, tile), lambda i: (0, i))],
        out_shape=[
            jax.ShapeDtypeStruct((rows, columns), bf16),
            jax.ShapeDtypeStruct((rows, width), bf16),
        ],
        scratch_shapes=[pltpu.VMEM((rows, columns), bf16)],
        compiler_params=params(),
        cost_estimate=cost(2 * rows * width * columns, 2 * width * (columns + rows)),
        name="head_grads",
    )(query_grad, own_grad, back, *tables, wide)


def attention_forward(stream, gain, wide, place, *others):
    pos, tables, sizes = place
    normed, inv_rms, queries, own = head_inputs(stream, gain, wide[0], tables, sizes)
    tail = from_behind(own, "ctx", 1)
    mixed, logs, partial = mix(pos, queries, tail, own, wide[1], sizes[1])
    total, *others = sum_tensor(partial, *others)
    return total, (stream.astype(f32), inv_rms[:, 0], normed, queries, tail, own, mixed, logs), *others


def ffn_forward_in(middle, gain, wides, hidden_width):
    normed, inv_rms = norm_forward(middle, gain)
    got = swap_cores(normed)
    both = jnp.concatenate([normed, got], axis=0)
    gate_up = [product(both, wide) for wide in wides]
    gate = gate_up[0][:, :hidden_width]
    if gate_up[0].shape[1] > hidden_width:
        gate_up.insert(1, gate_up[0][:, hidden_width:])
    up = jnp.concatenate(gate_up[1:], axis=1)
    hidden = (jax.nn.silu(gate) * up).astype(bf16)
    return (middle, inv_rms, normed, got, gate, up, hidden)


def ffn_share(state, down):
    middle, hidden = state[0], state[-1]
    return own_share(cols_product(hidden, down), middle.shape[0]).astype(bf16)


def ffn_backward(own_grad, other_grad, state, wides, down, head, *others):
    middle, _, normed, got, gate, up, hidden = state
    hidden_grad = product(jnp.concatenate([own_grad, other_grad], axis=0), down)
    sigmoid_gate = jax.nn.sigmoid(gate)
    gate_grad = (hidden_grad * up * sigmoid_gate * (1.0 + gate * (1.0 - sigmoid_gate))).astype(bf16)
    up_grad = (hidden_grad * gate * sigmoid_gate).astype(bf16)
    units = gate.shape[1]
    if len(wides) == 1:
        partial = cols_product(jnp.concatenate([gate_grad, up_grad], axis=1), wides[0])
    else:
        partial = cols_product(gate_grad, wides[0]) + cols_product(up_grad, wides[1])
    normed_grad, *others = sum_tensor(own_share(partial, middle.shape[0]), *others)
    own_sides, norm_sides = (own_grad, other_grad), (normed, got)
    early = token_terms([own_sides, norm_sides], [(0, hidden, 0, units), (1, gate_grad, 0, head)])
    early = lax.psum_scatter(early, "ctx", scatter_dimension=0, tiled=True)
    late = token_terms([norm_sides], [(0, gate_grad, head, units - head), (0, up_grad, 0, units)])
    return normed_grad, early, late, *others


def ffn_backward_out(upstream, normed_grad, state, gain):
    mid_part, gain_term = norm_backward(state[0], state[1], gain, normed_grad.astype(f32))
    return upstream.astype(f32) + mid_part, gain_term


def attention_backward(mid_grad, saved, wide, place, *others):
    pos, tables, sizes = place
    _, _, normed, queries, tail, own, mixed, logs = saved
    query_grad, back, own_grad, mid_grad_b = mix_back(
        pos, queries, tail, own, mixed, logs, tables, mid_grad, wide[1], sizes[1]
    )
    back = from_behind(back, "ctx", -1)
    grads, partial = head_grads(query_grad, own_grad, back, tables, wide[0], sizes[1])
    normed_grad, *others = sum_tensor(partial, *others)
    terms = attention_terms(normed, mid_grad_b, grads, mixed, lax.axis_size("ctx"))
    core = lax.axis_index("pipe")
    mine = take(terms, core)
    theirs = take(terms, 1 - core)
    return normed_grad, add_bf16(mine, swap_cores(theirs)), *others


def attention_backward_out(mid_grad, normed_grad, saved, gain):
    part, gain_term = norm_backward(saved[0], saved[1], gain, normed_grad.astype(f32))
    return (mid_grad + part).astype(bf16), gain_term


def on_device(
    inputs,
    out_grad,
    positions,
    attn_gain,
    w_query,
    w_key,
    w_value,
    w_out,
    ffn_gain,
    w_gate,
    w_up,
    w_down,
):
    core = lax.axis_index("pipe")
    first = core == 0
    shard = lax.axis_index("ctx")
    rows = inputs.shape[1]
    width = inputs.shape[2]
    n_query = w_query.shape[2]
    n_key = w_key.shape[2]
    half = w_gate.shape[2] // 2

    def pick(pair, index):
        return take(pair, index)

    def mine_theirs(array, axis):
        size = array.shape[axis] // 2
        mine = lax.dynamic_slice_in_dim(
            array, core * size, size, axis, allow_negative_indices=False
        )
        theirs = lax.dynamic_slice_in_dim(
            array, (1 - core) * size, size, axis, allow_negative_indices=False
        )
        return mine, theirs

    count = lax.axis_size("ctx")
    gain_row = jnp.concatenate([attn_gain, ffn_gain], axis=1)
    attn_shard = jnp.concatenate([w_query[0], w_key[0], w_value[0], w_out[0].T], axis=1)
    wide_columns = attn_shard.shape[1]
    gain_rows = jnp.pad(gain_row, ((0, 15), (0, wide_columns - gain_row.shape[1])))
    rows_mine, rows_theirs = mine_theirs(attn_shard, 0)
    attn_keep = jnp.concatenate([rows_mine, gain_rows], axis=0)
    attn_got = swap_cores(jnp.concatenate([rows_theirs, gain_rows], axis=0))

    inner_columns = n_query + 2 * n_key

    def attn_weights(pieces):
        got = swap_cores(pieces)
        both = jnp.stack([jnp.where(first, pieces, got), jnp.where(first, got, pieces)], axis=1)
        part_rows = attn_shard.shape[0] // 2
        wide = both[:, :, :part_rows].reshape(width, wide_columns)
        wide = (wide[:, :inner_columns], wide[:, inner_columns:])
        row = pieces[:, part_rows, : gain_row.shape[1]].astype(f32)
        return wide, row.reshape(count, 2, -1).transpose(1, 0, 2).reshape(2, width)

    gate_mine, gate_theirs = mine_theirs(w_gate[0], 1)
    up_mine, up_theirs = mine_theirs(w_up[0], 1)
    wide_keep = jnp.concatenate([gate_mine, up_mine], axis=1)
    wide_got = swap_cores(jnp.concatenate([gate_theirs, up_theirs], axis=1))
    down_mine, down_theirs = mine_theirs(w_down[0], 0)
    down_keep, down_got = down_mine.T, swap_cores(down_theirs.T)

    def for_sections(keep, got):
        return [jnp.where(first, keep, got), jnp.where(first, got, keep)]

    def gather(shard_part):
        return lax.all_gather(shard_part, "ctx", axis=0, tiled=True)

    attn_parts = for_sections(attn_keep, attn_got)
    wide_parts = for_sections(wide_keep, wide_got)
    down_parts = for_sections(down_keep, down_got)
    tail_columns = 3 * half // 8
    wide_low = lax.all_gather(
        wide_parts[0][:, :-tail_columns], ("pipe", "ctx"), axis=0, tiled=True
    )
    down_parts[0] = jnp.concatenate([down_parts[0], wide_parts[0][:, -tail_columns:]], axis=1)
    attn_pieces, attn_parts[1], wide_parts[1], *down_parts = pin(
        ring_gather(*ring_gather_start(attn_parts[0])), attn_parts[1], wide_parts[1], *down_parts
    )
    attn_low, gains_low = attn_weights(attn_pieces)
    down_and_tail = gather(down_parts[0])
    ring_columns = 3 * wide_parts[1].shape[1] // 8
    wide_high = gather(wide_parts[1][:, :-ring_columns])
    down_high = gather(down_parts[1])

    pos_row = pick(positions, core)
    place = (pos_row[:, None], rope_tables(pos_row, HEAD_DIM), (n_query, n_key))

    def scatter(terms):
        return lax.psum_scatter(terms, "ctx", scatter_dimension=0, tiled=True)

    def give_low(share):
        return lax.ppermute(share, "pipe", [(1, 0)])

    def give_high(share):
        return lax.ppermute(share, "pipe", [(0, 1)])

    stream = pick(inputs, core)
    total, attn_saved_low, wide_low, attn_part_high = attention_forward(
        stream, gains_low[0], attn_low, place, wide_low, attn_parts[1]
    )
    wide_low = pick(wide_low.reshape(2, width, -1), core)
    total, wide_low = pin(total, wide_low)
    middle = attn_saved_low[0] + total.astype(f32)
    down_low, wide_tail = down_and_tail[:, :half], down_and_tail[:, half:]
    state_low = ffn_forward_in(middle, gains_low[1], [wide_low, wide_tail], half)
    own_grad, other_grad = pick(out_grad, core), pick(out_grad, 1 - core)
    total, attn_part_high = sum_tensor(ffn_share(state_low, down_low), attn_part_high)
    attn_ring = ring_gather_start(attn_part_high)
    wide_low = jnp.concatenate([wide_low, wide_tail], axis=1)
    total, own_grad, other_grad, (attn_high, gains_high), wide_low = pin(
        total, own_grad, other_grad, attn_weights(ring_gather(*attn_ring)), wide_low
    )
    out_low = (middle + total.astype(f32)).astype(bf16)
    total, attn_saved_high, wide_high, wide_part_high = attention_forward(
        out_low, gains_high[0], attn_high, place, wide_high, wide_parts[1][:, -ring_columns:]
    )
    wide_ring = ring_gather_start(wide_part_high)
    up_high = jnp.concatenate(
        [wide_high[:, half:], ring_gather(*wide_ring).reshape(width, ring_columns)], axis=1
    )
    wide_high = [wide_high[:, :half], up_high]
    total, got_out_low, wide_high = pin(total, swap_cores(out_low), wide_high)
    middle = attn_saved_high[0] + total.astype(f32)
    state_high = ffn_forward_in(middle, gains_high[1], wide_high, half)

    gate, up, down_high = pin(state_high[4], state_high[5], down_high)
    hidden = (jax.nn.silu(gate) * up).astype(bf16)
    state_high = (*state_high[:4], gate, up, hidden)
    normed_grad, early_high, late_high = ffn_backward(
        own_grad, other_grad, state_high, wide_high, down_high, half // 2
    )
    normed_grad, late_high = pin(normed_grad, late_high)
    mid_grad, ffn_gain_high = ffn_backward_out(own_grad, normed_grad, state_high, gains_high[1])
    late_high = scatter(late_high)
    normed_grad, summed, early_high = attention_backward(
        mid_grad, attn_saved_high, attn_high, place, early_high
    )
    normed_grad, attn_ring, out_share = pin(
        normed_grad, ring_scatter_start(summed), ffn_share(state_high, down_high)
    )
    boundary_high, attn_gain_high = attention_backward_out(
        mid_grad, normed_grad, attn_saved_high, gains_high[0]
    )
    got_boundary_high = swap_cores(boundary_high)
    normed_grad, early_low, late_low, late_high = ffn_backward(
        boundary_high, got_boundary_high, state_low, [wide_low], down_low, half // 4, late_high
    )
    normed_grad, late_low, attn_share_high = pin(normed_grad, late_low, ring_scatter(*attn_ring))
    mid_grad, ffn_gain_low = ffn_backward_out(
        boundary_high, normed_grad, state_low, gains_low[1]
    )
    late_low = scatter(late_low)
    normed_grad, summed, early_low = attention_backward(
        mid_grad, attn_saved_low, attn_low, place, early_low
    )
    def from_other(low, high):
        return swap_cores(jnp.where(first, high, low))

    (total,) = sum_tensor(out_share)
    attn_pair = (ring_scatter(*ring_scatter_start(summed)), attn_share_high)
    attn_outs = attention_outputs(core, *attn_pair, from_other(*attn_pair), (n_query, n_key))
    early = (early_low, early_high, give_low(early_low), give_high(early_high))
    down_out = down_outputs(core, early, half)
    normed_grad, down_out, attn_outs, got_late_high = pin(
        normed_grad, down_out, attn_outs, give_high(late_high)
    )
    out_high = (middle + total.astype(f32)).astype(bf16)

    boundary_low, attn_gain_low = attention_backward_out(
        mid_grad, normed_grad, attn_saved_low, gains_low[0]
    )
    gains_out = share_gains(
        jnp.stack(
            [jnp.stack([attn_gain_low, ffn_gain_low]), jnp.stack([attn_gain_high, ffn_gain_high])]
        )
    )
    late_low, gains_out, got_out_high, got_boundary_low = pin(
        late_low, gains_out, swap_cores(out_high), swap_cores(boundary_low)
    )
    outs = (out_low, out_high, got_out_low, got_out_high)
    boundaries = (boundary_low, boundary_high, got_boundary_low, got_boundary_high)
    section_outputs, boundary_grads = section_stacks(core, *outs, *boundaries)
    late = (late_low, late_high, give_low(late_low), got_late_high)
    gate_out, up_out = wide_outputs(core, early, late, half)
    query_out, key_out, value_out, attn_out = attn_outs
    return (
        section_outputs[None],
        boundary_grads[None],
        gains_out[:1],
        query_out[None],
        key_out[None],
        value_out[None],
        attn_out[None],
        gains_out[1:],
        gate_out[None],
        up_out[None],
        down_out[None],
    )


def solution(mesh):
    in_specs = (
        P(None, "ctx", None),
        P(None, "ctx", None),
        P(None, "ctx"),
        P("pipe", "ctx"),
        P("pipe", "ctx", "tensor"),
        P("pipe", "ctx", "tensor"),
        P("pipe", "ctx", "tensor"),
        P("pipe", "tensor", "ctx"),
        P("pipe", "ctx"),
        P("pipe", "ctx", "tensor"),
        P("pipe", "ctx", "tensor"),
        P("pipe", "tensor", "ctx"),
    )
    out_specs = (
        P("pipe", None, "ctx", None),
        P("pipe", None, "ctx", None),
        P("pipe", "ctx"),
        P("pipe", "ctx", "tensor"),
        P("pipe", "ctx", "tensor"),
        P("pipe", "ctx", "tensor"),
        P("pipe", "tensor", "ctx"),
        P("pipe", "ctx"),
        P("pipe", "ctx", "tensor"),
        P("pipe", "ctx", "tensor"),
        P("pipe", "tensor", "ctx"),
    )
    return jax.shard_map(
        on_device, mesh=mesh, in_specs=in_specs, out_specs=out_specs, check_vma=False
    )
```
